128 devices in a mesh: tm: 32 (over x, y, core), row: 4 (over z).
Axes of the slice: x: 4, y: 4, z: 4, core: 2. Of those that a mesh axis runs over, the one named last changes fastest.
Arguments:
- prior: float32 [256], replicated, may hold values from -6 to 6
- dynamics: float32 [2048, 256, 256], P('tm', 'row'), as said below
- gains: float32 [2048, 256, 256], P('tm', 'row'), may hold values from -0.0048828125 to 0.0048828125
- observed: float32 [131072, 256], P('tm', 'row'), may hold values from -6 to 6
- owner: int32 [131072, 1], P('tm'), may hold values from 0 to 31; in each aligned block of 4096 rows (0 to 4095, 4096 to 8191, ...) at most 512 rows name the same one
- step: int32 [131072], P('tm'), may hold values from 0 to 63
Outputs:
- states: float32 [2048, 256], P('tm', 'row')
The draws below stay inside these ranges and needn't reach their ends.
Inputs may be any that keep to these rules, and one draw needn't show every extreme that they name: Among the rows of one index of tm, no owner is named more than 512 times, a bound that some block reaches. Each dynamics[k] is a diagonal plus a dense part of small independent entries.
All inputs are finite; a program needn't handle non-finite values.
Results may differ from the reference program's by a relative error of at most 0.0003.
Values sent between devices are 32-bit elements; how exact they have to be, the bound alone decides.
No kernel may reach another device: no remote copies, remote signals or barrier semaphores. Data moves between devices by JAX's collectives and lax.ppermute only.
A program may use at most 128 MiB of HBM per device.

```python
import math
import jax
import jax.numpy as jnp
import numpy as np
from jax import lax

D = 256
STEP_DEV = 64
OBS_DEV = 4096
HORIZON_LENGTH = 2048
OBS = 131072
CAP = 512
N_TM = 32


def draw_dynamics(key, part):
    sampler_seeds = jax.random.split(key, 4)
    damping_factors = jnp.exp(jax.random.uniform(sampler_seeds[0], (D,), jnp.float32, math.log(0.5 / HORIZON_LENGTH), math.log(1.0 / 30.0)))
    small_perturbation = jnp.exp(jax.random.uniform(sampler_seeds[1], (HORIZON_LENGTH, D), jnp.float32, -0.35, 0.35))
    sudden_impulse = jnp.where(jax.random.uniform(sampler_seeds[2], (HORIZON_LENGTH, 1), jnp.float32) < 4.0 / HORIZON_LENGTH, 0.6, 1.0)
    main_coefficients = jnp.exp(-damping_factors[None, :] * small_perturbation - 0.004) * sudden_impulse
    spread = jax.random.normal(sampler_seeds[3], (HORIZON_LENGTH, D, D), jnp.float32) * (0.1 / math.sqrt(D))
    unit = (jnp.arange(D)[:, None] == jnp.arange(D)[None, :]).astype(jnp.float32)
    return spread + main_coefficients[:, :, None] * unit[None, :, :]


def set_ends(array, stream_key, least, high):
    place = [jax.random.randint(jax.random.fold_in(stream_key, axis), (), 0, length) for axis, length in enumerate(array.shape)]
    widest = array.shape.index(max(array.shape))
    neighbour = place[:widest] + [(place[widest] + 1) % array.shape[widest]] + place[widest + 1:]
    return array.at[tuple(place)].set(least).at[tuple(neighbour)].set(high)


def steps_of(key, dims, shards, smallest, top_value):
    def one(position, parts):
        steps = jax.random.uniform(jax.random.fold_in(jax.random.fold_in(key, 6), position), (parts,), jnp.float32, smallest / len(shards), top_value / len(shards))
        return jnp.repeat(jnp.exp(steps), dims[position] // parts).reshape((-1,) + (1,) * (len(dims) - position - 1))

    level = one(*shards[0])
    for cut in shards[1:]:
        level = level * one(*cut)
    return level


def deal_out(stream_key, own, number, rows, amount, top, bound, slope):
    order = jax.random.permutation(stream_key, amount)
    packed, ordinary = shares(amount, rows * top, bound, slope, True), shares(amount, rows * top, bound, slope, False)
    places = jnp.arange(amount)

    def named(sizes, turn):
        used = int((sizes > 0).sum())
        fixed = max(1, used // 4)
        passed = fixed + (places - fixed + turn * (used - fixed)) % max(1, amount - fixed)
        return jnp.zeros((amount,), jnp.int32).at[order[jnp.where(places < fixed, places, passed)]].set(jnp.asarray(sizes, jnp.int32))

    sizes = jnp.where(number % 4 == 0, named(packed, number // 4), named(ordinary, number - number // 4 - 1))
    mixed = jax.random.permutation(jax.random.fold_in(own, 3), amount)
    donor, sink = mixed[0:amount // 2 * 2:2], mixed[1:amount // 2 * 2:2]
    margin = jnp.minimum(sizes[donor] - 1, bound - sizes[sink]) // 2
    margin = jnp.where((donor == order[0]) | (sink == order[0]) | (sizes[sink] == 0), 0, jnp.maximum(margin, 0))
    passed = jax.random.randint(jax.random.fold_in(own, 4), (amount // 2,), 0, 1 << 20) % (margin + 1)
    sizes = sizes.at[donor].add(-passed).at[sink].add(passed)
    members = jnp.searchsorted(jnp.cumsum(sizes), jnp.arange(rows * top), side="right").astype(jnp.int32)
    grid = members.reshape(top, rows).T
    grid = grid[jax.random.permutation(jax.random.fold_in(own, 1), rows)]
    turn = jax.random.randint(jax.random.fold_in(own, 2), (rows, 1), 0, top)
    return jnp.take_along_axis(grid, (jnp.arange(top)[None, :] + turn) % top, axis=1)


def shares(number_of, total, reach, slope, full):
    loads = [(1 << 20) // math.isqrt(rank ** slope) + 1 for rank in range(1, number_of + 1)]
    largest = reach if full else min(reach, max(-(-total // number_of), total * loads[0] // sum(loads)))
    least = 1 if total - largest >= number_of - 1 else 0
    counts, rest = [largest] + [least] * (number_of - 1), total - largest - least * (number_of - 1)
    while rest > 0:
        free = [i for i in range(1, number_of) if counts[i] < largest] or [i for i in range(1, number_of) if counts[i] < reach]
        whole, budget = sum([loads[i] for i in free]), rest
        for i in free:
            more = min(reach - counts[i], max(1, budget * loads[i] // whole), rest)
            counts[i] = counts[i] + more
            rest = rest - more
    return np.array(counts)


def noise(rng, shape, deviation, most, pieces=(), held_as=jnp.bfloat16):
    gain = steps_of(rng, shape, pieces, -0.22, 0.18) if pieces else 1.0
    result = jax.random.normal(rng, shape, jnp.float32) * deviation * gain
    return jnp.minimum(jnp.maximum(result, -most), most).astype(held_as)


def setup_inputs(seed: int = 0) -> dict:
    key_of = jax.random.split(jax.random.key(seed), 7)
    prior = noise(key_of[0], (D,), 1.0, 6.0, (), jnp.float32)
    dynamics = draw_dynamics(jax.random.fold_in(key_of[6], 71), 0)
    gains = noise(key_of[2], (HORIZON_LENGTH, D, D), (100 * D * OBS_DEV // STEP_DEV) ** -0.5, 0.0048828125, ((0, 32), (1, 4)), jnp.float32)
    observed = noise(key_of[3], (OBS, D), 1.0, 6.0, ((0, 32), (1, 4)), jnp.float32)
    owner_keys = jax.random.split(jax.random.fold_in(key_of[4], 1), OBS // OBS_DEV)
    owner_turns = jax.random.permutation(jax.random.fold_in(key_of[4], 3), OBS // OBS_DEV)
    owner = jax.vmap(lambda own, number: deal_out(jax.random.fold_in(key_of[4], 2), own, number, OBS_DEV, N_TM, 1, CAP, 2))(owner_keys, owner_turns).reshape((OBS, 1))
    step = set_ends(jax.random.randint(key_of[5], (OBS,), 0, STEP_DEV), jax.random.fold_in(key_of[5], 1), 0, STEP_DEV - 1).astype(jnp.int32)
    return dict(prior=prior, dynamics=dynamics, gains=gains, observed=observed, owner=owner, step=step)


def reference(prior, dynamics, gains, observed, owner, step):
    when = owner[:, 0] * STEP_DEV + step
    info = jnp.zeros((HORIZON_LENGTH, D), jnp.float32).at[when].add(observed)
    offset = jnp.einsum("kij,kj->ki", gains.astype(jnp.float32), info, precision=lax.Precision.HIGHEST)

    def advance(state, element):
        matrix, shift_vec = element
        fresh = jnp.dot(matrix, state, precision=lax.Precision.HIGHEST, preferred_element_type=jnp.float32) + shift_vec
        return fresh, fresh

    _, states = lax.scan(advance, prior.astype(jnp.float32), (dynamics, offset))
    return states
```

```python
import functools

import jax
import jax.numpy as jnp
from jax import lax
from jax.experimental import pallas as pl
from jax.experimental.pallas import tpu as pltpu
from jax.sharding import PartitionSpec as P

F32 = jnp.float32
BF16 = jnp.bfloat16
PARAMS = pltpu.CompilerParams(vmem_limit_bytes=56 * 1024 * 1024)
VM = pl.BlockSpec(memory_space=pltpu.VMEM)
SM = pl.BlockSpec(memory_space=pltpu.SMEM)
N = 256
PAD = 16
R = N + PAD
ROWS = 4
SUB = 16
SEG = 4


def split(x):
    hi = x.astype(BF16)
    return hi, (x - hi.astype(F32)).astype(BF16)


def dot_nn(a, b):
    return lax.dot_general(a, b, (((1,), (0,)), ((), ())), preferred_element_type=F32)


def dot_nt(a, b):
    return lax.dot_general(a, b, (((1,), (1,)), ((), ())), preferred_element_type=F32)


def mm(a, b, dot=dot_nn):
    ah, al = split(a)
    bh, bl = split(b)
    return dot(ah, bh) + dot(al, bh) + dot(ah, bl)


def then(first, second):
    out = mm(first, second[:N])
    return jnp.concatenate([out[:N], out[N:] + second[N:]], axis=0)


def apply(s, m):
    return mm(s, m[:N]) + m[N:]


def eye_map():
    r = lax.broadcasted_iota(jnp.int32, (R, N), 0)
    c = lax.broadcasted_iota(jnp.int32, (R, N), 1)
    return jnp.where(r == c, 1.0, 0.0).astype(F32)


def call(kernel, outs, args, specs=None, scratch=(), **kw):
    return pl.pallas_call(
        kernel,
        out_shape=[jax.ShapeDtypeStruct(s, F32) for s in outs],
        in_specs=specs,
        out_specs=[VM] * len(outs),
        scratch_shapes=list(scratch),
        compiler_params=PARAMS,
        **kw,
    )(*args)


BIN_M = 256


def bin_kernel(rid_ref, obs_ref, out_ref, rhs, acc):
    i = pl.program_id(0)
    n_m = pl.num_programs(0)

    @pl.when(i == 0)
    def _():
        x = obs_ref[...]
        hi = x.astype(BF16)
        rest = x - hi.astype(F32)
        mid = rest.astype(BF16)
        low = (rest - mid.astype(F32)).astype(BF16)
        rhs[...] = jnp.concatenate([hi, mid, low, jnp.zeros_like(hi)], axis=1)

    rows = lax.broadcasted_iota(jnp.int32, (BIN_M, rid_ref.shape[1]), 0) + i * BIN_M
    onehot = jnp.where(rows == rid_ref[...], 1.0, 0.0).astype(BF16)
    got = dot_nn(onehot, rhs[...])
    a = got[:, :128]
    b = got[:, 128:]
    ab = a + b
    acc[pl.ds(pl.multiple_of(i * BIN_M, BIN_M), BIN_M), :] = a + pltpu.roll(a, 64, 1) + b + pltpu.roll(b, 64, 1)

    @pl.when(i == n_m - 1)
    def _():
        half = out_ref.shape[0]
        lane = lax.broadcasted_iota(jnp.int32, (half, 128), 1)
        out_ref[...] = jnp.where(lane < 64, acc[:half, :], acc[half:, :])


def binned(rid, observed):
    n_bins = 2048
    obs_rows, width = observed.shape
    return pl.pallas_call(
        bin_kernel,
        out_shape=jax.ShapeDtypeStruct((n_bins // 2, 128), F32),
        grid=(n_bins // BIN_M,),
        in_specs=[
            pl.BlockSpec((1, obs_rows), lambda i: (0, 0)),
            pl.BlockSpec((obs_rows, width), lambda i: (0, 0)),
        ],
        out_specs=pl.BlockSpec((n_bins // 2, 128), lambda i: (0, 0)),
        scratch_shapes=[pltpu.VMEM((obs_rows, 4 * width), BF16), pltpu.VMEM((n_bins, 128), F32)],
        compiler_params=PARAMS,
    )(rid, observed)


def compose_kernel(z_ref, a0, a1, a2, a3, b0, b1, b2, b3, pref, whole, a_s, b_s):
    z = z_ref[0]
    for d, (a, b) in enumerate(((a0, b0), (a1, b1), (a2, b2), (a3, b3))):
        slot = lax.rem(z - d + ROWS, ROWS)
        a_s[:, pl.ds(pl.multiple_of(slot * 64, 64), 64), :] = a[...]
        b_s[slot] = b[...]
    b = jnp.concatenate([b_s[i] for i in range(ROWS)], axis=1)
    first = lax.broadcasted_iota(jnp.int32, (PAD, N), 0) == 0
    cur = [eye_map()] * (SUB // SEG)
    for t in range(SEG):
        for c in range(SUB // SEG):
            k = c * SEG + t
            out = mm(cur[c], a_s[k], dot_nt)
            pref[k, :N, :] = out[:N]
            pref[k, N:, :] = out[N:] + jnp.where(first, b[k : k + 1, :], 0.0)
            cur[c] = pref[k]
    whole[...] = then(then(cur[0], cur[1]), then(cur[2], cur[3]))


def four_kernel(pos_ref, m0, m1, m2, m3, total, before, m_s):
    pos = pos_ref[0]
    for d, m in enumerate((m0, m1, m2, m3)):
        m_s[lax.rem(pos - d + 4, 4)] = m[...]
    m01 = then(m_s[0], m_s[1])
    m23 = then(m_s[2], m_s[3])
    total[...] = then(m01, m23)
    before[...] = eye_map()

    @pl.when(pos == 1)
    def _():
        before[...] = m_s[0]

    @pl.when(pos == 2)
    def _():
        before[...] = m01

    @pl.when(pos == 3)
    def _():
        before[...] = then(m01, m_s[2])


def pair_kernel(c_ref, own, other, before_in, total, before):
    c = c_ref[0]
    swap = c == 1

    @pl.when(swap)
    def _():
        total[...] = then(other[...], own[...])
        before[...] = then(other[...], before_in[...])

    @pl.when(jnp.logical_not(swap))
    def _():
        total[...] = then(own[...], other[...])
        before[...] = before_in[...]


def top_kernel(pos_ref, prior, m0, m1, m2, m3, ybefore, out, m_s, s_s):
    pos = pos_ref[0]
    for d, m in enumerate((m0, m1, m2, m3)):
        m_s[lax.rem(pos - d + 4, 4)] = m[...]
    r = lax.broadcasted_iota(jnp.int32, (PAD, N), 0)
    s_s[...] = jnp.where(r == 0, prior[...], 0.0)
    for i in range(3):

        @pl.when(i < pos)
        def _(i=i):
            s_s[...] = apply(s_s[...], m_s[i])

    out[...] = apply(s_s[...], ybefore[...])


def states_kernel(idx_ref, mine, other, before, pref, o0, o1, o2, o3, st_s, s_s):
    z = idx_ref[0]
    c = idx_ref[1]
    s_s[...] = jnp.where(c == 0, mine[...], other[...])
    s = apply(s_s[...], before[...])
    eye = lax.broadcasted_iota(jnp.int32, (N, N), 0) == lax.broadcasted_iota(jnp.int32, (N, N), 1)
    for q in range(SUB // SEG):
        col = jnp.sum(jnp.where(eye, s[0:1, :], 0.0), axis=1, keepdims=True)
        for t in range(SEG):
            k = q * SEG + t
            row = jnp.sum(pref[k, :N, :] * col, axis=0, keepdims=True) + pref[k, N : N + 1, :]
            for j in range(ROWS):
                st_s[j, k : k + 1, :] = row[:, j * 64 : (j + 1) * 64]
        if q < SUB // SEG - 1:
            s = apply(s, pref[q * SEG + SEG - 1])
    for d, o in enumerate((o0, o1, o2, o3)):
        o[...] = st_s[lax.rem(z + d, ROWS)]


def place_kernel(z_ref, r0, r1, r2, r3, out):
    z = z_ref[0]
    for d, r in enumerate((r0, r1, r2, r3)):
        slot = lax.rem(z - d + ROWS, ROWS)
        out[pl.ds(pl.multiple_of(slot * SUB, SUB), SUB), :] = r[...]


def along_row(x, d):
    return lax.ppermute(x, "row", [(i, (i + d) % ROWS) for i in range(ROWS)])


def pick(x, i):
    return lax.dynamic_index_in_dim(x, i, 0, keepdims=False)


def shards(prior, dynamics, gains, observed, owner, step):
    tm = lax.axis_index("tm").astype(jnp.int32)
    z = lax.axis_index("row").astype(jnp.int32)
    x, y, c = tm // 8, (tm // 2) % 4, tm % 2
    z1 = z.reshape(1)

    parts = dynamics.reshape(ROWS, SUB, 64, N)
    mats = [pick(parts, z)] + [along_row(pick(parts, (z + d) % ROWS), d) for d in (1, 2, 3)]

    rid = owner[:, 0] * 32 + step % 32 + 1024 * (step // 32)
    partial = binned(rid.reshape(1, -1), observed)
    sums = lax.all_to_all(partial, "tm", 0, 0, tiled=True)
    info = jnp.sum(sums.reshape(32, 32, 128), axis=0)
    infos = [info] + [along_row(info, d) for d in (1, 2, 3)]
    cyc = [infos[3], infos[2], infos[1], infos[0]] * 2
    ordered = lax.dynamic_slice_in_dim(jnp.stack(cyc), 3 - z, ROWS, 0)
    full = ordered.reshape(ROWS, 32, 2, 64).transpose(2, 1, 0, 3).reshape(64, N)
    offset = jnp.sum(gains * full[:, None, :], axis=2)
    off = offset.reshape(ROWS, SUB, 64)
    offs = [pick(off, z)] + [along_row(pick(off, (z + d) % ROWS), d) for d in (1, 2, 3)]

    pref, whole = call(
        compose_kernel,
        [(SUB, R, N), (R, N)],
        (z1, *mats, *offs),
        [SM] + [VM] * 8,
        [pltpu.VMEM((SUB, N, N), F32), pltpu.VMEM((ROWS, SUB, 64), F32)],
    )

    four = functools.partial(
        call, four_kernel, [(R, N), (R, N)], specs=[SM] + [VM] * 4, scratch=[pltpu.VMEM((4, R, N), F32)]
    )
    block, before = four(args=(z1, whole, *[along_row(whole, d) for d in (1, 2, 3)]))
    swapped = lax.ppermute(block, "tm", [(i, i ^ 1) for i in range(32)])
    column, before = call(
        pair_kernel, [(R, N), (R, N)], (c.reshape(1), block, swapped, before), [SM] + [VM] * 3
    )

    def along_y(m, d):
        return lax.ppermute(
            m, "tm", [(8 * i + 2 * j, 8 * i + 2 * ((j + d) % 4)) for i in range(4) for j in range(4)]
        )

    def along_x(m, d):
        return lax.ppermute(
            m, "tm", [(8 * i + 2 * j, 8 * (i + d) + 2 * j) for i in range(4 - d) for j in range(4)]
        )

    plane, ybefore = four(args=(y.reshape(1), column, *[along_y(column, d) for d in (1, 2, 3)]))
    (entry,) = call(
        top_kernel,
        [(PAD, N)],
        (x.reshape(1), prior.reshape(1, N), plane, *[along_x(plane, d) for d in (1, 2, 3)], ybefore),
        [SM] + [VM] * 6,
        [pltpu.VMEM((4, R, N), F32), pltpu.VMEM((PAD, N), F32)],
    )
    handed = lax.ppermute(entry, "tm", [(2 * i, 2 * i + 1) for i in range(16)])
    outs = call(
        states_kernel,
        [(SUB, 64)] * 4,
        (jnp.stack([z, c]), entry, handed, before, pref),
        [SM] + [VM] * 4,
        [pltpu.VMEM((ROWS, SUB, 64), F32), pltpu.VMEM((PAD, N), F32)],
    )
    got = [outs[0]] + [along_row(outs[d], d) for d in (1, 2, 3)]
    (states,) = call(place_kernel, [(64, 64)], (z1, *got), [SM] + [VM] * 4)
    return states


def solution(mesh):
    return jax.shard_map(
        shards,
        mesh=mesh,
        in_specs=(
            P(),
            P("tm", "row", None),
            P("tm", "row", None),
            P("tm", "row"),
            P("tm", None),
            P("tm"),
        ),
        out_specs=P("tm", "row"),
        check_vma=False,
    )
```

```python
import functools

import jax
import jax.numpy as jnp
from jax import lax
from jax.experimental import pallas as pl
from jax.experimental.pallas import tpu as pltpu
from jax.sharding import PartitionSpec as P

F32 = jnp.float32
BF16 = jnp.bfloat16
PARAMS = pltpu.CompilerParams(vmem_limit_bytes=56 * 1024 * 1024)
VM = pl.BlockSpec(memory_space=pltpu.VMEM)
SM = pl.BlockSpec(memory_space=pltpu.SMEM)
N = 256
PAD = 16
R = N + PAD
ROWS = 4
SUB = 16
SEG = 4


def split(x):
    hi = x.astype(BF16)
    return hi, (x - hi.astype(F32)).astype(BF16)


def dot_nn(a, b):
    return lax.dot_general(a, b, (((1,), (0,)), ((), ())), preferred_element_type=F32)


def dot_nt(a, b):
    return lax.dot_general(a, b, (((1,), (1,)), ((), ())), preferred_element_type=F32)


def mm(a, b, dot=dot_nn):
    ah, al = split(a)
    bh, bl = split(b)
    return dot(ah, bh) + dot(al, bh) + dot(ah, bl)


def then(first, second):
    out = mm(first, second[:N])
    return jnp.concatenate([out[:N], out[N:] + second[N:]], axis=0)


def apply(s, m):
    return mm(s, m[:N]) + m[N:]


def eye_map():
    r = lax.broadcasted_iota(jnp.int32, (R, N), 0)
    c = lax.broadcasted_iota(jnp.int32, (R, N), 1)
    return jnp.where(r == c, 1.0, 0.0).astype(F32)


def call(kernel, outs, args, specs=None, scratch=(), **kw):
    return pl.pallas_call(
        kernel,
        out_shape=[jax.ShapeDtypeStruct(s, F32) for s in outs],
        in_specs=specs,
        out_specs=[VM] * len(outs),
        scratch_shapes=list(scratch),
        compiler_params=PARAMS,
        **kw,
    )(*args)


BIN_M = 256


def bin_kernel(rid_ref, obs_ref, out_ref, rhs, acc):
    i = pl.program_id(0)
    n_m = pl.num_programs(0)

    @pl.when(i == 0)
    def _():
        x = obs_ref[...]
        hi = x.astype(BF16)
        rest = x - hi.astype(F32)
        mid = rest.astype(BF16)
        low = (rest - mid.astype(F32)).astype(BF16)
        rhs[...] = jnp.concatenate([hi, mid, low, jnp.zeros_like(hi)], axis=0)

    rows = lax.broadcasted_iota(jnp.int32, (BIN_M, rid_ref.shape[1]), 0) + i * BIN_M
    onehot = jnp.where(rows == rid_ref[...], 1.0, 0.0).astype(BF16)
    got = dot_nt(onehot, rhs[...])
    a = got[:, :128] + got[:, 128:]
    acc[pl.ds(pl.multiple_of(i * BIN_M, BIN_M), BIN_M), :] = a + pltpu.roll(a, 64, 1)

    @pl.when(i == n_m - 1)
    def _():
        part = out_ref.shape[0]
        low_half = lax.broadcasted_iota(jnp.int32, (part, 128), 1) < 64
        for h in range(2):
            even = acc[2 * h * part : (2 * h + 1) * part, :]
            odd = acc[(2 * h + 1) * part : (2 * h + 2) * part, :]
            out_ref[:, h * 128 : (h + 1) * 128] = jnp.where(low_half, even, odd)


def binned(rid, observed):
    n_bins = 2048
    width, obs_rows = observed.shape
    return pl.pallas_call(
        bin_kernel,
        out_shape=jax.ShapeDtypeStruct((n_bins // 4, N), F32),
        grid=(n_bins // BIN_M,),
        in_specs=[
            pl.BlockSpec((1, obs_rows), lambda i: (0, 0)),
            pl.BlockSpec((width, obs_rows), lambda i: (0, 0)),
        ],
        out_specs=pl.BlockSpec((n_bins // 4, N), lambda i: (0, 0)),
        scratch_shapes=[pltpu.VMEM((4 * width, obs_rows), BF16), pltpu.VMEM((n_bins, 128), F32)],
        compiler_params=PARAMS,
    )(rid, observed)


def assemble(z, parts, ah, al):
    for d, part in enumerate(parts):
        slot = lax.rem(z - d + ROWS, ROWS)
        rows = pl.ds(pl.multiple_of(slot * 64, 64), 64)
        for k in range(ah.shape[0]):
            hi, lo = split(part[k * 64 : (k + 1) * 64, :])
            ah[k, rows, :] = hi
            al[k, rows, :] = lo


def by_step(x, ah, al):
    xh, xl = split(x)
    return dot_nt(xh, ah) + dot_nt(xl, ah) + dot_nt(xh, al)


def chains(ah, al, pref):
    n_chains = ah.shape[0] // SEG
    eye = jnp.where(
        lax.broadcasted_iota(jnp.int32, (N, N), 0) == lax.broadcasted_iota(jnp.int32, (N, N), 1), 1.0, 0.0
    ).astype(BF16)
    for t in range(SEG):
        for c in range(n_chains):
            k = c * SEG + t
            if t == 0:
                pref[k] = dot_nt(eye, ah[k]) + dot_nt(eye, al[k])
            else:
                pref[k] = by_step(pref[k - 1], ah[k], al[k])


def first_kernel(z_ref, a0, a1, a2, a3, pref, ah, al, both):
    assemble(z_ref[0], (a0, a1, a2, a3), ah, al)
    chains(ah, al, pref)
    both[...] = mm(pref[SEG - 1], pref[2 * SEG - 1])


def second_kernel(z_ref, a0, a1, a2, a3, both, pref, ah, al, three):
    assemble(z_ref[0], (a0, a1, a2, a3), ah, al)
    chains(ah, al, pref)
    three[...] = mm(both[...], pref[SEG - 1])


def third_kernel(
    z_ref, a0, a1, a2, a3, b0, p01, ah01, al01, p2, ah2, al2, three, pref, shifts, whole, ah, al, b_s
):
    z = z_ref[0]
    assemble(z, (a0, a1, a2, a3), ah, al)
    b_s[z] = b0[...]
    for d, a in ((1, a1), (2, a2), (3, a3)):
        b_s[lax.rem(z - d + ROWS, ROWS)] = a[SEG * 64 :, :]
    b = jnp.concatenate([b_s[i, :, :64] for i in range(ROWS)], axis=1)
    first = lax.broadcasted_iota(jnp.int32, (PAD, N), 0) == 0

    def row(k):
        return jnp.where(first, b[k : k + 1, :], 0.0)

    mats = [(ah01, al01, i) for i in range(2 * SEG)] + [(ah2, al2, i) for i in range(SEG)]
    mats += [(ah, al, i) for i in range(SEG)]
    p = [row(c * SEG) for c in range(SUB // SEG)]
    for c in range(SUB // SEG):
        shifts[c * SEG : c * SEG + 1, :] = p[c][:1]
    for t in range(1, SEG):
        for c in range(SUB // SEG):
            k = c * SEG + t
            h, l, i = mats[k]
            p[c] = by_step(p[c], h[i], l[i]) + row(k)
            shifts[k : k + 1, :] = p[c][:1]
    chains(ah, al, pref)
    v = mm(p[0], p01[2 * SEG - 1]) + p[1]
    v = mm(v, p2[SEG - 1]) + p[2]
    v = mm(v, pref[SEG - 1]) + p[3]
    whole[:N, :] = mm(three[...], pref[SEG - 1])
    whole[N:, :] = v


def four_kernel(pos_ref, m0, m1, m2, m3, total, before, m_s):
    pos = pos_ref[0]
    for d, m in enumerate((m0, m1, m2, m3)):
        m_s[lax.rem(pos - d + 4, 4)] = m[...]
    m01 = then(m_s[0], m_s[1])
    m23 = then(m_s[2], m_s[3])
    total[...] = then(m01, m23)
    before[...] = eye_map()

    @pl.when(pos == 1)
    def _():
        before[...] = m_s[0]

    @pl.when(pos == 2)
    def _():
        before[...] = m01

    @pl.when(pos == 3)
    def _():
        before[...] = then(m01, m_s[2])


def pair_kernel(c_ref, own, other, before_in, total, before):
    c = c_ref[0]
    swap = c == 1

    @pl.when(swap)
    def _():
        total[...] = then(other[...], own[...])
        before[...] = then(other[...], before_in[...])

    @pl.when(jnp.logical_not(swap))
    def _():
        total[...] = then(own[...], other[...])
        before[...] = before_in[...]


def top_kernel(pos_ref, prior, m0, m1, m2, m3, ybefore, out, m_s, s_s):
    pos = pos_ref[0]
    for d, m in enumerate((m0, m1, m2, m3)):
        m_s[lax.rem(pos - d + 4, 4)] = m[...]
    r = lax.broadcasted_iota(jnp.int32, (PAD, N), 0)
    s_s[...] = jnp.where(r == 0, prior[...], 0.0)
    for i in range(3):

        @pl.when(i < pos)
        def _(i=i):
            s_s[...] = apply(s_s[...], m_s[i])

    out[...] = apply(s_s[...], ybefore[...])


def states_kernel(idx_ref, mine, other, before, p01, p2, p3, shifts, o0, o1, o2, o3, st_s, s_s):
    z = idx_ref[0]
    c = idx_ref[1]
    s_s[...] = jnp.where(c == 0, mine[...], other[...])
    s = apply(s_s[...], before[...])
    eye = lax.broadcasted_iota(jnp.int32, (N, N), 0) == lax.broadcasted_iota(jnp.int32, (N, N), 1)
    first = lax.broadcasted_iota(jnp.int32, (PAD, N), 0) == 0
    prefs = [(p01, i) for i in range(2 * SEG)] + [(p2, i) for i in range(SEG)] + [(p3, i) for i in range(SEG)]
    for q in range(SUB // SEG):
        col = jnp.sum(jnp.where(eye, s[0:1, :], 0.0), axis=1, keepdims=True)
        for t in range(SEG):
            k = q * SEG + t
            m, i = prefs[k]
            row = jnp.sum(m[i] * col, axis=0, keepdims=True) + shifts[k : k + 1, :]
            for j in range(ROWS):
                st_s[j, k : k + 1, :] = row[:, j * 64 : (j + 1) * 64]
        if q < SUB // SEG - 1:
            m, i = prefs[q * SEG + SEG - 1]
            k = q * SEG + SEG - 1
            s = mm(s, m[i]) + jnp.where(first, shifts[k : k + 1, :], 0.0)
    for d, o in enumerate((o0, o1, o2, o3)):
        o[...] = st_s[lax.rem(z + d, ROWS)]


def offset_kernel(z_ref, g, i0, r1, r2, r3, o0, o1, o2, o3, info_s, off_s):
    z = z_ref[0]
    info_s[z] = i0[...]
    for d, r in ((1, r1), (2, r2), (3, r3)):
        info_s[lax.rem(z - d + ROWS, ROWS)] = r[r.shape[0] - 16 :, :]
    lane = lax.broadcasted_iota(jnp.int32, (64, 128), 1)
    for q in range(4):
        full = jnp.concatenate([info_s[i, :, q * 64 : (q + 1) * 64] for i in range(ROWS)], axis=1)
        acc = jnp.zeros((64, 128), F32)
        for k in range(16):
            col = jnp.sum(g[16 * q + k] * full[k : k + 1, :], axis=1, keepdims=True)
            acc = jnp.where(lane == k, col, acc)
        off_s[q] = jnp.concatenate([acc, jnp.zeros((64, 128), F32)], axis=0).T[:16, :]
    for d, o in enumerate((o0, o1, o2, o3)):
        o[:, :128] = off_s[lax.rem(z + d, ROWS)]
        o[:, 128:] = jnp.zeros((16, 128), F32)


def place_kernel(z_ref, r0, r1, r2, r3, out):
    z = z_ref[0]
    for d, r in enumerate((r0, r1, r2, r3)):
        slot = lax.rem(z - d + ROWS, ROWS)
        out[pl.ds(pl.multiple_of(slot * SUB, SUB), SUB), :] = r[...]


def along_row(x, d):
    return lax.ppermute(x, "row", [(i, (i + d) % ROWS) for i in range(ROWS)])


def shards(prior, dynamics, gains, observed, owner, step):
    tm = lax.axis_index("tm").astype(jnp.int32)
    z = lax.axis_index("row").astype(jnp.int32)
    x, y, c = tm // 8, (tm // 2) % 4, tm % 2
    z1 = z.reshape(1)

    flat = dynamics.reshape(ROWS * SUB * 64, N)

    def piece(d, start, count):
        return lax.dynamic_slice_in_dim(flat, ((z + d) % ROWS) * (SUB * 64) + start * 64, count * 64, 0)

    part_a = [piece(0, 0, 8)] + [along_row(piece(d, 0, 8), d) for d in (1, 2, 3)]

    rid = owner[:, 0] * 16 + step % 16 + 512 * (step // 16)
    partial = binned(rid.reshape(1, -1), observed.T)
    sums = lax.all_to_all(partial, "tm", 0, 0, tiled=True)
    info = jnp.sum(sums.reshape(32, 16, N), axis=0)
    info, *part_a = lax.optimization_barrier((info, *part_a))

    sent_b = [jnp.concatenate([piece(d, 8, 4), info], axis=0) for d in (1, 2, 3)]
    part_b = [piece(0, 8, 4)] + [along_row(sent_b[d - 1], d) for d in (1, 2, 3)]
    p01, ah01, al01, both = pl.pallas_call(
        first_kernel,
        out_shape=[
            jax.ShapeDtypeStruct((8, N, N), F32),
            jax.ShapeDtypeStruct((8, N, N), BF16),
            jax.ShapeDtypeStruct((8, N, N), BF16),
            jax.ShapeDtypeStruct((N, N), F32),
        ],
        in_specs=[SM] + [VM] * 4,
        out_specs=[VM] * 4,
        compiler_params=PARAMS,
    )(z1, *part_a)
    offs = call(
        offset_kernel,
        [(16, N)] * 4,
        (z1, gains, info, *part_b[1:]),
        [SM] + [VM] * 5,
        [pltpu.VMEM((ROWS, 16, N), F32), pltpu.VMEM((ROWS, 16, 128), F32)],
    )
    sent_c = [jnp.concatenate([piece(d, 12, 4), offs[d]], axis=0) for d in (1, 2, 3)]
    part_c = [piece(0, 12, 4)] + [along_row(sent_c[d - 1], d) for d in (1, 2, 3)]
    p2, ah2, al2, three = pl.pallas_call(
        second_kernel,
        out_shape=[
            jax.ShapeDtypeStruct((4, N, N), F32),
            jax.ShapeDtypeStruct((4, N, N), BF16),
            jax.ShapeDtypeStruct((4, N, N), BF16),
            jax.ShapeDtypeStruct((N, N), F32),
        ],
        in_specs=[SM] + [VM] * 5,
        out_specs=[VM] * 4,
        compiler_params=PARAMS,
    )(z1, *part_b, both)
    p3, shifts, whole = call(
        third_kernel,
        [(4, N, N), (SUB, N), (R, N)],
        (z1, *part_c, offs[0], p01, ah01, al01, p2, ah2, al2, three),
        [SM] + [VM] * 12,
        [pltpu.VMEM((4, N, N), BF16), pltpu.VMEM((4, N, N), BF16), pltpu.VMEM((ROWS, 16, N), F32)],
    )

    four = functools.partial(
        call, four_kernel, [(R, N), (R, N)], specs=[SM] + [VM] * 4, scratch=[pltpu.VMEM((4, R, N), F32)]
    )
    block, before = four(args=(z1, whole, *[along_row(whole, d) for d in (1, 2, 3)]))
    swapped = lax.ppermute(block, "tm", [(i, i ^ 1) for i in range(32)])
    column, before = call(
        pair_kernel, [(R, N), (R, N)], (c.reshape(1), block, swapped, before), [SM] + [VM] * 3
    )

    def along_y(m, d):
        return lax.ppermute(
            m, "tm", [(8 * i + 2 * j, 8 * i + 2 * ((j + d) % 4)) for i in range(4) for j in range(4)]
        )

    def along_x(m, d):
        return lax.ppermute(
            m, "tm", [(8 * i + 2 * j, 8 * (i + d) + 2 * j) for i in range(4 - d) for j in range(4)]
        )

    plane, ybefore = four(args=(y.reshape(1), column, *[along_y(column, d) for d in (1, 2, 3)]))
    (entry,) = call(
        top_kernel,
        [(PAD, N)],
        (x.reshape(1), prior.reshape(1, N), plane, *[along_x(plane, d) for d in (1, 2, 3)], ybefore),
        [SM] + [VM] * 6,
        [pltpu.VMEM((4, R, N), F32), pltpu.VMEM((PAD, N), F32)],
    )
    handed = lax.ppermute(entry, "tm", [(2 * i, 2 * i + 1) for i in range(16)])
    outs = call(
        states_kernel,
        [(SUB, 64)] * 4,
        (jnp.stack([z, c]), entry, handed, before, p01, p2, p3, shifts),
        [SM] + [VM] * 7,
        [pltpu.VMEM((ROWS, SUB, 64), F32), pltpu.VMEM((PAD, N), F32)],
    )
    got = [outs[0]] + [along_row(outs[d], d) for d in (1, 2, 3)]
    (states,) = call(place_kernel, [(64, 64)], (z1, *got), [SM] + [VM] * 4)
    return states


def solution(mesh):
    return jax.shard_map(
        shards,
        mesh=mesh,
        in_specs=(
            P(),
            P("tm", "row", None),
            P("tm", "row", None),
            P("tm", "row"),
            P("tm", None),
            P("tm"),
        ),
        out_specs=P("tm", "row"),
        check_vma=False,
    )
```

```python
import jax
import jax.numpy as jnp
from jax import lax
from jax.experimental import pallas as pl
from jax.experimental.pallas import tpu as pltpu
from jax.sharding import PartitionSpec as P

F32 = jnp.float32
BF16 = jnp.bfloat16
PARAMS = pltpu.CompilerParams(vmem_limit_bytes=24 * 1024 * 1024)
VM = pl.BlockSpec(memory_space=pltpu.VMEM)
SM = pl.BlockSpec(memory_space=pltpu.SMEM)
N = 256
PAD = 16
R = N + PAD
ROWS = 4
SUB = 16
CHUNKS = ((5, 5), (3,), (3,))
SEGS = tuple(n for chunk in CHUNKS for n in chunk)
SIZES = tuple(sum(chunk) for chunk in CHUNKS)
ENDS = tuple(sum(SEGS[: i + 1]) for i in range(len(SEGS)))


def split(x):
    hi = x.astype(BF16)
    return hi, (x - hi.astype(F32)).astype(BF16)


def dot_nn(a, b):
    return lax.dot_general(a, b, (((1,), (0,)), ((), ())), preferred_element_type=F32)


def dot_nt(a, b):
    return lax.dot_general(a, b, (((1,), (1,)), ((), ())), preferred_element_type=F32)


def mm(a, b, dot=dot_nn):
    ah, al = split(a)
    bh, bl = split(b)
    return dot(ah, bh) + dot(al, bh) + dot(ah, bl)


def then(first, second):
    out = mm(first, second[:N])
    return jnp.concatenate([out[:N], out[N:] + second[N:]], axis=0)


def apply(s, m):
    return mm(s, m[:N]) + m[N:]


def eye_map():
    r = lax.broadcasted_iota(jnp.int32, (R, N), 0)
    c = lax.broadcasted_iota(jnp.int32, (R, N), 1)
    return jnp.where(r == c, 1.0, 0.0).astype(F32)


def near(x):
    return pltpu.with_memory_space_constraint(x, pltpu.VMEM)


def call(kernel, outs, scalars, args, scratch=(), far=()):
    outs = [o if isinstance(o[0], tuple) else (o, F32) for o in outs]
    return pl.pallas_call(
        kernel,
        out_shape=[pltpu.VMEM(s, t) for s, t in outs],
        in_specs=[SM] * len(scalars) + [VM] * (len(far) + len(args)),
        out_specs=[VM] * len(outs),
        scratch_shapes=list(scratch),
        compiler_params=PARAMS,
    )(*scalars, *far, *[near(a) for a in args])


BIN_M = 256


def bin_kernel(rid_ref, obs_ref, out_ref, rhs, acc):
    i = pl.program_id(0)
    n_m = pl.num_programs(0)

    @pl.when(i == 0)
    def _():
        x = obs_ref[...]
        hi = x.astype(BF16)
        rest = x - hi.astype(F32)
        mid = rest.astype(BF16)
        low = (rest - mid.astype(F32)).astype(BF16)
        rhs[...] = jnp.concatenate([hi, mid, low, jnp.zeros_like(hi)], axis=0)

    rows = lax.broadcasted_iota(jnp.int32, (BIN_M, rid_ref.shape[1]), 0) + i * BIN_M
    onehot = jnp.where(rows == rid_ref[...], 1.0, 0.0).astype(BF16)
    got = dot_nt(onehot, rhs[...])
    a = got[:, :128] + got[:, 128:]
    acc[pl.ds(pl.multiple_of(i * BIN_M, BIN_M), BIN_M), :] = a + pltpu.roll(a, 64, 1)

    @pl.when(i == n_m - 1)
    def _():
        part = out_ref.shape[0]
        low_half = lax.broadcasted_iota(jnp.int32, (part, 128), 1) < 64
        for h in range(2):
            even = acc[2 * h * part : (2 * h + 1) * part, :]
            odd = acc[(2 * h + 1) * part : (2 * h + 2) * part, :]
            out_ref[:, h * 128 : (h + 1) * 128] = jnp.where(low_half, even, odd)


def binned(rid, observed):
    n_bins = 2048
    width, obs_rows = observed.shape
    return pl.pallas_call(
        bin_kernel,
        out_shape=jax.ShapeDtypeStruct((n_bins // 4, N), F32),
        grid=(n_bins // BIN_M,),
        in_specs=[
            pl.BlockSpec((1, obs_rows), lambda i: (0, 0)),
            pl.BlockSpec((width, obs_rows), lambda i: (0, 0)),
        ],
        out_specs=pl.BlockSpec((n_bins // 4, N), lambda i: (0, 0)),
        scratch_shapes=[pltpu.VMEM((4 * width, obs_rows), BF16), pltpu.VMEM((n_bins, 128), F32)],
        compiler_params=PARAMS,
    )(rid, observed)


def assemble(z, parts, ah, al):
    for d, part in enumerate(parts):
        slot = lax.rem(z - d + ROWS, ROWS)
        rows = pl.ds(pl.multiple_of(slot * 64, 64), 64)
        for k in range(ah.shape[0]):
            hi, lo = split(part[k * 64 : (k + 1) * 64, :])
            ah[k, rows, :] = hi
            al[k, rows, :] = lo


def by_step(x, ah, al):
    xh, xl = split(x)
    return dot_nt(xh, ah) + dot_nt(xl, ah) + dot_nt(xh, al)


def chains(lengths, ah, al, pref):
    eye = jnp.where(
        lax.broadcasted_iota(jnp.int32, (N, N), 0) == lax.broadcasted_iota(jnp.int32, (N, N), 1), 1.0, 0.0
    ).astype(BF16)
    for t in range(max(lengths)):
        for c, length in enumerate(lengths):
            if t >= length:
                continue
            k = sum(lengths[:c]) + t
            if t == 0:
                pref[k] = dot_nt(eye, ah[k]) + dot_nt(eye, al[k])
            else:
                pref[k] = by_step(pref[k - 1], ah[k], al[k])


def first_kernel(z_ref, a0, a1, a2, a3, pref, ah, al, both):
    assemble(z_ref[0], (a0, a1, a2, a3), ah, al)
    chains(CHUNKS[0], ah, al, pref)
    both[...] = mm(pref[CHUNKS[0][0] - 1], pref[SIZES[0] - 1])


def second_kernel(z_ref, a0, a1, a2, a3, both, pref, ah, al, three):
    assemble(z_ref[0], (a0, a1, a2, a3), ah, al)
    chains(CHUNKS[1], ah, al, pref)
    three[...] = mm(both[...], pref[SIZES[1] - 1])


def third_kernel(
    z_ref, a0, a1, a2, a3, b0, p01, ah01, al01, p2, ah2, al2, three, pref, shifts, whole, ah, al, b_s
):
    z = z_ref[0]
    assemble(z, (a0, a1, a2, a3), ah, al)
    b_s[z] = b0[...]
    for d, a in ((1, a1), (2, a2), (3, a3)):
        b_s[lax.rem(z - d + ROWS, ROWS)] = a[SIZES[2] * 64 :, :]
    b = jnp.concatenate([b_s[i, :, :64] for i in range(ROWS)], axis=1)
    first = lax.broadcasted_iota(jnp.int32, (PAD, N), 0) == 0

    def row(k):
        return jnp.where(first, b[k : k + 1, :], 0.0)

    mats = [(ah01, al01, i) for i in range(SIZES[0])] + [(ah2, al2, i) for i in range(SIZES[1])]
    mats += [(ah, al, i) for i in range(SIZES[2])]
    starts = [end - n for end, n in zip(ENDS, SEGS)]
    p = [row(k) for k in starts]
    for c, k in enumerate(starts):
        shifts[k : k + 1, :] = p[c][:1]
    for t in range(1, max(SEGS)):
        for c, start in enumerate(starts):
            if t >= SEGS[c]:
                continue
            k = start + t
            h, l, i = mats[k]
            p[c] = by_step(p[c], h[i], l[i]) + row(k)
            shifts[k : k + 1, :] = p[c][:1]
    chains(CHUNKS[2], ah, al, pref)
    v = mm(p[0], p01[SIZES[0] - 1]) + p[1]
    v = mm(v, p2[SIZES[1] - 1]) + p[2]
    v = mm(v, pref[SIZES[2] - 1]) + p[3]
    whole[:N, :] = mm(three[...], pref[SIZES[2] - 1])
    whole[N:, :] = v


def four_kernel(pos_ref, m0, m1, m2, m3, total, before, m_s):
    pos = pos_ref[0]
    for d, m in enumerate((m0, m1, m2, m3)):
        m_s[lax.rem(pos - d + 4, 4)] = m[...]
    m01 = then(m_s[0], m_s[1])
    m23 = then(m_s[2], m_s[3])
    total[...] = then(m01, m23)
    before[...] = eye_map()

    @pl.when(pos == 1)
    def _():
        before[...] = m_s[0]

    @pl.when(pos == 2)
    def _():
        before[...] = m01

    @pl.when(pos == 3)
    def _():
        before[...] = then(m01, m_s[2])


def pair_kernel(c_ref, own, other, before_in, total, before):
    c = c_ref[0]
    swap = c == 1

    @pl.when(swap)
    def _():
        total[...] = then(other[...], own[...])
        before[...] = then(other[...], before_in[...])

    @pl.when(jnp.logical_not(swap))
    def _():
        total[...] = then(own[...], other[...])
        before[...] = before_in[...]


def top_kernel(pos_ref, prior, m0, m1, m2, m3, ybefore, out, m_s, s_s):
    pos = pos_ref[0]
    for d, m in enumerate((m0, m1, m2, m3)):
        m_s[lax.rem(pos - d + 4, 4)] = m[...]
    r = lax.broadcasted_iota(jnp.int32, (PAD, N), 0)
    s_s[...] = jnp.where(r == 0, prior[...], 0.0)
    for i in range(3):

        @pl.when(i < pos)
        def _(i=i):
            s_s[...] = apply(s_s[...], m_s[i])

    out[...] = apply(s_s[...], ybefore[...])


def states_kernel(z_ref, c_ref, mine, other, before, p01, p2, p3, shifts, o0, o1, o2, o3, st_s, s_s):
    z = z_ref[0]
    c = c_ref[0]
    s_s[...] = jnp.where(c == 0, mine[...], other[...])
    s = apply(s_s[...], before[...])
    eye = lax.broadcasted_iota(jnp.int32, (N, N), 0) == lax.broadcasted_iota(jnp.int32, (N, N), 1)
    first = lax.broadcasted_iota(jnp.int32, (PAD, N), 0) == 0
    prefs = [(p01, i) for i in range(SIZES[0])] + [(p2, i) for i in range(SIZES[1])]
    prefs += [(p3, i) for i in range(SIZES[2])]
    for end, n in zip(ENDS, SEGS):
        col = jnp.sum(jnp.where(eye, s[0:1, :], 0.0), axis=1, keepdims=True)
        for k in range(end - n, end):
            m, i = prefs[k]
            row = jnp.sum(m[i] * col, axis=0, keepdims=True) + shifts[k : k + 1, :]
            for j in range(ROWS):
                st_s[j, k : k + 1, :] = row[:, j * 64 : (j + 1) * 64]
        if end < SUB:
            m, i = prefs[end - 1]
            s = mm(s, m[i]) + jnp.where(first, shifts[end - 1 : end, :], 0.0)
    for d, o in enumerate((o0, o1, o2, o3)):
        o[...] = st_s[lax.rem(z + d, ROWS)]


def offset_kernel(z_ref, g, i0, r1, r2, r3, o0, o1, o2, o3, info_s, off_s):
    z = z_ref[0]
    info_s[z] = i0[...]
    for d, r in ((1, r1), (2, r2), (3, r3)):
        info_s[lax.rem(z - d + ROWS, ROWS)] = r[r.shape[0] - 16 :, :]
    lane = lax.broadcasted_iota(jnp.int32, (64, 128), 1)
    for q in range(4):
        full = jnp.concatenate([info_s[i, :, q * 64 : (q + 1) * 64] for i in range(ROWS)], axis=1)
        acc = jnp.zeros((64, 128), F32)
        for k in range(16):
            col = jnp.sum(g[16 * q + k] * full[k : k + 1, :], axis=1, keepdims=True)
            acc = jnp.where(lane == k, col, acc)
        off_s[q] = jnp.concatenate([acc, jnp.zeros((64, 128), F32)], axis=0).T[:16, :]
    for d, o in enumerate((o0, o1, o2, o3)):
        o[:, :128] = off_s[lax.rem(z + d, ROWS)]
        o[:, 128:] = jnp.zeros((16, 128), F32)


def place_kernel(z_ref, r0, r1, r2, r3, out):
    z = z_ref[0]
    for d, r in enumerate((r0, r1, r2, r3)):
        slot = lax.rem(z - d + ROWS, ROWS)
        out[pl.ds(pl.multiple_of(slot * SUB, SUB), SUB), :] = r[...]


def along_row(x, d):
    return lax.ppermute(x, "row", [(i, (i + d) % ROWS) for i in range(ROWS)])


def shards(prior, dynamics, gains, observed, owner, step):
    tm = lax.axis_index("tm").astype(jnp.int32)
    z = lax.axis_index("row").astype(jnp.int32)
    x, y, c = tm // 8, (tm // 2) % 4, tm % 2
    z1 = z.reshape(1)

    flat = dynamics.reshape(ROWS * SUB * 64, N)

    def piece(d, start, count):
        return lax.dynamic_slice_in_dim(flat, ((z + d) % ROWS) * (SUB * 64) + start * 64, count * 64, 0)

    at_b, at_c = SIZES[0], SIZES[0] + SIZES[1]
    part_a = [piece(0, 0, SIZES[0])] + [along_row(piece(d, 0, SIZES[0]), d) for d in (1, 2, 3)]

    rid = owner[:, 0] * 16 + step % 16 + 512 * (step // 16)
    partial = binned(rid.reshape(1, -1), observed.T)
    sums = lax.all_to_all(partial, "tm", 0, 0, tiled=True)
    info = jnp.sum(sums.reshape(32, 16, N), axis=0)
    info, *part_a = lax.optimization_barrier((info, *part_a))

    sent_b = [jnp.concatenate([piece(d, at_b, SIZES[1]), info], axis=0) for d in (1, 2, 3)]
    part_b = [piece(0, at_b, SIZES[1])] + [along_row(sent_b[d - 1], d) for d in (1, 2, 3)]
    p01, ah01, al01, both = call(
        first_kernel,
        [(SIZES[0], N, N), ((SIZES[0], N, N), BF16), ((SIZES[0], N, N), BF16), (N, N)],
        (z1,),
        part_a,
    )
    p01, ah01, al01, both, *part_b = lax.optimization_barrier((p01, ah01, al01, both, *part_b))
    offs = call(
        offset_kernel,
        [(16, N)] * 4,
        (z1,),
        (info, *part_b[1:]),
        [pltpu.VMEM((ROWS, 16, N), F32), pltpu.VMEM((ROWS, 16, 128), F32)],
        far=(gains,),
    )
    sent_c = [jnp.concatenate([piece(d, at_c, SIZES[2]), offs[d]], axis=0) for d in (1, 2, 3)]
    part_c = [piece(0, at_c, SIZES[2])] + [along_row(sent_c[d - 1], d) for d in (1, 2, 3)]
    p2, ah2, al2, three = call(
        second_kernel,
        [(SIZES[1], N, N), ((SIZES[1], N, N), BF16), ((SIZES[1], N, N), BF16), (N, N)],
        (z1,),
        (*part_b, both),
    )
    p3, shifts, whole = call(
        third_kernel,
        [(SIZES[2], N, N), (SUB, N), (R, N)],
        (z1,),
        (*part_c, offs[0], p01, ah01, al01, p2, ah2, al2, three),
        [pltpu.VMEM((SIZES[2], N, N), BF16)] * 2 + [pltpu.VMEM((ROWS, 16, N), F32)],
    )

    def four(pos, maps):
        return call(four_kernel, [(R, N), (R, N)], (pos.reshape(1),), maps, [pltpu.VMEM((4, R, N), F32)])

    block, before = four(z, [whole] + [along_row(whole, d) for d in (1, 2, 3)])
    swapped = lax.ppermute(block, "tm", [(i, i ^ 1) for i in range(32)])
    column, before = call(pair_kernel, [(R, N), (R, N)], (c.reshape(1),), (block, swapped, before))

    def along_y(m, d):
        return lax.ppermute(
            m, "tm", [(8 * i + 2 * j, 8 * i + 2 * ((j + d) % 4)) for i in range(4) for j in range(4)]
        )

    def along_x(m, d):
        return lax.ppermute(
            m, "tm", [(8 * i + 2 * j, 8 * (i + d) + 2 * j) for i in range(4 - d) for j in range(4)]
        )

    plane, ybefore = four(y, [column] + [along_y(column, d) for d in (1, 2, 3)])
    (entry,) = call(
        top_kernel,
        [(PAD, N)],
        (x.reshape(1),),
        (prior.reshape(1, N), plane, *[along_x(plane, d) for d in (1, 2, 3)], ybefore),
        [pltpu.VMEM((4, R, N), F32), pltpu.VMEM((PAD, N), F32)],
    )
    handed = lax.ppermute(entry, "tm", [(2 * i, 2 * i + 1) for i in range(16)])
    outs = call(
        states_kernel,
        [(SUB, 64)] * 4,
        (z1, c.reshape(1)),
        (entry, handed, before, p01, p2, p3, shifts),
        [pltpu.VMEM((ROWS, SUB, 64), F32), pltpu.VMEM((PAD, N), F32)],
    )
    got = [outs[0]] + [along_row(outs[d], d) for d in (1, 2, 3)]
    states = pl.pallas_call(
        place_kernel,
        out_shape=jax.ShapeDtypeStruct((64, 64), F32),
        in_specs=[SM] + [VM] * 4,
        out_specs=VM,
        compiler_params=PARAMS,
    )(z1, *[near(g) for g in got])
    return states


def solution(mesh):
    return jax.shard_map(
        shards,
        mesh=mesh,
        in_specs=(
            P(),
            P("tm", "row", None),
            P("tm", "row", None),
            P("tm", "row"),
            P("tm", None),
            P("tm"),
        ),
        out_specs=P("tm", "row"),
        check_vma=False,
    )
```

```python
import jax
import jax.numpy as jnp
from jax import lax
from jax.experimental import pallas as pl
from jax.experimental.pallas import tpu as pltpu
from jax.sharding import PartitionSpec as P

F32 = jnp.float32
BF16 = jnp.bfloat16
MIB = 1024 * 1024
VM = pl.BlockSpec(memory_space=pltpu.VMEM)
SM = pl.BlockSpec(memory_space=pltpu.SMEM)
N = 256
PAD = 16
R = N + PAD
Z, C, Y, X = range(4)
HALF = R // 2
ROWS = 4
SUB = 16
CHUNKS = ((5, 5), (3,), (3,))
SEGS = tuple(n for chunk in CHUNKS for n in chunk)
SIZES = tuple(sum(chunk) for chunk in CHUNKS)
ENDS = tuple(sum(SEGS[: i + 1]) for i in range(len(SEGS)))


def split(x):
    hi = x.astype(BF16)
    return hi, (x - hi.astype(F32)).astype(BF16)


def dot_nn(a, b):
    return lax.dot_general(a, b, (((1,), (0,)), ((), ())), preferred_element_type=F32)


def dot_nt(a, b):
    return lax.dot_general(a, b, (((1,), (1,)), ((), ())), preferred_element_type=F32)


def mm(a, b, dot=dot_nn):
    ah, al = split(a)
    bh, bl = split(b)
    return dot(ah, bh) + dot(al, bh) + dot(ah, bl)


def then(first, second):
    out = mm(first, second[:N])
    return jnp.concatenate([out[:N], out[N:] + second[N:]], axis=0)


def apply(s, m):
    return mm(s, m[:N]) + m[N:]


def eye_map():
    r = lax.broadcasted_iota(jnp.int32, (R, N), 0)
    c = lax.broadcasted_iota(jnp.int32, (R, N), 1)
    return jnp.where(r == c, 1.0, 0.0).astype(F32)


FAR = pl.BlockSpec(memory_space=pltpu.HBM)


def near(x):
    return pltpu.with_memory_space_constraint(x, pltpu.VMEM)


def call(kernel, outs, idx, args, scratch=(), far=(), mib=8):
    outs = [o if isinstance(o[0], tuple) else (o, F32) for o in outs]
    return pl.pallas_call(
        kernel,
        out_shape=[pltpu.VMEM(s, t) for s, t in outs],
        in_specs=[SM] + [FAR] * len(far) + [VM] * len(args),
        out_specs=[VM] * len(outs),
        scratch_shapes=list(scratch),
        compiler_params=pltpu.CompilerParams(vmem_limit_bytes=mib * MIB),
    )(idx, *[pltpu.with_memory_space_constraint(f, pltpu.HBM) for f in far], *[near(a) for a in args])


BIN_M = 256


def bin_kernel(rid_ref, obs_ref, out_ref, rhs, acc):
    i = pl.program_id(0)
    n_m = pl.num_programs(0)

    @pl.when(i == 0)
    def _():
        x = obs_ref[...]
        hi = x.astype(BF16)
        rest = x - hi.astype(F32)
        mid = rest.astype(BF16)
        low = (rest - mid.astype(F32)).astype(BF16)
        rhs[...] = jnp.concatenate([hi, mid, low, jnp.zeros_like(hi)], axis=0)

    rows = lax.broadcasted_iota(jnp.int32, (BIN_M, rid_ref.shape[1]), 0) + i * BIN_M
    onehot = jnp.where(rows == rid_ref[...], 1.0, 0.0).astype(BF16)
    got = dot_nt(onehot, rhs[...])
    a = got[:, :128] + got[:, 128:]
    acc[pl.ds(pl.multiple_of(i * BIN_M, BIN_M), BIN_M), :] = a + pltpu.roll(a, 64, 1)

    @pl.when(i == n_m - 1)
    def _():
        part = out_ref.shape[0]
        low_half = lax.broadcasted_iota(jnp.int32, (part, 128), 1) < 64
        for h in range(2):
            even = acc[2 * h * part : (2 * h + 1) * part, :]
            odd = acc[(2 * h + 1) * part : (2 * h + 2) * part, :]
            out_ref[:, h * 128 : (h + 1) * 128] = jnp.where(low_half, even, odd)


def binned(rid, observed):
    n_bins = 2048
    width, obs_rows = observed.shape
    return pl.pallas_call(
        bin_kernel,
        out_shape=jax.ShapeDtypeStruct((n_bins // 4, N), F32),
        grid=(n_bins // BIN_M,),
        in_specs=[
            pl.BlockSpec((1, obs_rows), lambda i: (0, 0)),
            pl.BlockSpec((width, obs_rows), lambda i: (0, 0)),
        ],
        out_specs=pl.BlockSpec((n_bins // 4, N), lambda i: (0, 0)),
        scratch_shapes=[pltpu.VMEM((4 * width, obs_rows), BF16), pltpu.VMEM((n_bins, 128), F32)],
        compiler_params=pltpu.CompilerParams(vmem_limit_bytes=24 * MIB),
    )(rid, observed)


def own_copy(z, flat, own, start, sem):
    return pltpu.make_async_copy(flat.at[pl.ds(pl.multiple_of(z * (SUB * 64) + start * 64, 64), own.shape[0])], own, sem)


def assemble(z, parts, ah, al, own=None):
    for d in (1, 2, 3, 0):
        slot = lax.rem(z - d + ROWS, ROWS)
        rows = pl.ds(pl.multiple_of(slot * 64, 64), 64)
        if d == 0:
            own.wait()
        for k in range(ah.shape[0]):
            hi, lo = split(parts[d][k * 64 : (k + 1) * 64, :])
            ah[k, rows, :] = hi
            al[k, rows, :] = lo


def by_step(x, ah, al):
    xh, xl = split(x)
    return dot_nt(xh, ah) + dot_nt(xl, ah) + dot_nt(xh, al)


def chains(lengths, ah, al, pref):
    eye = jnp.where(
        lax.broadcasted_iota(jnp.int32, (N, N), 0) == lax.broadcasted_iota(jnp.int32, (N, N), 1), 1.0, 0.0
    ).astype(BF16)
    for t in range(max(lengths)):
        for c, length in enumerate(lengths):
            if t >= length:
                continue
            k = sum(lengths[:c]) + t
            if t == 0:
                pref[k] = dot_nt(eye, ah[k]) + dot_nt(eye, al[k])
            else:
                pref[k] = by_step(pref[k - 1], ah[k], al[k])


def first_kernel(idx, flat, gains, a1, a2, a3, pref, ah, al, both, staged, own, sems):
    z = idx[Z]
    late = pltpu.make_async_copy(gains, staged, sems.at[1])
    copy = own_copy(z, flat, own, 0, sems.at[0])
    copy.start()
    late.start()
    assemble(z, (own, a1, a2, a3), ah, al, copy)
    chains(CHUNKS[0], ah, al, pref)
    both[...] = mm(pref[CHUNKS[0][0] - 1], pref[SIZES[0] - 1])
    late.wait()


def second_kernel(idx, flat, a1, a2, a3, both, pref, ah, al, three, own, sem):
    z = idx[Z]
    copy = own_copy(z, flat, own, SIZES[0], sem)
    copy.start()
    assemble(z, (own, a1, a2, a3), ah, al, copy)
    chains(CHUNKS[1], ah, al, pref)
    three[...] = mm(both[...], pref[SIZES[1] - 1])


def third_kernel(
    idx, flat, a1, a2, a3, b0, p01, ah01, al01, p2, ah2, al2, three, pref, shifts, whole, ah, al, b_s, own, sem
):
    z = idx[Z]
    copy = own_copy(z, flat, own, SIZES[0] + SIZES[1], sem)
    copy.start()
    assemble(z, (own, a1, a2, a3), ah, al, copy)
    b_s[z] = b0[...]
    for d, a in ((1, a1), (2, a2), (3, a3)):
        b_s[lax.rem(z - d + ROWS, ROWS)] = a[SIZES[2] * 64 :, :]
    b = jnp.concatenate([b_s[i, :, :64] for i in range(ROWS)], axis=1)
    first = lax.broadcasted_iota(jnp.int32, (PAD, N), 0) == 0

    def row(k):
        return jnp.where(first, b[k : k + 1, :], 0.0)

    mats = [(ah01, al01, i) for i in range(SIZES[0])] + [(ah2, al2, i) for i in range(SIZES[1])]
    mats += [(ah, al, i) for i in range(SIZES[2])]
    starts = [end - n for end, n in zip(ENDS, SEGS)]
    p = [row(k) for k in starts]
    for c, k in enumerate(starts):
        shifts[k : k + 1, :] = p[c][:1]
    for t in range(1, max(SEGS)):
        for c, start in enumerate(starts):
            if t >= SEGS[c]:
                continue
            k = start + t
            h, l, i = mats[k]
            p[c] = by_step(p[c], h[i], l[i]) + row(k)
            shifts[k : k + 1, :] = p[c][:1]
    chains(CHUNKS[2], ah, al, pref)
    v = mm(p[0], p01[SIZES[0] - 1]) + p[1]
    v = mm(v, p2[SIZES[1] - 1]) + p[2]
    v = mm(v, pref[SIZES[2] - 1]) + p[3]
    whole[:N, :] = mm(three[...], pref[SIZES[2] - 1])
    whole[N:, :] = v


def combine(pos, m_s, before):
    m01 = then(m_s[0], m_s[1])
    m23 = then(m_s[2], m_s[3])
    before[...] = eye_map()

    @pl.when(pos == 1)
    def _():
        before[...] = m_s[0]

    @pl.when(pos == 2)
    def _():
        before[...] = m01

    @pl.when(pos == 3)
    def _():
        before[...] = then(m01, m_s[2])

    return then(m01, m23)


def four_kernel(idx, m0, m1, m2, m3, total, before, m_s):
    pos = idx[Z]
    for d, m in enumerate((m0, m1, m2, m3)):
        m_s[lax.rem(pos - d + 4, 4)] = m[...]
    total[...] = combine(pos, m_s, before)


def half_rows(c):
    return pl.ds(pl.multiple_of(c * HALF, 8), HALF)


def join_halves(pos, c, mine, others, m_s):
    for d, (m, o) in enumerate(zip(mine, others)):
        slot = lax.rem(pos - d + 3, 4)
        m_s[slot, half_rows(c), :] = m[...]
        m_s[slot, half_rows(1 - c), :] = o[...]


def halves_kernel(idx, own, h1, h2, h3, o1, o2, o3, half, before, m_s):
    pos, c = idx[Y], idx[C]
    m_s[pos] = own[...]
    join_halves(pos, c, (h1, h2, h3), (o1, o2, o3), m_s)
    m_s[4] = combine(pos, m_s, before)
    half[...] = m_s[4, half_rows(c), :]


def pair_kernel(idx, own, other, before_in, total, half, before):
    c = idx[C]
    swap = c == 1

    @pl.when(swap)
    def _():
        total[...] = then(other[...], own[...])
        before[...] = then(other[...], before_in[...])

    @pl.when(jnp.logical_not(swap))
    def _():
        total[...] = then(own[...], other[...])
        before[...] = before_in[...]

    half[...] = total[half_rows(c), :]


def fold_kernel(idx, first, second, out):
    out[...] = then(first[...], second[...])


def states_kernel(
    idx, prior, h1, h2, h3, g1, g2, g3, before, p01, p2, p3, shifts, o0, o1, o2, o3, st_s, m_s, s_s
):
    z, pos = idx[Z], idx[X]
    join_halves(pos, idx[C], (h1, h2, h3), (g1, g2, g3), m_s)
    s_s[...] = jnp.where(lax.broadcasted_iota(jnp.int32, (PAD, N), 0) == 0, prior[...], 0.0)
    for i in range(3):

        @pl.when(i < pos)
        def _(i=i):
            s_s[...] = apply(s_s[...], m_s[i])

    s = apply(s_s[...], before[...])
    eye = lax.broadcasted_iota(jnp.int32, (N, N), 0) == lax.broadcasted_iota(jnp.int32, (N, N), 1)
    first = lax.broadcasted_iota(jnp.int32, (PAD, N), 0) == 0
    prefs = [(p01, i) for i in range(SIZES[0])] + [(p2, i) for i in range(SIZES[1])]
    prefs += [(p3, i) for i in range(SIZES[2])]
    for end, n in zip(ENDS, SEGS):
        col = jnp.sum(jnp.where(eye, s[0:1, :], 0.0), axis=1, keepdims=True)
        for k in range(end - n, end):
            m, i = prefs[k]
            row = jnp.sum(m[i] * col, axis=0, keepdims=True) + shifts[k : k + 1, :]
            for j in range(ROWS):
                st_s[j, k : k + 1, :] = row[:, j * 64 : (j + 1) * 64]
        if end < SUB:
            m, i = prefs[end - 1]
            s = mm(s, m[i]) + jnp.where(first, shifts[end - 1 : end, :], 0.0)
    for d, o in enumerate((o0, o1, o2, o3)):
        o[...] = st_s[lax.rem(z + d, ROWS)]


def send_copies(z, flat, outs, start, count, sems):
    copies = []
    for d, o in enumerate(outs, 1):
        at = lax.rem(z + d, ROWS) * (SUB * 64) + start * 64
        source = flat.at[pl.ds(pl.multiple_of(at, 64), count * 64)]
        copies.append(pltpu.make_async_copy(source, o.at[pl.ds(0, count * 64)], sems.at[d - 1]))
    for copy in copies:
        copy.start()
    return copies


def send_a_kernel(idx, flat, o1, o2, o3, sems):
    for copy in send_copies(idx[Z], flat, (o1, o2, o3), 0, SIZES[0], sems):
        copy.wait()


def send_b_kernel(idx, flat, sums, o1, o2, o3, info, sems):
    copies = send_copies(idx[Z], flat, (o1, o2, o3), SIZES[0], SIZES[1], sems)
    info[...] = jnp.sum(sums[...], axis=0)
    for copy, o in zip(copies, (o1, o2, o3)):
        copy.wait()
        o[SIZES[1] * 64 :, :] = info[...]


def send_c_kernel(idx, flat, t1, t2, t3, o1, o2, o3, sems):
    copies = send_copies(idx[Z], flat, (o1, o2, o3), SIZES[0] + SIZES[1], SIZES[2], sems)
    for copy, o, t in zip(copies, (o1, o2, o3), (t1, t2, t3)):
        copy.wait()
        o[SIZES[2] * 64 :, :] = t[...]


def offset_kernel(idx, g, i0, r1, r2, r3, o0, o1, o2, o3, info_s, off_s):
    z = idx[Z]
    info_s[z] = i0[...]
    for d, r in ((1, r1), (2, r2), (3, r3)):
        info_s[lax.rem(z - d + ROWS, ROWS)] = r[r.shape[0] - 16 :, :]
    lane = lax.broadcasted_iota(jnp.int32, (64, 128), 1)
    for q in range(4):
        full = jnp.concatenate([info_s[i, :, q * 64 : (q + 1) * 64] for i in range(ROWS)], axis=1)
        acc = jnp.zeros((64, 128), F32)
        for k in range(16):
            col = jnp.sum(g[16 * q + k] * full[k : k + 1, :], axis=1, keepdims=True)
            acc = jnp.where(lane == k, col, acc)
        off_s[q] = jnp.concatenate([acc, jnp.zeros((64, 128), F32)], axis=0).T[:16, :]
    for d, o in enumerate((o0, o1, o2, o3)):
        o[:, :128] = off_s[lax.rem(z + d, ROWS)]
        o[:, 128:] = jnp.zeros((16, 128), F32)


def place_kernel(idx, r0, r1, r2, r3, out):
    z = idx[Z]
    for d, r in enumerate((r0, r1, r2, r3)):
        slot = lax.rem(z - d + ROWS, ROWS)
        out[pl.ds(pl.multiple_of(slot * SUB, SUB), SUB), :] = r[...]


def along_row(x, d):
    return lax.ppermute(x, "row", [(i, (i + d) % ROWS) for i in range(ROWS)])


def shards(prior, dynamics, gains, observed, owner, step):
    tm = lax.axis_index("tm").astype(jnp.int32)
    z = lax.axis_index("row").astype(jnp.int32)
    idx = jnp.stack([z, tm & 1, (tm >> 1) & 3, tm >> 3])
    prior = prior.reshape(1, N)
    flat = dynamics.reshape(ROWS * SUB * 64, N)
    dma3 = pltpu.SemaphoreType.DMA((3,))

    def along_rows(blocks):
        return [along_row(b, d) for d, b in enumerate(blocks, 1)]

    part_a = along_rows(call(send_a_kernel, [(SIZES[0] * 64, N)] * 3, idx, (), [dma3], far=(flat,)))

    rid = owner[:, 0] * 16 + step % 16 + 512 * (step // 16)
    partial = binned(rid.reshape(1, -1), observed.T)
    sums = lax.all_to_all(partial, "tm", 0, 0, tiled=True).reshape(32, 16, N)
    sums, idx, prior, *part_a = lax.optimization_barrier((sums, idx, prior, *part_a))

    *sent_b, info = call(
        send_b_kernel, [(SIZES[1] * 64 + 16, N)] * 3 + [(16, N)], idx, (sums,), [dma3], far=(flat,)
    )
    part_b = along_rows(sent_b)
    p01, ah01, al01, both, staged = call(
        first_kernel,
        [(SIZES[0], N, N), ((SIZES[0], N, N), BF16), ((SIZES[0], N, N), BF16), (N, N), gains.shape],
        idx,
        part_a,
        [pltpu.VMEM((SIZES[0] * 64, N), F32), pltpu.SemaphoreType.DMA((2,))],
        far=(flat, gains),
    )
    p01, ah01, al01, both, staged, *part_b = lax.optimization_barrier((p01, ah01, al01, both, staged, *part_b))
    offs = call(
        offset_kernel,
        [(16, N)] * 4,
        idx,
        (staged, info, *part_b),
        [pltpu.VMEM((ROWS, 16, N), F32), pltpu.VMEM((ROWS, 16, 128), F32)],
    )
    sent_c = call(send_c_kernel, [(SIZES[2] * 64 + 16, N)] * 3, idx, offs[1:], [dma3], far=(flat,))
    part_c = along_rows(sent_c)
    p2, ah2, al2, three = call(
        second_kernel,
        [(SIZES[1], N, N), ((SIZES[1], N, N), BF16), ((SIZES[1], N, N), BF16), (N, N)],
        idx,
        (*part_b, both),
        [pltpu.VMEM((SIZES[1] * 64, N), F32), pltpu.SemaphoreType.DMA],
        far=(flat,),
    )
    p3, shifts, whole = call(
        third_kernel,
        [(SIZES[2], N, N), (SUB, N), (R, N)],
        idx,
        (*part_c, offs[0], p01, ah01, al01, p2, ah2, al2, three),
        [pltpu.VMEM((SIZES[2], N, N), BF16)] * 2
        + [pltpu.VMEM((ROWS, 16, N), F32), pltpu.VMEM((SIZES[2] * 64, N), F32), pltpu.SemaphoreType.DMA],
        far=(flat,),
    )

    block, before = call(
        four_kernel,
        [(R, N), (R, N)],
        idx,
        (whole, *[along_row(whole, d) for d in (1, 2, 3)]),
        [pltpu.VMEM((4, R, N), F32)],
    )

    def other_core(m):
        return lax.ppermute(m, "tm", [(i, i ^ 1) for i in range(32)])

    def along_tm(m, d, n, stride):
        places = [(i, i - i % (n * stride) + (i + d * stride) % (n * stride)) for i in range(32)]
        return lax.ppermute(m, "tm", places)

    column, half, before = call(
        pair_kernel, [(R, N), (HALF, N), (R, N)], idx, (block, other_core(block), before)
    )
    halves = [along_tm(half, d, 4, 2) for d in (1, 2, 3)]
    half, ybefore = call(
        halves_kernel,
        [(HALF, N), (R, N)],
        idx,
        (column, *halves, *[other_core(h) for h in halves]),
        [pltpu.VMEM((5, R, N), F32)],
    )
    halves = [along_tm(half, d, 4, 8) for d in (1, 2, 3)]
    (before,) = call(fold_kernel, [(R, N)], idx, (ybefore, before))
    outs = call(
        states_kernel,
        [(SUB, 64)] * 4,
        idx,
        (prior, *halves, *[other_core(h) for h in halves], before, p01, p2, p3, shifts),
        [pltpu.VMEM((ROWS, SUB, 64), F32), pltpu.VMEM((4, R, N), F32), pltpu.VMEM((PAD, N), F32)],
    )
    got = [outs[0], *along_rows(outs[1:])]
    return pl.pallas_call(
        place_kernel,
        out_shape=jax.ShapeDtypeStruct((64, 64), F32),
        in_specs=[SM] + [VM] * 4,
        out_specs=VM,
        compiler_params=pltpu.CompilerParams(vmem_limit_bytes=4 * MIB),
    )(idx, *[near(g) for g in got])


def solution(mesh):
    return jax.shard_map(
        shards,
        mesh=mesh,
        in_specs=(
            P(),
            P("tm", "row", None),
            P("tm", "row", None),
            P("tm", "row"),
            P("tm", None),
            P("tm"),
        ),
        out_specs=P("tm", "row"),
        check_vma=False,
    )
```

```python
import jax
import jax.numpy as jnp
from jax import lax
from jax.experimental import pallas as pl
from jax.experimental.pallas import tpu as pltpu
from jax.sharding import PartitionSpec as P

F32 = jnp.float32
BF16 = jnp.bfloat16
MIB = 1024 * 1024
VM = pl.BlockSpec(memory_space=pltpu.VMEM)
SM = pl.BlockSpec(memory_space=pltpu.SMEM)
N = 256
PAD = 16
R = N + PAD
Z, C, Y, X = range(4)
HALF = R // 2
ROWS = 4
SUB = 16
CHUNKS = ((5, 5), (3, 3))
SEGS = tuple(n for chunk in CHUNKS for n in chunk)
SIZES = tuple(sum(chunk) for chunk in CHUNKS)
ENDS = tuple(sum(SEGS[: i + 1]) for i in range(len(SEGS)))


def split(x):
    hi = x.astype(BF16)
    return hi, (x - hi.astype(F32)).astype(BF16)


def dot_nn(a, b):
    return lax.dot_general(a, b, (((1,), (0,)), ((), ())), preferred_element_type=F32)


def dot_nt(a, b):
    return lax.dot_general(a, b, (((1,), (1,)), ((), ())), preferred_element_type=F32)


def mm(a, b, dot=dot_nn):
    ah, al = split(a)
    bh, bl = split(b)
    return dot(ah, bh) + dot(al, bh) + dot(ah, bl)


def then(first, second):
    out = mm(first, second[:N])
    return jnp.concatenate([out[:N], out[N:] + second[N:]], axis=0)


def apply(s, m):
    return mm(s, m[:N]) + m[N:]


def eye_map():
    r = lax.broadcasted_iota(jnp.int32, (R, N), 0)
    c = lax.broadcasted_iota(jnp.int32, (R, N), 1)
    return jnp.where(r == c, 1.0, 0.0).astype(F32)


FAR = pl.BlockSpec(memory_space=pltpu.HBM)


def near(x):
    return pltpu.with_memory_space_constraint(x, pltpu.VMEM)


def call(kernel, outs, idx, args, scratch=(), far=(), mib=8):
    outs = [o if isinstance(o[0], tuple) else (o, F32) for o in outs]
    return pl.pallas_call(
        kernel,
        out_shape=[pltpu.VMEM(s, t) for s, t in outs],
        in_specs=[SM] + [FAR] * len(far) + [VM] * len(args),
        out_specs=[VM] * len(outs),
        scratch_shapes=list(scratch),
        compiler_params=pltpu.CompilerParams(vmem_limit_bytes=mib * MIB),
    )(idx, *[pltpu.with_memory_space_constraint(f, pltpu.HBM) for f in far], *[near(a) for a in args])


BIN_M = 256


def bin_kernel(rid_ref, obs_ref, out_ref, rhs, acc):
    i = pl.program_id(0)
    n_m = pl.num_programs(0)

    @pl.when(i == 0)
    def _():
        x = obs_ref[...]
        hi = x.astype(BF16)
        rest = x - hi.astype(F32)
        mid = rest.astype(BF16)
        low = (rest - mid.astype(F32)).astype(BF16)
        rhs[...] = jnp.concatenate([hi, mid, low, jnp.zeros_like(hi)], axis=0)

    rows = lax.broadcasted_iota(jnp.int32, (BIN_M, rid_ref.shape[1]), 0) + i * BIN_M
    onehot = jnp.where(rows == rid_ref[...], 1.0, 0.0).astype(BF16)
    got = dot_nt(onehot, rhs[...])
    a = got[:, :128] + got[:, 128:]
    acc[pl.ds(pl.multiple_of(i * BIN_M, BIN_M), BIN_M), :] = a + pltpu.roll(a, 64, 1)

    @pl.when(i == n_m - 1)
    def _():
        part = out_ref.shape[0]
        low_half = lax.broadcasted_iota(jnp.int32, (part, 128), 1) < 64
        for h in range(2):
            even = acc[2 * h * part : (2 * h + 1) * part, :]
            odd = acc[(2 * h + 1) * part : (2 * h + 2) * part, :]
            out_ref[:, h * 128 : (h + 1) * 128] = jnp.where(low_half, even, odd)


def binned(rid, observed):
    n_bins = 2048
    width, obs_rows = observed.shape
    return pl.pallas_call(
        bin_kernel,
        out_shape=jax.ShapeDtypeStruct((n_bins // 4, N), F32),
        grid=(n_bins // BIN_M,),
        in_specs=[
            pl.BlockSpec((1, obs_rows), lambda i: (0, 0)),
            pl.BlockSpec((width, obs_rows), lambda i: (0, 0)),
        ],
        out_specs=pl.BlockSpec((n_bins // 4, N), lambda i: (0, 0)),
        scratch_shapes=[pltpu.VMEM((4 * width, obs_rows), BF16), pltpu.VMEM((n_bins, 128), F32)],
        compiler_params=pltpu.CompilerParams(vmem_limit_bytes=24 * MIB),
    )(rid, observed)


def own_copy(z, flat, own, start, sem):
    return pltpu.make_async_copy(flat.at[pl.ds(pl.multiple_of(z * (SUB * 64) + start * 64, 64), own.shape[0])], own, sem)


def assemble(z, parts, ah, al, own=None):
    for d in (1, 2, 3, 0):
        slot = lax.rem(z - d + ROWS, ROWS)
        rows = pl.ds(pl.multiple_of(slot * 64, 64), 64)
        if d == 0:
            own.wait()
        for k in range(ah.shape[0]):
            hi, lo = split(parts[d][k * 64 : (k + 1) * 64, :])
            ah[k, rows, :] = hi
            al[k, rows, :] = lo


def by_step(x, ah, al):
    xh, xl = split(x)
    return dot_nt(xh, ah) + dot_nt(xl, ah) + dot_nt(xh, al)


def chains(lengths, ah, al, pref):
    eye = jnp.where(
        lax.broadcasted_iota(jnp.int32, (N, N), 0) == lax.broadcasted_iota(jnp.int32, (N, N), 1), 1.0, 0.0
    ).astype(BF16)
    for t in range(max(lengths)):
        for c, length in enumerate(lengths):
            if t >= length:
                continue
            k = sum(lengths[:c]) + t
            if t == 0:
                pref[k] = dot_nt(eye, ah[k]) + dot_nt(eye, al[k])
            else:
                pref[k] = by_step(pref[k - 1], ah[k], al[k])


def first_kernel(idx, flat, gains, a1, a2, a3, pref, ah, al, both, staged, own, sems):
    z = idx[Z]
    late = pltpu.make_async_copy(gains, staged, sems.at[1])
    copy = own_copy(z, flat, own, 0, sems.at[0])
    copy.start()
    late.start()
    assemble(z, (own, a1, a2, a3), ah, al, copy)
    chains(CHUNKS[0], ah, al, pref)
    both[...] = mm(pref[CHUNKS[0][0] - 1], pref[SIZES[0] - 1])
    late.wait()


def second_kernel(idx, flat, a1, a2, a3, both, pref, ah, al, four, three, own, sem):
    z = idx[Z]
    copy = own_copy(z, flat, own, SIZES[0], sem)
    copy.start()
    assemble(z, (own, a1, a2, a3), ah, al, copy)
    chains(CHUNKS[1], ah, al, pref)
    three[...] = mm(both[...], pref[CHUNKS[1][0] - 1])
    four[...] = mm(three[...], pref[SIZES[1] - 1])


def third_kernel(idx, b0, b1, b2, b3, p01, ah01, al01, p23, ah23, al23, four, shifts, whole, b_s):
    z = idx[Z]
    for d, b in enumerate((b0, b1, b2, b3)):
        b_s[lax.rem(z - d + ROWS, ROWS)] = b[...]
    b = jnp.concatenate([b_s[i, :, :64] for i in range(ROWS)], axis=1)
    first = lax.broadcasted_iota(jnp.int32, (PAD, N), 0) == 0

    def row(k):
        return jnp.where(first, b[k : k + 1, :], 0.0)

    mats = [(ah01, al01, i) for i in range(SIZES[0])] + [(ah23, al23, i) for i in range(SIZES[1])]
    starts = [end - n for end, n in zip(ENDS, SEGS)]
    p = [row(k) for k in starts]
    for c, k in enumerate(starts):
        shifts[k : k + 1, :] = p[c][:1]
    for t in range(1, max(SEGS)):
        for c, start in enumerate(starts):
            if t >= SEGS[c]:
                continue
            k = start + t
            h, l, i = mats[k]
            p[c] = by_step(p[c], h[i], l[i]) + row(k)
            shifts[k : k + 1, :] = p[c][:1]
    v = mm(p[0], p01[SIZES[0] - 1]) + p[1]
    v = mm(v, p23[CHUNKS[1][0] - 1]) + p[2]
    v = mm(v, p23[SIZES[1] - 1]) + p[3]
    whole[:N, :] = four[...]
    whole[N:, :] = v


def combine(pos, m_s, before):
    m01 = then(m_s[0], m_s[1])
    m23 = then(m_s[2], m_s[3])
    before[...] = eye_map()

    @pl.when(pos == 1)
    def _():
        before[...] = m_s[0]

    @pl.when(pos == 2)
    def _():
        before[...] = m01

    @pl.when(pos == 3)
    def _():
        before[...] = then(m01, m_s[2])

    return then(m01, m23)


def four_kernel(idx, m0, m1, m2, m3, total, before, m_s):
    pos = idx[Z]
    for d, m in enumerate((m0, m1, m2, m3)):
        m_s[lax.rem(pos - d + 4, 4)] = m[...]
    total[...] = combine(pos, m_s, before)


def half_rows(c):
    return pl.ds(pl.multiple_of(c * HALF, 8), HALF)


def join_halves(pos, c, mine, others, m_s):
    for d, (m, o) in enumerate(zip(mine, others)):
        slot = lax.rem(pos - d + 3, 4)
        m_s[slot, half_rows(c), :] = m[...]
        m_s[slot, half_rows(1 - c), :] = o[...]


def halves_kernel(idx, own, h1, h2, h3, o1, o2, o3, half, before, m_s):
    pos, c = idx[Y], idx[C]
    m_s[pos] = own[...]
    join_halves(pos, c, (h1, h2, h3), (o1, o2, o3), m_s)
    m_s[4] = combine(pos, m_s, before)
    half[...] = m_s[4, half_rows(c), :]


def pair_kernel(idx, own, other, before_in, total, half, before):
    c = idx[C]
    swap = c == 1

    @pl.when(swap)
    def _():
        total[...] = then(other[...], own[...])
        before[...] = then(other[...], before_in[...])

    @pl.when(jnp.logical_not(swap))
    def _():
        total[...] = then(own[...], other[...])
        before[...] = before_in[...]

    half[...] = total[half_rows(c), :]


def fold_kernel(idx, first, second, out):
    out[...] = then(first[...], second[...])


def states_kernel(
    idx, prior, h1, h2, h3, g1, g2, g3, before, p01, p23, shifts, o0, o1, o2, o3, st_s, m_s, s_s
):
    z, pos = idx[Z], idx[X]
    join_halves(pos, idx[C], (h1, h2, h3), (g1, g2, g3), m_s)
    s_s[...] = jnp.where(lax.broadcasted_iota(jnp.int32, (PAD, N), 0) == 0, prior[...], 0.0)
    for i in range(3):

        @pl.when(i < pos)
        def _(i=i):
            s_s[...] = apply(s_s[...], m_s[i])

    s = apply(s_s[...], before[...])
    eye = lax.broadcasted_iota(jnp.int32, (N, N), 0) == lax.broadcasted_iota(jnp.int32, (N, N), 1)
    first = lax.broadcasted_iota(jnp.int32, (PAD, N), 0) == 0
    prefs = [(p01, i) for i in range(SIZES[0])] + [(p23, i) for i in range(SIZES[1])]
    for end, n in zip(ENDS, SEGS):
        col = jnp.sum(jnp.where(eye, s[0:1, :], 0.0), axis=1, keepdims=True)
        for k in range(end - n, end):
            m, i = prefs[k]
            row = jnp.sum(m[i] * col, axis=0, keepdims=True) + shifts[k : k + 1, :]
            for j in range(ROWS):
                st_s[j, k : k + 1, :] = row[:, j * 64 : (j + 1) * 64]
        if end < SUB:
            m, i = prefs[end - 1]
            s = mm(s, m[i]) + jnp.where(first, shifts[end - 1 : end, :], 0.0)
    for d, o in enumerate((o0, o1, o2, o3)):
        o[...] = st_s[lax.rem(z + d, ROWS)]


def send_copies(z, flat, outs, start, count, sems):
    copies = []
    for d, o in enumerate(outs, 1):
        at = lax.rem(z + d, ROWS) * (SUB * 64) + start * 64
        source = flat.at[pl.ds(pl.multiple_of(at, 64), count * 64)]
        copies.append(pltpu.make_async_copy(source, o.at[pl.ds(0, count * 64)], sems.at[d - 1]))
    for copy in copies:
        copy.start()
    return copies


def send_a_kernel(idx, flat, o1, o2, o3, sems):
    for copy in send_copies(idx[Z], flat, (o1, o2, o3), 0, SIZES[0], sems):
        copy.wait()


def sum_kernel(idx, sums, info):
    info[...] = jnp.sum(sums[...], axis=0)


def send_b_kernel(idx, flat, o1, o2, o3, sems):
    for copy in send_copies(idx[Z], flat, (o1, o2, o3), SIZES[0], SIZES[1], sems):
        copy.wait()


def offset_kernel(idx, g, i0, r1, r2, r3, o0, o1, o2, o3, info_s, off_s):
    z = idx[Z]
    info_s[z] = i0[...]
    for d, r in ((1, r1), (2, r2), (3, r3)):
        info_s[lax.rem(z - d + ROWS, ROWS)] = r[...]
    lane = lax.broadcasted_iota(jnp.int32, (64, 128), 1)
    for q in range(4):
        full = jnp.concatenate([info_s[i, :, q * 64 : (q + 1) * 64] for i in range(ROWS)], axis=1)
        acc = jnp.zeros((64, 128), F32)
        for k in range(16):
            col = jnp.sum(g[16 * q + k] * full[k : k + 1, :], axis=1, keepdims=True)
            acc = jnp.where(lane == k, col, acc)
        off_s[q] = jnp.concatenate([acc, jnp.zeros((64, 128), F32)], axis=0).T[:16, :]
    for d, o in enumerate((o0, o1, o2, o3)):
        o[:, :128] = off_s[lax.rem(z + d, ROWS)]
        o[:, 128:] = jnp.zeros((16, 128), F32)


def place_kernel(idx, r0, r1, r2, r3, out):
    z = idx[Z]
    for d, r in enumerate((r0, r1, r2, r3)):
        slot = lax.rem(z - d + ROWS, ROWS)
        out[pl.ds(pl.multiple_of(slot * SUB, SUB), SUB), :] = r[...]


def along_row(x, d):
    return lax.ppermute(x, "row", [(i, (i + d) % ROWS) for i in range(ROWS)])


def shards(prior, dynamics, gains, observed, owner, step):
    tm = lax.axis_index("tm").astype(jnp.int32)
    z = lax.axis_index("row").astype(jnp.int32)
    idx = jnp.stack([z, tm & 1, (tm >> 1) & 3, tm >> 3])
    prior = prior.reshape(1, N)
    flat = dynamics.reshape(ROWS * SUB * 64, N)
    dma3 = pltpu.SemaphoreType.DMA((3,))

    def along_rows(blocks):
        return [along_row(b, d) for d, b in enumerate(blocks, 1)]

    part_a = along_rows(call(send_a_kernel, [(SIZES[0] * 64, N)] * 3, idx, (), [dma3], far=(flat,)))

    rid = owner[:, 0] * 16 + step % 16 + 512 * (step // 16)
    partial = binned(rid.reshape(1, -1), observed.T)
    sums = lax.all_to_all(partial, "tm", 0, 0, tiled=True).reshape(32, 16, N)
    sums, idx, prior, *part_a = lax.optimization_barrier((sums, idx, prior, *part_a))

    (info,) = call(sum_kernel, [(16, N)], idx, (sums,))
    infos = along_rows([info] * 3)
    sent_b = call(send_b_kernel, [(SIZES[1] * 64, N)] * 3, idx, (), [dma3], far=(flat,))
    infos, sent_b = lax.optimization_barrier((infos, sent_b))
    part_b = along_rows(sent_b)
    p01, ah01, al01, both, staged = call(
        first_kernel,
        [(SIZES[0], N, N), ((SIZES[0], N, N), BF16), ((SIZES[0], N, N), BF16), (N, N), gains.shape],
        idx,
        part_a,
        [pltpu.VMEM((SIZES[0] * 64, N), F32), pltpu.SemaphoreType.DMA((2,))],
        far=(flat, gains),
    )
    offs = call(
        offset_kernel,
        [(16, N)] * 4,
        idx,
        (staged, info, *infos),
        [pltpu.VMEM((ROWS, 16, N), F32), pltpu.VMEM((ROWS, 16, 128), F32)],
    )
    offs = [offs[0], *along_rows(offs[1:])]
    p23, ah23, al23, four = call(
        second_kernel,
        [(SIZES[1], N, N), ((SIZES[1], N, N), BF16), ((SIZES[1], N, N), BF16), (N, N)],
        idx,
        (*part_b, both),
        [pltpu.VMEM((N, N), F32), pltpu.VMEM((SIZES[1] * 64, N), F32), pltpu.SemaphoreType.DMA],
        far=(flat,),
    )
    shifts, whole = call(
        third_kernel,
        [(SUB, N), (R, N)],
        idx,
        (*offs, p01, ah01, al01, p23, ah23, al23, four),
        [pltpu.VMEM((ROWS, 16, N), F32)],
    )

    block, before = call(
        four_kernel,
        [(R, N), (R, N)],
        idx,
        (whole, *[along_row(whole, d) for d in (1, 2, 3)]),
        [pltpu.VMEM((4, R, N), F32)],
    )

    def other_core(m):
        return lax.ppermute(m, "tm", [(i, i ^ 1) for i in range(32)])

    def along_tm(m, d, n, stride):
        places = [(i, i - i % (n * stride) + (i + d * stride) % (n * stride)) for i in range(32)]
        return lax.ppermute(m, "tm", places)

    column, half, before = call(
        pair_kernel, [(R, N), (HALF, N), (R, N)], idx, (block, other_core(block), before)
    )
    halves = [along_tm(half, d, 4, 2) for d in (1, 2, 3)]
    half, ybefore = call(
        halves_kernel,
        [(HALF, N), (R, N)],
        idx,
        (column, *halves, *[other_core(h) for h in halves]),
        [pltpu.VMEM((5, R, N), F32)],
    )
    halves = [along_tm(half, d, 4, 8) for d in (1, 2, 3)]
    (before,) = call(fold_kernel, [(R, N)], idx, (ybefore, before))
    outs = call(
        states_kernel,
        [(SUB, 64)] * 4,
        idx,
        (prior, *halves, *[other_core(h) for h in halves], before, p01, p23, shifts),
        [pltpu.VMEM((ROWS, SUB, 64), F32), pltpu.VMEM((4, R, N), F32), pltpu.VMEM((PAD, N), F32)],
    )
    got = [outs[0], *along_rows(outs[1:])]
    return pl.pallas_call(
        place_kernel,
        out_shape=jax.ShapeDtypeStruct((64, 64), F32),
        in_specs=[SM] + [VM] * 4,
        out_specs=VM,
        compiler_params=pltpu.CompilerParams(vmem_limit_bytes=4 * MIB),
    )(idx, *[near(g) for g in got])


def solution(mesh):
    return jax.shard_map(
        shards,
        mesh=mesh,
        in_specs=(
            P(),
            P("tm", "row", None),
            P("tm", "row", None),
            P("tm", "row"),
            P("tm", None),
            P("tm"),
        ),
        out_specs=P("tm", "row"),
        check_vma=False,
    )
```

```python
import jax
import jax.numpy as jnp
from jax import lax
from jax.experimental import pallas as pl
from jax.experimental.pallas import tpu as pltpu
from jax.sharding import PartitionSpec as P

F32 = jnp.float32
BF16 = jnp.bfloat16
MIB = 1024 * 1024
VM = pl.BlockSpec(memory_space=pltpu.VMEM)
SM = pl.BlockSpec(memory_space=pltpu.SMEM)
N = 256
PAD = 16
R = N + PAD
Z, C, Y, X = range(4)
HALF = R // 2
ROWS = 4
SUB = 16
CHUNKS = ((4, 4, 4), (2, 2))
SEGS = tuple(n for chunk in CHUNKS for n in chunk)
SIZES = tuple(sum(chunk) for chunk in CHUNKS)
ENDS = tuple(sum(SEGS[: i + 1]) for i in range(len(SEGS)))


def split(x):
    hi = x.astype(BF16)
    return hi, (x - hi.astype(F32)).astype(BF16)


def dot_nn(a, b):
    return lax.dot_general(a, b, (((1,), (0,)), ((), ())), preferred_element_type=F32)


def dot_nt(a, b):
    return lax.dot_general(a, b, (((1,), (1,)), ((), ())), preferred_element_type=F32)


def mm(a, b, dot=dot_nn):
    ah, al = split(a)
    bh, bl = split(b)
    return dot(ah, bh) + dot(al, bh) + dot(ah, bl)


def then(first, second):
    out = mm(first, second[:N])
    return jnp.concatenate([out[:N], out[N:] + second[N:]], axis=0)


def apply(s, m):
    return mm(s, m[:N]) + m[N:]


def eye_map():
    r = lax.broadcasted_iota(jnp.int32, (R, N), 0)
    c = lax.broadcasted_iota(jnp.int32, (R, N), 1)
    return jnp.where(r == c, 1.0, 0.0).astype(F32)


FAR = pl.BlockSpec(memory_space=pltpu.HBM)


def near(x):
    return pltpu.with_memory_space_constraint(x, pltpu.VMEM)


def call(kernel, outs, idx, args, scratch=(), far=(), mib=8):
    outs = [o if isinstance(o[0], tuple) else (o, F32) for o in outs]
    return pl.pallas_call(
        kernel,
        out_shape=[pltpu.VMEM(s, t) for s, t in outs],
        in_specs=[SM] + [FAR] * len(far) + [VM] * len(args),
        out_specs=[VM] * len(outs),
        scratch_shapes=list(scratch),
        compiler_params=pltpu.CompilerParams(vmem_limit_bytes=mib * MIB),
    )(idx, *[pltpu.with_memory_space_constraint(f, pltpu.HBM) for f in far], *[near(a) for a in args])


BIN_M = 256


def bin_kernel(rid_ref, obs_ref, out_ref, rhs, acc):
    i = pl.program_id(0)
    n_m = pl.num_programs(0)

    @pl.when(i == 0)
    def _():
        x = obs_ref[...]
        hi = x.astype(BF16)
        rest = x - hi.astype(F32)
        mid = rest.astype(BF16)
        low = (rest - mid.astype(F32)).astype(BF16)
        rhs[...] = jnp.concatenate([hi, mid, low, jnp.zeros_like(hi)], axis=0)

    rows = lax.broadcasted_iota(jnp.int32, (BIN_M, rid_ref.shape[1]), 0) + i * BIN_M
    onehot = jnp.where(rows == rid_ref[...], 1.0, 0.0).astype(BF16)
    got = dot_nt(onehot, rhs[...])
    a = got[:, :128] + got[:, 128:]
    acc[pl.ds(pl.multiple_of(i * BIN_M, BIN_M), BIN_M), :] = a + pltpu.roll(a, 64, 1)

    @pl.when(i == n_m - 1)
    def _():
        part = out_ref.shape[0]
        low_half = lax.broadcasted_iota(jnp.int32, (part, 128), 1) < 64
        for h in range(2):
            even = acc[2 * h * part : (2 * h + 1) * part, :]
            odd = acc[(2 * h + 1) * part : (2 * h + 2) * part, :]
            out_ref[:, h * 128 : (h + 1) * 128] = jnp.where(low_half, even, odd)


def binned(rid, observed):
    n_bins = 2048
    width, obs_rows = observed.shape
    return pl.pallas_call(
        bin_kernel,
        out_shape=jax.ShapeDtypeStruct((n_bins // 4, N), F32),
        grid=(n_bins // BIN_M,),
        in_specs=[
            pl.BlockSpec((1, obs_rows), lambda i: (0, 0)),
            pl.BlockSpec((width, obs_rows), lambda i: (0, 0)),
        ],
        out_specs=pl.BlockSpec((n_bins // 4, N), lambda i: (0, 0)),
        scratch_shapes=[pltpu.VMEM((4 * width, obs_rows), BF16), pltpu.VMEM((n_bins, 128), F32)],
        compiler_params=pltpu.CompilerParams(vmem_limit_bytes=24 * MIB),
    )(rid, observed)


def own_copy(z, flat, own, start, sem):
    return pltpu.make_async_copy(flat.at[pl.ds(pl.multiple_of(z * (SUB * 64) + start * 64, 64), own.shape[0])], own, sem)


def assemble(z, parts, ah, al, own=None):
    for d in (1, 2, 3, 0):
        slot = lax.rem(z - d + ROWS, ROWS)
        rows = pl.ds(pl.multiple_of(slot * 64, 64), 64)
        if d == 0:
            own.wait()
        for k in range(ah.shape[0]):
            hi, lo = split(parts[d][k * 64 : (k + 1) * 64, :])
            ah[k, rows, :] = hi
            al[k, rows, :] = lo


def by_step(x, ah, al):
    xh, xl = split(x)
    return dot_nt(xh, ah) + dot_nt(xl, ah) + dot_nt(xh, al)


def chains(lengths, ah, al, pref):
    eye = jnp.where(
        lax.broadcasted_iota(jnp.int32, (N, N), 0) == lax.broadcasted_iota(jnp.int32, (N, N), 1), 1.0, 0.0
    ).astype(BF16)
    for t in range(max(lengths)):
        for c, length in enumerate(lengths):
            if t >= length:
                continue
            k = sum(lengths[:c]) + t
            if t == 0:
                pref[k] = dot_nt(eye, ah[k]) + dot_nt(eye, al[k])
            else:
                pref[k] = by_step(pref[k - 1], ah[k], al[k])


def first_kernel(idx, flat, gains, a1, a2, a3, pref, ah, al, tail, staged, own, sems):
    z = idx[Z]
    late = pltpu.make_async_copy(gains, staged, sems.at[1])
    copy = own_copy(z, flat, own, 0, sems.at[0])
    copy.start()
    late.start()
    assemble(z, (own, a1, a2, a3), ah, al, copy)
    chains(CHUNKS[0], ah, al, pref)
    tail[0] = mm(pref[ENDS[1] - 1], pref[ENDS[2] - 1])
    tail[1] = mm(pref[ENDS[0] - 1], tail[0])
    late.wait()


def second_kernel(idx, flat, a1, a2, a3, tail, pref, ah, al, last, own, sem):
    z = idx[Z]
    copy = own_copy(z, flat, own, SIZES[0], sem)
    copy.start()
    assemble(z, (own, a1, a2, a3), ah, al, copy)
    chains(CHUNKS[1], ah, al, pref)
    last[0] = mm(pref[CHUNKS[1][0] - 1], pref[SIZES[1] - 1])
    last[1] = mm(tail[1], last[0])


def third_kernel(idx, b0, b1, b2, b3, p01, ah01, al01, tail, p23, ah23, al23, last, shifts, whole, b_s):
    z = idx[Z]
    for d, b in enumerate((b0, b1, b2, b3)):
        b_s[lax.rem(z - d + ROWS, ROWS)] = b[...]
    b = jnp.concatenate([b_s[i, :, :64] for i in range(ROWS)], axis=1)
    first = lax.broadcasted_iota(jnp.int32, (PAD, N), 0) == 0

    def row(k):
        return jnp.where(first, b[k : k + 1, :], 0.0)

    mats = [(ah01, al01, i) for i in range(SIZES[0])] + [(ah23, al23, i) for i in range(SIZES[1])]
    starts = [end - n for end, n in zip(ENDS, SEGS)]
    p = [row(k) for k in starts]
    for c, k in enumerate(starts):
        shifts[k : k + 1, :] = p[c][:1]
    for t in range(1, max(SEGS)):
        for c, start in enumerate(starts):
            if t >= SEGS[c]:
                continue
            k = start + t
            h, l, i = mats[k]
            p[c] = by_step(p[c], h[i], l[i]) + row(k)
            shifts[k : k + 1, :] = p[c][:1]
    v = mm(p[0], tail[0]) + mm(p[1], p01[SIZES[0] - 1]) + p[2]
    v = mm(v, last[0]) + (mm(p[3], p23[SIZES[1] - 1]) + p[4])
    whole[:N, :] = last[1]
    whole[N:, :] = v


def combine(pos, m_s, before):
    m01 = then(m_s[0], m_s[1])
    m23 = then(m_s[2], m_s[3])
    before[...] = eye_map()

    @pl.when(pos == 1)
    def _():
        before[...] = m_s[0]

    @pl.when(pos == 2)
    def _():
        before[...] = m01

    @pl.when(pos == 3)
    def _():
        before[...] = then(m01, m_s[2])

    return then(m01, m23)


def four_kernel(idx, m0, m1, m2, m3, total, before, m_s):
    pos = idx[Z]
    for d, m in enumerate((m0, m1, m2, m3)):
        m_s[lax.rem(pos - d + 4, 4)] = m[...]
    total[...] = combine(pos, m_s, before)


def half_rows(c):
    return pl.ds(pl.multiple_of(c * HALF, 8), HALF)


def join_halves(pos, c, mine, others, m_s):
    for d, (m, o) in enumerate(zip(mine, others)):
        slot = lax.rem(pos - d + 3, 4)
        m_s[slot, half_rows(c), :] = m[...]
        m_s[slot, half_rows(1 - c), :] = o[...]


def halves_kernel(idx, own, h1, h2, h3, o1, o2, o3, half, before, m_s):
    pos, c = idx[Y], idx[C]
    m_s[pos] = own[...]
    join_halves(pos, c, (h1, h2, h3), (o1, o2, o3), m_s)
    m_s[4] = combine(pos, m_s, before)
    half[...] = m_s[4, half_rows(c), :]


def pair_kernel(idx, own, other, before_in, total, half, before):
    c = idx[C]
    swap = c == 1

    @pl.when(swap)
    def _():
        total[...] = then(other[...], own[...])
        before[...] = then(other[...], before_in[...])

    @pl.when(jnp.logical_not(swap))
    def _():
        total[...] = then(own[...], other[...])
        before[...] = before_in[...]

    half[...] = total[half_rows(c), :]


def fold_kernel(idx, first, second, out):
    out[...] = then(first[...], second[...])


def states_kernel(
    idx, prior, h1, h2, h3, g1, g2, g3, before, p01, p23, shifts, o0, o1, o2, o3, st_s, m_s, s_s
):
    z, pos = idx[Z], idx[X]
    join_halves(pos, idx[C], (h1, h2, h3), (g1, g2, g3), m_s)
    s_s[...] = jnp.where(lax.broadcasted_iota(jnp.int32, (PAD, N), 0) == 0, prior[...], 0.0)
    for i in range(3):

        @pl.when(i < pos)
        def _(i=i):
            s_s[...] = apply(s_s[...], m_s[i])

    s = apply(s_s[...], before[...])
    eye = lax.broadcasted_iota(jnp.int32, (N, N), 0) == lax.broadcasted_iota(jnp.int32, (N, N), 1)
    first = lax.broadcasted_iota(jnp.int32, (PAD, N), 0) == 0
    prefs = [(p01, i) for i in range(SIZES[0])] + [(p23, i) for i in range(SIZES[1])]
    for end, n in zip(ENDS, SEGS):
        col = jnp.sum(jnp.where(eye, s[0:1, :], 0.0), axis=1, keepdims=True)
        for k in range(end - n, end):
            m, i = prefs[k]
            row = jnp.sum(m[i] * col, axis=0, keepdims=True) + shifts[k : k + 1, :]
            for j in range(ROWS):
                st_s[j, k : k + 1, :] = row[:, j * 64 : (j + 1) * 64]
        if end < SUB:
            m, i = prefs[end - 1]
            s = mm(s, m[i]) + jnp.where(first, shifts[end - 1 : end, :], 0.0)
    for d, o in enumerate((o0, o1, o2, o3)):
        o[...] = st_s[lax.rem(z + d, ROWS)]


def send_copies(z, flat, outs, start, count, sems):
    copies = []
    for d, o in enumerate(outs, 1):
        at = lax.rem(z + d, ROWS) * (SUB * 64) + start * 64
        source = flat.at[pl.ds(pl.multiple_of(at, 64), count * 64)]
        copies.append(pltpu.make_async_copy(source, o.at[pl.ds(0, count * 64)], sems.at[d - 1]))
    for copy in copies:
        copy.start()
    return copies


def send_a_kernel(idx, flat, o1, o2, o3, sems):
    for copy in send_copies(idx[Z], flat, (o1, o2, o3), 0, SIZES[0], sems):
        copy.wait()


def sum_kernel(idx, sums, info):
    info[...] = jnp.sum(sums[...], axis=0)


def send_b_kernel(idx, flat, o1, o2, o3, sems):
    for copy in send_copies(idx[Z], flat, (o1, o2, o3), SIZES[0], SIZES[1], sems):
        copy.wait()


def offset_kernel(idx, g, i0, r1, r2, r3, o0, o1, o2, o3, info_s, off_s):
    z = idx[Z]
    info_s[z] = i0[...]
    for d, r in ((1, r1), (2, r2), (3, r3)):
        info_s[lax.rem(z - d + ROWS, ROWS)] = r[...]
    lane = lax.broadcasted_iota(jnp.int32, (64, 128), 1)
    for q in range(4):
        full = jnp.concatenate([info_s[i, :, q * 64 : (q + 1) * 64] for i in range(ROWS)], axis=1)
        acc = jnp.zeros((64, 128), F32)
        for k in range(16):
            col = jnp.sum(g[16 * q + k] * full[k : k + 1, :], axis=1, keepdims=True)
            acc = jnp.where(lane == k, col, acc)
        off_s[q] = jnp.concatenate([acc, jnp.zeros((64, 128), F32)], axis=0).T[:16, :]
    for d, o in enumerate((o0, o1, o2, o3)):
        o[:, :128] = off_s[lax.rem(z + d, ROWS)]
        o[:, 128:] = jnp.zeros((16, 128), F32)


def place_kernel(idx, r0, r1, r2, r3, out):
    z = idx[Z]
    for d, r in enumerate((r0, r1, r2, r3)):
        slot = lax.rem(z - d + ROWS, ROWS)
        out[pl.ds(pl.multiple_of(slot * SUB, SUB), SUB), :] = r[...]


def along_row(x, d):
    return lax.ppermute(x, "row", [(i, (i + d) % ROWS) for i in range(ROWS)])


def shards(prior, dynamics, gains, observed, owner, step):
    tm = lax.axis_index("tm").astype(jnp.int32)
    z = lax.axis_index("row").astype(jnp.int32)
    idx = jnp.stack([z, tm & 1, (tm >> 1) & 3, tm >> 3])
    prior = prior.reshape(1, N)
    flat = dynamics.reshape(ROWS * SUB * 64, N)
    dma3 = pltpu.SemaphoreType.DMA((3,))

    def along_rows(blocks):
        return [along_row(b, d) for d, b in enumerate(blocks, 1)]

    part_a = along_rows(call(send_a_kernel, [(SIZES[0] * 64, N)] * 3, idx, (), [dma3], far=(flat,)))

    rid = owner[:, 0] * 16 + step % 16 + 512 * (step // 16)
    partial = binned(rid.reshape(1, -1), observed.T)
    sums = lax.all_to_all(partial, "tm", 0, 0, tiled=True).reshape(32, 16, N)
    (info,) = call(sum_kernel, [(16, N)], idx, (sums,))
    infos = along_rows([info] * 3)
    sent_b = call(send_b_kernel, [(SIZES[1] * 64, N)] * 3, idx, (), [dma3], far=(flat,))
    infos, sent_b, part_a, idx, prior = lax.optimization_barrier((infos, sent_b, part_a, idx, prior))
    part_b = along_rows(sent_b)
    p01, ah01, al01, tail, staged = call(
        first_kernel,
        [(SIZES[0], N, N), ((SIZES[0], N, N), BF16), ((SIZES[0], N, N), BF16), (2, N, N), gains.shape],
        idx,
        part_a,
        [pltpu.VMEM((SIZES[0] * 64, N), F32), pltpu.SemaphoreType.DMA((2,))],
        far=(flat, gains),
    )
    offs = call(
        offset_kernel,
        [(16, N)] * 4,
        idx,
        (staged, info, *infos),
        [pltpu.VMEM((ROWS, 16, N), F32), pltpu.VMEM((ROWS, 16, 128), F32)],
    )
    offs = [offs[0], *along_rows(offs[1:])]
    p23, ah23, al23, last = call(
        second_kernel,
        [(SIZES[1], N, N), ((SIZES[1], N, N), BF16), ((SIZES[1], N, N), BF16), (2, N, N)],
        idx,
        (*part_b, tail),
        [pltpu.VMEM((SIZES[1] * 64, N), F32), pltpu.SemaphoreType.DMA],
        far=(flat,),
    )
    shifts, whole = call(
        third_kernel,
        [(SUB, N), (R, N)],
        idx,
        (*offs, p01, ah01, al01, tail, p23, ah23, al23, last),
        [pltpu.VMEM((ROWS, 16, N), F32)],
    )

    block, before = call(
        four_kernel,
        [(R, N), (R, N)],
        idx,
        (whole, *[along_row(whole, d) for d in (1, 2, 3)]),
        [pltpu.VMEM((4, R, N), F32)],
    )

    def other_core(m):
        return lax.ppermute(m, "tm", [(i, i ^ 1) for i in range(32)])

    def along_tm(m, d, n, stride):
        places = [(i, i - i % (n * stride) + (i + d * stride) % (n * stride)) for i in range(32)]
        return lax.ppermute(m, "tm", places)

    column, half, before = call(
        pair_kernel, [(R, N), (HALF, N), (R, N)], idx, (block, other_core(block), before)
    )
    halves = [along_tm(half, d, 4, 2) for d in (1, 2, 3)]
    half, ybefore = call(
        halves_kernel,
        [(HALF, N), (R, N)],
        idx,
        (column, *halves, *[other_core(h) for h in halves]),
        [pltpu.VMEM((5, R, N), F32)],
    )
    halves = [along_tm(half, d, 4, 8) for d in (1, 2, 3)]
    (before,) = call(fold_kernel, [(R, N)], idx, (ybefore, before))
    outs = call(
        states_kernel,
        [(SUB, 64)] * 4,
        idx,
        (prior, *halves, *[other_core(h) for h in halves], before, p01, p23, shifts),
        [pltpu.VMEM((ROWS, SUB, 64), F32), pltpu.VMEM((4, R, N), F32), pltpu.VMEM((PAD, N), F32)],
    )
    got = [outs[0], *along_rows(outs[1:])]
    return pl.pallas_call(
        place_kernel,
        out_shape=jax.ShapeDtypeStruct((64, 64), F32),
        in_specs=[SM] + [VM] * 4,
        out_specs=VM,
        compiler_params=pltpu.CompilerParams(vmem_limit_bytes=4 * MIB),
    )(idx, *[near(g) for g in got])


def solution(mesh):
    return jax.shard_map(
        shards,
        mesh=mesh,
        in_specs=(
            P(),
            P("tm", "row", None),
            P("tm", "row", None),
            P("tm", "row"),
            P("tm", None),
            P("tm"),
        ),
        out_specs=P("tm", "row"),
        check_vma=False,
    )
```

```python
import jax
import jax.numpy as jnp
from jax import lax
from jax.experimental import pallas as pl
from jax.experimental.pallas import tpu as pltpu
from jax.sharding import PartitionSpec as P

F32 = jnp.float32
BF16 = jnp.bfloat16
MIB = 1024 * 1024
VM = pl.BlockSpec(memory_space=pltpu.VMEM)
SM = pl.BlockSpec(memory_space=pltpu.SMEM)
N = 256
PAD = 16
R = N + PAD
Z, C, Y, X = range(4)
HALF = R // 2
ROWS = 4
SUB = 16
CHUNKS = ((5, 5, 4), (2,))
SEGS = tuple(n for chunk in CHUNKS for n in chunk)
SIZES = tuple(sum(chunk) for chunk in CHUNKS)
ENDS = tuple(sum(SEGS[: i + 1]) for i in range(len(SEGS)))


def split(x):
    hi = x.astype(BF16)
    return hi, (x - hi.astype(F32)).astype(BF16)


def dot_nn(a, b):
    return lax.dot_general(a, b, (((1,), (0,)), ((), ())), preferred_element_type=F32)


def dot_nt(a, b):
    return lax.dot_general(a, b, (((1,), (1,)), ((), ())), preferred_element_type=F32)


def mm(a, b, dot=dot_nn):
    ah, al = split(a)
    bh, bl = split(b)
    return dot(ah, bh) + dot(al, bh) + dot(ah, bl)


def then(first, second):
    out = mm(first, second[:N])
    return jnp.concatenate([out[:N], out[N:] + second[N:]], axis=0)


def apply(s, m):
    return mm(s, m[:N]) + m[N:]


def eye_map():
    r = lax.broadcasted_iota(jnp.int32, (R, N), 0)
    c = lax.broadcasted_iota(jnp.int32, (R, N), 1)
    return jnp.where(r == c, 1.0, 0.0).astype(F32)


FAR = pl.BlockSpec(memory_space=pltpu.HBM)


def near(x):
    return pltpu.with_memory_space_constraint(x, pltpu.VMEM)


def call(kernel, outs, idx, args, scratch=(), far=(), mib=8):
    outs = [o if isinstance(o[0], tuple) else (o, F32) for o in outs]
    return pl.pallas_call(
        kernel,
        out_shape=[pltpu.VMEM(s, t) for s, t in outs],
        in_specs=[SM] + [FAR] * len(far) + [VM] * len(args),
        out_specs=[VM] * len(outs),
        scratch_shapes=list(scratch),
        compiler_params=pltpu.CompilerParams(vmem_limit_bytes=mib * MIB),
    )(idx, *[pltpu.with_memory_space_constraint(f, pltpu.HBM) for f in far], *[near(a) for a in args])


BIN_M = 256


def bin_kernel(rid_ref, obs_ref, out_ref, rhs, acc):
    i = pl.program_id(0)
    n_m = pl.num_programs(0)

    @pl.when(i == 0)
    def _():
        x = obs_ref[...]
        hi = x.astype(BF16)
        rest = x - hi.astype(F32)
        mid = rest.astype(BF16)
        low = (rest - mid.astype(F32)).astype(BF16)
        rhs[...] = jnp.concatenate([hi, mid, low, jnp.zeros_like(hi)], axis=0)

    rows = lax.broadcasted_iota(jnp.int32, (BIN_M, rid_ref.shape[1]), 0) + i * BIN_M
    onehot = jnp.where(rows == rid_ref[...], 1.0, 0.0).astype(BF16)
    got = dot_nt(onehot, rhs[...])
    a = got[:, :128] + got[:, 128:]
    acc[pl.ds(pl.multiple_of(i * BIN_M, BIN_M), BIN_M), :] = a + pltpu.roll(a, 64, 1)

    @pl.when(i == n_m - 1)
    def _():
        part = out_ref.shape[0]
        low_half = lax.broadcasted_iota(jnp.int32, (part, 128), 1) < 64
        for h in range(2):
            even = acc[2 * h * part : (2 * h + 1) * part, :]
            odd = acc[(2 * h + 1) * part : (2 * h + 2) * part, :]
            out_ref[:, h * 128 : (h + 1) * 128] = jnp.where(low_half, even, odd)


def binned(rid, observed):
    n_bins = 2048
    width, obs_rows = observed.shape
    return pl.pallas_call(
        bin_kernel,
        out_shape=jax.ShapeDtypeStruct((n_bins // 4, N), F32),
        grid=(n_bins // BIN_M,),
        in_specs=[
            pl.BlockSpec((1, obs_rows), lambda i: (0, 0)),
            pl.BlockSpec((width, obs_rows), lambda i: (0, 0)),
        ],
        out_specs=pl.BlockSpec((n_bins // 4, N), lambda i: (0, 0)),
        scratch_shapes=[pltpu.VMEM((4 * width, obs_rows), BF16), pltpu.VMEM((n_bins, 128), F32)],
        compiler_params=pltpu.CompilerParams(vmem_limit_bytes=24 * MIB),
    )(rid, observed)


def own_copy(z, flat, own, start, sem):
    return pltpu.make_async_copy(flat.at[pl.ds(pl.multiple_of(z * (SUB * 64) + start * 64, 64), own.shape[0])], own, sem)


def assemble(z, parts, ah, al, own=None):
    for d in (1, 2, 3, 0):
        slot = lax.rem(z - d + ROWS, ROWS)
        rows = pl.ds(pl.multiple_of(slot * 64, 64), 64)
        if d == 0:
            own.wait()
        for k in range(ah.shape[0]):
            hi, lo = split(parts[d][k * 64 : (k + 1) * 64, :])
            ah[k, rows, :] = hi
            al[k, rows, :] = lo


def by_step(x, ah, al):
    xh, xl = split(x)
    return dot_nt(xh, ah) + dot_nt(xl, ah) + dot_nt(xh, al)


def chains(lengths, ah, al, pref):
    eye = jnp.where(
        lax.broadcasted_iota(jnp.int32, (N, N), 0) == lax.broadcasted_iota(jnp.int32, (N, N), 1), 1.0, 0.0
    ).astype(BF16)
    for t in range(max(lengths)):
        for c, length in enumerate(lengths):
            if t >= length:
                continue
            k = sum(lengths[:c]) + t
            if t == 0:
                pref[k] = dot_nt(eye, ah[k]) + dot_nt(eye, al[k])
            else:
                pref[k] = by_step(pref[k - 1], ah[k], al[k])


def first_kernel(idx, flat, gains, a1, a2, a3, pref, ah, al, tail, staged, own, sems):
    z = idx[Z]
    late = pltpu.make_async_copy(gains, staged, sems.at[1])
    copy = own_copy(z, flat, own, 0, sems.at[0])
    copy.start()
    late.start()
    assemble(z, (own, a1, a2, a3), ah, al, copy)
    chains(CHUNKS[0], ah, al, pref)
    tail[0] = mm(pref[ENDS[1] - 1], pref[ENDS[2] - 1])
    tail[1] = mm(pref[ENDS[0] - 1], tail[0])
    late.wait()


def second_kernel(idx, flat, a1, a2, a3, tail, pref, ah, al, last, own, sem):
    z = idx[Z]
    copy = own_copy(z, flat, own, SIZES[0], sem)
    copy.start()
    assemble(z, (own, a1, a2, a3), ah, al, copy)
    total = tail[1]
    for k in range(SIZES[1]):
        total = by_step(total, ah[k], al[k])
    last[...] = total
    chains(CHUNKS[1], ah, al, pref)


def third_kernel(idx, b0, b1, b2, b3, p01, ah01, al01, tail, p23, ah23, al23, last, shifts, whole, b_s):
    z = idx[Z]
    for d, b in enumerate((b0, b1, b2, b3)):
        b_s[lax.rem(z - d + ROWS, ROWS)] = b[...]
    b = jnp.concatenate([b_s[i, :, :64] for i in range(ROWS)], axis=1)
    first = lax.broadcasted_iota(jnp.int32, (PAD, N), 0) == 0

    def row(k):
        return jnp.where(first, b[k : k + 1, :], 0.0)

    mats = [(ah01, al01, i) for i in range(SIZES[0])] + [(ah23, al23, i) for i in range(SIZES[1])]
    starts = [end - n for end, n in zip(ENDS, SEGS)]
    p = [row(k) for k in starts]
    for c, k in enumerate(starts):
        shifts[k : k + 1, :] = p[c][:1]
    for t in range(1, max(SEGS)):
        for c, start in enumerate(starts):
            if t >= SEGS[c]:
                continue
            k = start + t
            h, l, i = mats[k]
            p[c] = by_step(p[c], h[i], l[i]) + row(k)
            shifts[k : k + 1, :] = p[c][:1]
    v = mm(p[0], tail[0]) + mm(p[1], p01[SIZES[0] - 1]) + p[2]
    v = mm(v, p23[SIZES[1] - 1]) + p[3]
    whole[:N, :] = last[...]
    whole[N:, :] = v


def combine(pos, m_s, before):
    m01 = then(m_s[0], m_s[1])
    m23 = then(m_s[2], m_s[3])
    before[...] = eye_map()

    @pl.when(pos == 1)
    def _():
        before[...] = m_s[0]

    @pl.when(pos == 2)
    def _():
        before[...] = m01

    @pl.when(pos == 3)
    def _():
        before[...] = then(m01, m_s[2])

    return then(m01, m23)


def four_kernel(idx, m0, m1, m2, m3, total, before, m_s):
    pos = idx[Z]
    for d, m in enumerate((m0, m1, m2, m3)):
        m_s[lax.rem(pos - d + 4, 4)] = m[...]
    total[...] = combine(pos, m_s, before)


def half_rows(c):
    return pl.ds(pl.multiple_of(c * HALF, 8), HALF)


def join(pos, c, near_map, near_other, far_half, far_other, m_s):
    m_s[lax.rem(pos + 3 + 2 * c, 4)] = near_map[...]
    m_s[lax.rem(pos + 5 - 2 * c, 4)] = near_other[...]
    m_s[lax.rem(pos + 2, 4), half_rows(c), :] = far_half[...]
    m_s[lax.rem(pos + 2, 4), half_rows(1 - c), :] = far_other[...]


def plane_kernel(idx, own, n, no, f, fo, total, half, before, m_s):
    pos, c = idx[Y], idx[C]
    m_s[pos] = own[...]
    join(pos, c, n, no, f, fo, m_s)
    total[...] = combine(pos, m_s, before)
    half[...] = total[half_rows(c), :]


def pair_kernel(idx, own, other, before_in, total, half, before):
    c = idx[C]
    swap = c == 1

    @pl.when(swap)
    def _():
        total[...] = then(other[...], own[...])
        before[...] = then(other[...], before_in[...])

    @pl.when(jnp.logical_not(swap))
    def _():
        total[...] = then(own[...], other[...])
        before[...] = before_in[...]

    half[...] = total[half_rows(c), :]


def fold_kernel(idx, first, second, out):
    out[...] = then(first[...], second[...])


def states_kernel(
    idx, prior, n, no, f, fo, before, p01, p23, shifts, o0, o1, o2, o3, st_s, m_s, s_s
):
    z, pos = idx[Z], idx[X]
    join(pos, idx[C], n, no, f, fo, m_s)
    s_s[...] = jnp.where(lax.broadcasted_iota(jnp.int32, (PAD, N), 0) == 0, prior[...], 0.0)
    for i in range(3):

        @pl.when(i < pos)
        def _(i=i):
            s_s[...] = apply(s_s[...], m_s[i])

    s = apply(s_s[...], before[...])
    eye = lax.broadcasted_iota(jnp.int32, (N, N), 0) == lax.broadcasted_iota(jnp.int32, (N, N), 1)
    first = lax.broadcasted_iota(jnp.int32, (PAD, N), 0) == 0
    prefs = [(p01, i) for i in range(SIZES[0])] + [(p23, i) for i in range(SIZES[1])]
    for end, n in zip(ENDS, SEGS):
        col = jnp.sum(jnp.where(eye, s[0:1, :], 0.0), axis=1, keepdims=True)
        for k in range(end - n, end):
            m, i = prefs[k]
            row = jnp.sum(m[i] * col, axis=0, keepdims=True) + shifts[k : k + 1, :]
            for j in range(ROWS):
                st_s[j, k : k + 1, :] = row[:, j * 64 : (j + 1) * 64]
        if end < SUB:
            m, i = prefs[end - 1]
            s = mm(s, m[i]) + jnp.where(first, shifts[end - 1 : end, :], 0.0)
    for d, o in enumerate((o0, o1, o2, o3)):
        o[...] = st_s[lax.rem(z + d, ROWS)]


def send_copies(z, flat, outs, start, count, sems):
    copies = []
    for d, o in enumerate(outs, 1):
        at = lax.rem(z + d, ROWS) * (SUB * 64) + start * 64
        source = flat.at[pl.ds(pl.multiple_of(at, 64), count * 64)]
        copies.append(pltpu.make_async_copy(source, o.at[pl.ds(0, count * 64)], sems.at[d - 1]))
    for copy in copies:
        copy.start()
    return copies


def send_a_kernel(idx, flat, o1, o2, o3, sems):
    for copy in send_copies(idx[Z], flat, (o1, o2, o3), 0, SIZES[0], sems):
        copy.wait()


def sum_kernel(idx, sums, info):
    info[...] = jnp.sum(sums[...], axis=0)


def send_b_kernel(idx, flat, o1, o2, o3, sems):
    for copy in send_copies(idx[Z], flat, (o1, o2, o3), SIZES[0], SIZES[1], sems):
        copy.wait()


def offset_kernel(idx, g, i0, r1, r2, r3, o0, o1, o2, o3, info_s, off_s):
    z = idx[Z]
    info_s[z] = i0[...]
    for d, r in ((1, r1), (2, r2), (3, r3)):
        info_s[lax.rem(z - d + ROWS, ROWS)] = r[...]
    lane = lax.broadcasted_iota(jnp.int32, (64, 128), 1)
    for q in range(4):
        full = jnp.concatenate([info_s[i, :, q * 64 : (q + 1) * 64] for i in range(ROWS)], axis=1)
        acc = jnp.zeros((64, 128), F32)
        for k in range(16):
            col = jnp.sum(g[16 * q + k] * full[k : k + 1, :], axis=1, keepdims=True)
            acc = jnp.where(lane == k, col, acc)
        off_s[q] = jnp.concatenate([acc, jnp.zeros((64, 128), F32)], axis=0).T[:16, :]
    for d, o in enumerate((o0, o1, o2, o3)):
        o[:, :128] = off_s[lax.rem(z + d, ROWS)]
        o[:, 128:] = jnp.zeros((16, 128), F32)


def place_kernel(idx, r0, r1, r2, r3, out):
    z = idx[Z]
    for d, r in enumerate((r0, r1, r2, r3)):
        slot = lax.rem(z - d + ROWS, ROWS)
        out[pl.ds(pl.multiple_of(slot * SUB, SUB), SUB), :] = r[...]


def along_row(x, d):
    return lax.ppermute(x, "row", [(i, (i + d) % ROWS) for i in range(ROWS)])


def shards(prior, dynamics, gains, observed, owner, step):
    tm = lax.axis_index("tm").astype(jnp.int32)
    z = lax.axis_index("row").astype(jnp.int32)
    idx = jnp.stack([z, tm & 1, (tm >> 1) & 3, tm >> 3])
    prior = prior.reshape(1, N)
    flat = dynamics.reshape(ROWS * SUB * 64, N)
    dma3 = pltpu.SemaphoreType.DMA((3,))

    def along_rows(blocks):
        return [along_row(b, d) for d, b in enumerate(blocks, 1)]

    part_a = along_rows(call(send_a_kernel, [(SIZES[0] * 64, N)] * 3, idx, (), [dma3], far=(flat,)))

    rid = owner[:, 0] * 16 + step % 16 + 512 * (step // 16)
    partial = binned(rid.reshape(1, -1), observed.T)
    sums = lax.all_to_all(partial, "tm", 0, 0, tiled=True).reshape(32, 16, N)
    (info,) = call(sum_kernel, [(16, N)], idx, (sums,))
    infos = along_rows([info] * 3)
    sent_b = call(send_b_kernel, [(SIZES[1] * 64, N)] * 3, idx, (), [dma3], far=(flat,))
    infos, sent_b, part_a, idx, prior = lax.optimization_barrier((infos, sent_b, part_a, idx, prior))
    part_b = along_rows(sent_b)
    p01, ah01, al01, tail, staged = call(
        first_kernel,
        [(SIZES[0], N, N), ((SIZES[0], N, N), BF16), ((SIZES[0], N, N), BF16), (2, N, N), gains.shape],
        idx,
        part_a,
        [pltpu.VMEM((SIZES[0] * 64, N), F32), pltpu.SemaphoreType.DMA((2,))],
        far=(flat, gains),
    )
    offs = call(
        offset_kernel,
        [(16, N)] * 4,
        idx,
        (staged, info, *infos),
        [pltpu.VMEM((ROWS, 16, N), F32), pltpu.VMEM((ROWS, 16, 128), F32)],
    )
    offs = [offs[0], *along_rows(offs[1:])]
    p23, ah23, al23, last = call(
        second_kernel,
        [(SIZES[1], N, N), ((SIZES[1], N, N), BF16), ((SIZES[1], N, N), BF16), (N, N)],
        idx,
        (*part_b, tail),
        [pltpu.VMEM((SIZES[1] * 64, N), F32), pltpu.SemaphoreType.DMA],
        far=(flat,),
    )
    shifts, whole = call(
        third_kernel,
        [(SUB, N), (R, N)],
        idx,
        (*offs, p01, ah01, al01, tail, p23, ah23, al23, last),
        [pltpu.VMEM((ROWS, 16, N), F32)],
    )

    block, before = call(
        four_kernel,
        [(R, N), (R, N)],
        idx,
        (whole, *[along_row(whole, d) for d in (1, 2, 3)]),
        [pltpu.VMEM((4, R, N), F32)],
    )

    def other_core(m):
        return lax.ppermute(m, "tm", [(i, i ^ 1) for i in range(32)])

    def along_tm(m, stride, moves):
        n = 4 * stride
        return lax.ppermute(m, "tm", [(i, i - i % n + (i + moves[i % 2] * stride) % n) for i in range(32)])

    def gathered(m, half, stride):
        far, near_map = along_tm(half, stride, (2, 2)), along_tm(m, stride, (1, 3))
        return near_map, other_core(near_map), far, other_core(far)

    column, half, before = call(
        pair_kernel, [(R, N), (HALF, N), (R, N)], idx, (block, other_core(block), before)
    )
    plane, half, ybefore = call(
        plane_kernel,
        [(R, N), (HALF, N), (R, N)],
        idx,
        (column, *gathered(column, half, 2)),
        [pltpu.VMEM((4, R, N), F32)],
    )
    (before,) = call(fold_kernel, [(R, N)], idx, (ybefore, before))
    outs = call(
        states_kernel,
        [(SUB, 64)] * 4,
        idx,
        (prior, *gathered(plane, half, 8), before, p01, p23, shifts),
        [pltpu.VMEM((ROWS, SUB, 64), F32), pltpu.VMEM((4, R, N), F32), pltpu.VMEM((PAD, N), F32)],
    )
    got = [outs[0], *along_rows(outs[1:])]
    return pl.pallas_call(
        place_kernel,
        out_shape=jax.ShapeDtypeStruct((64, 64), F32),
        in_specs=[SM] + [VM] * 4,
        out_specs=VM,
        compiler_params=pltpu.CompilerParams(vmem_limit_bytes=4 * MIB),
    )(idx, *[near(g) for g in got])


def solution(mesh):
    return jax.shard_map(
        shards,
        mesh=mesh,
        in_specs=(
            P(),
            P("tm", "row", None),
            P("tm", "row", None),
            P("tm", "row"),
            P("tm", None),
            P("tm"),
        ),
        out_specs=P("tm", "row"),
        check_vma=False,
    )
```

```python
import jax
import jax.numpy as jnp
from jax import lax
from jax.experimental import pallas as pl
from jax.experimental.pallas import tpu as pltpu
from jax.sharding import PartitionSpec as P

F32 = jnp.float32
BF16 = jnp.bfloat16
MIB = 1024 * 1024
VM = pl.BlockSpec(memory_space=pltpu.VMEM)
SM = pl.BlockSpec(memory_space=pltpu.SMEM)
N = 256
PAD = 16
R = N + PAD
Z, C, Y, X = range(4)
HALF = R // 2
ROWS = 4
SUB = 16
CHUNKS = ((5, 5), (3, 3))
SEGS = tuple(n for chunk in CHUNKS for n in chunk)
SIZES = tuple(sum(chunk) for chunk in CHUNKS)
ENDS = tuple(sum(SEGS[: i + 1]) for i in range(len(SEGS)))


def split(x):
    hi = x.astype(BF16)
    return hi, (x - hi.astype(F32)).astype(BF16)


def dot_nn(a, b):
    return lax.dot_general(a, b, (((1,), (0,)), ((), ())), preferred_element_type=F32)


def dot_nt(a, b):
    return lax.dot_general(a, b, (((1,), (1,)), ((), ())), preferred_element_type=F32)


def mm(a, b, dot=dot_nn):
    ah, al = split(a)
    bh, bl = split(b)
    return dot(ah, bh) + dot(al, bh) + dot(ah, bl)


def then(first, second):
    out = mm(first, second[:N])
    return jnp.concatenate([out[:N], out[N:] + second[N:]], axis=0)


def apply(s, m):
    return mm(s, m[:N]) + m[N:]


def eye_map():
    r = lax.broadcasted_iota(jnp.int32, (R, N), 0)
    c = lax.broadcasted_iota(jnp.int32, (R, N), 1)
    return jnp.where(r == c, 1.0, 0.0).astype(F32)


FAR = pl.BlockSpec(memory_space=pltpu.HBM)


def near(x):
    return pltpu.with_memory_space_constraint(x, pltpu.VMEM)


def call(kernel, outs, idx, args, scratch=(), far=(), mib=8):
    outs = [o if isinstance(o[0], tuple) else (o, F32) for o in outs]
    return pl.pallas_call(
        kernel,
        out_shape=[pltpu.VMEM(s, t) for s, t in outs],
        in_specs=[SM] + [FAR] * len(far) + [VM] * len(args),
        out_specs=[VM] * len(outs),
        scratch_shapes=list(scratch),
        compiler_params=pltpu.CompilerParams(vmem_limit_bytes=mib * MIB),
    )(idx, *[pltpu.with_memory_space_constraint(f, pltpu.HBM) for f in far], *[near(a) for a in args])


BIN_M = 256


def bin_kernel(rid_ref, obs_ref, out_ref, rhs, acc):
    i = pl.program_id(0)
    n_m = pl.num_programs(0)

    @pl.when(i == 0)
    def _():
        x = obs_ref[...]
        hi = x.astype(BF16)
        rest = x - hi.astype(F32)
        mid = rest.astype(BF16)
        low = (rest - mid.astype(F32)).astype(BF16)
        rhs[...] = jnp.concatenate([hi, mid, low, jnp.zeros_like(hi)], axis=0)

    rows = lax.broadcasted_iota(jnp.int32, (BIN_M, rid_ref.shape[1]), 0) + i * BIN_M
    onehot = jnp.where(rows == rid_ref[...], 1.0, 0.0).astype(BF16)
    got = dot_nt(onehot, rhs[...])
    a = got[:, :128] + got[:, 128:]
    acc[pl.ds(pl.multiple_of(i * BIN_M, BIN_M), BIN_M), :] = a + pltpu.roll(a, 64, 1)

    @pl.when(i == n_m - 1)
    def _():
        part = out_ref.shape[0]
        low_half = lax.broadcasted_iota(jnp.int32, (part, 128), 1) < 64
        for h in range(2):
            even = acc[2 * h * part : (2 * h + 1) * part, :]
            odd = acc[(2 * h + 1) * part : (2 * h + 2) * part, :]
            out_ref[:, h * 128 : (h + 1) * 128] = jnp.where(low_half, even, odd)


def binned(rid, observed):
    n_bins = 2048
    width, obs_rows = observed.shape
    return pl.pallas_call(
        bin_kernel,
        out_shape=jax.ShapeDtypeStruct((n_bins // 4, N), F32),
        grid=(n_bins // BIN_M,),
        in_specs=[
            pl.BlockSpec((1, obs_rows), lambda i: (0, 0)),
            pl.BlockSpec((width, obs_rows), lambda i: (0, 0)),
        ],
        out_specs=pl.BlockSpec((n_bins // 4, N), lambda i: (0, 0)),
        scratch_shapes=[pltpu.VMEM((4 * width, obs_rows), BF16), pltpu.VMEM((n_bins, 128), F32)],
        compiler_params=pltpu.CompilerParams(vmem_limit_bytes=24 * MIB),
    )(rid, observed)


def own_copy(z, flat, own, start, sem):
    return pltpu.make_async_copy(flat.at[pl.ds(pl.multiple_of(z * (SUB * 64) + start * 64, 64), own.shape[0])], own, sem)


def assemble(z, first, prev, after, opposite, own, copy, ah, al):
    n = ah.shape[0]
    for d in (1, 3, 2, 0):
        slot = lax.rem(z - d + ROWS, ROWS)
        rows = pl.ds(pl.multiple_of(slot * 64, 64), 64)
        if d == 0:
            copy.wait()
        for k in range(n):
            ref, at = {
                0: (own, k),
                1: (prev, first + k),
                2: (opposite[2 * k // n], k % (n // 2)),
                3: (after, first + k),
            }[d]
            hi, lo = split(ref[at * 64 : (at + 1) * 64, :])
            ah[k, rows, :] = hi
            al[k, rows, :] = lo


def by_step(x, ah, al):
    xh, xl = split(x)
    return dot_nt(xh, ah) + dot_nt(xl, ah) + dot_nt(xh, al)


def chains(lengths, ah, al, pref):
    eye = jnp.where(
        lax.broadcasted_iota(jnp.int32, (N, N), 0) == lax.broadcasted_iota(jnp.int32, (N, N), 1), 1.0, 0.0
    ).astype(BF16)
    for t in range(max(lengths)):
        for c, length in enumerate(lengths):
            if t >= length:
                continue
            k = sum(lengths[:c]) + t
            if t == 0:
                pref[k] = dot_nt(eye, ah[k]) + dot_nt(eye, al[k])
            else:
                pref[k] = by_step(pref[k - 1], ah[k], al[k])


def first_kernel(idx, flat, prev, after, q1, q2, pref, ah, al, tail, own, sem):
    z = idx[Z]
    copy = own_copy(z, flat, own, 0, sem)
    copy.start()
    assemble(z, 0, prev, after, (q1, q2), own, copy, ah, al)
    chains(CHUNKS[0], ah, al, pref)
    tail[...] = mm(pref[ENDS[0] - 1], pref[ENDS[1] - 1])


def second_kernel(idx, flat, prev, after, q1, q2, tail, pref, ah, al, last, own, sem):
    z = idx[Z]
    copy = own_copy(z, flat, own, SIZES[0], sem)
    copy.start()
    assemble(z, SIZES[0], prev, after, (q1, q2), own, copy, ah, al)
    chains(CHUNKS[1], ah, al, pref)
    last[0] = mm(pref[CHUNKS[1][0] - 1], pref[SIZES[1] - 1])
    last[1] = mm(tail[...], last[0])


def third_kernel(idx, b0, b1, b2, b3, p01, ah01, al01, p23, ah23, al23, last, shifts, whole, b_s):
    z = idx[Z]
    for d, b in enumerate((b0, b1, b2, b3)):
        b_s[lax.rem(z - d + ROWS, ROWS)] = b[...]
    b = jnp.concatenate([b_s[i, :, :64] for i in range(ROWS)], axis=1)
    first = lax.broadcasted_iota(jnp.int32, (PAD, N), 0) == 0

    def row(k):
        return jnp.where(first, b[k : k + 1, :], 0.0)

    mats = [(ah01, al01, i) for i in range(SIZES[0])] + [(ah23, al23, i) for i in range(SIZES[1])]
    starts = [end - n for end, n in zip(ENDS, SEGS)]
    p = [row(k) for k in starts]
    for c, k in enumerate(starts):
        shifts[k : k + 1, :] = p[c][:1]
    for t in range(1, max(SEGS)):
        for c, start in enumerate(starts):
            if t >= SEGS[c]:
                continue
            k = start + t
            h, l, i = mats[k]
            p[c] = by_step(p[c], h[i], l[i]) + row(k)
            shifts[k : k + 1, :] = p[c][:1]
    v = mm(p[0], p01[SIZES[0] - 1]) + p[1]
    v = mm(v, last[0]) + (mm(p[2], p23[SIZES[1] - 1]) + p[3])
    whole[:N, :] = last[1]
    whole[N:, :] = v


def combine(pos, m_s, before):
    m01 = then(m_s[0], m_s[1])
    m23 = then(m_s[2], m_s[3])
    before[...] = eye_map()

    @pl.when(pos == 1)
    def _():
        before[...] = m_s[0]

    @pl.when(pos == 2)
    def _():
        before[...] = m01

    @pl.when(pos == 3)
    def _():
        before[...] = then(m01, m_s[2])

    return then(m01, m23)


def four_kernel(idx, m0, m1, m2, m3, total, before, m_s):
    pos = idx[Z]
    for d, m in enumerate((m0, m1, m2, m3)):
        m_s[lax.rem(pos - d + 4, 4)] = m[...]
    total[...] = combine(pos, m_s, before)


def half_rows(c):
    return pl.ds(pl.multiple_of(c * HALF, 8), HALF)


def join(pos, c, mine, rest, far, o_mine, o_rest, o_far, m_s):
    mine_at, other_at = half_rows(c), half_rows(1 - c)
    near_slot, other_slot, far_slot = lax.rem(pos + 3 + 2 * c, 4), lax.rem(pos + 5 - 2 * c, 4), lax.rem(pos + 2, 4)
    m_s[near_slot, mine_at, :] = mine[...]
    m_s[near_slot, other_at, :] = rest[...]
    m_s[other_slot, other_at, :] = o_mine[...]
    m_s[other_slot, mine_at, :] = o_rest[...]
    m_s[far_slot, mine_at, :] = far[...]
    m_s[far_slot, other_at, :] = o_far[...]


def halve(c, whole, mine, rest):
    mine[...] = whole[half_rows(c), :]
    rest[...] = whole[half_rows(1 - c), :]


def plane_kernel(idx, own, n0, n1, n2, o0, o1, o2, mine, rest, before, m_s, all_s):
    pos, c = idx[Y], idx[C]
    m_s[pos] = own[...]
    join(pos, c, n0, n1, n2, o0, o1, o2, m_s)
    all_s[...] = combine(pos, m_s, before)
    halve(c, all_s, mine, rest)


def pair_kernel(idx, own, other, before_in, total, mine, rest, before):
    c = idx[C]
    swap = c == 1

    @pl.when(swap)
    def _():
        total[...] = then(other[...], own[...])
        before[...] = then(other[...], before_in[...])

    @pl.when(jnp.logical_not(swap))
    def _():
        total[...] = then(own[...], other[...])
        before[...] = before_in[...]

    halve(c, total, mine, rest)


def fold_kernel(idx, first, second, out):
    out[...] = then(first[...], second[...])


def states_kernel(
    idx, prior, n0, n1, n2, g0, g1, g2, before, p01, p23, shifts, o0, o1, o2, o3, st_s, m_s, s_s
):
    z, pos = idx[Z], idx[X]
    join(pos, idx[C], n0, n1, n2, g0, g1, g2, m_s)
    s_s[...] = jnp.where(lax.broadcasted_iota(jnp.int32, (PAD, N), 0) == 0, prior[...], 0.0)
    for i in range(3):

        @pl.when(i < pos)
        def _(i=i):
            s_s[...] = apply(s_s[...], m_s[i])

    s = apply(s_s[...], before[...])
    eye = lax.broadcasted_iota(jnp.int32, (N, N), 0) == lax.broadcasted_iota(jnp.int32, (N, N), 1)
    first = lax.broadcasted_iota(jnp.int32, (PAD, N), 0) == 0
    prefs = [(p01, i) for i in range(SIZES[0])] + [(p23, i) for i in range(SIZES[1])]
    for end, n in zip(ENDS, SEGS):
        col = jnp.sum(jnp.where(eye, s[0:1, :], 0.0), axis=1, keepdims=True)
        for k in range(end - n, end):
            m, i = prefs[k]
            row = jnp.sum(m[i] * col, axis=0, keepdims=True) + shifts[k : k + 1, :]
            for j in range(ROWS):
                st_s[j, k : k + 1, :] = row[:, j * 64 : (j + 1) * 64]
        if end < SUB:
            m, i = prefs[end - 1]
            s = mm(s, m[i]) + jnp.where(first, shifts[end - 1 : end, :], 0.0)
    for d, o in enumerate((o0, o1, o2, o3)):
        o[...] = st_s[lax.rem(z + d, ROWS)]


RELAYED = tuple(
    [(sum(SIZES[:i]) + w * n // 2, n // 2) for i, n in enumerate(SIZES)] for w in range(2)
)
SENT = SUB + SUB // 2


def send_kernel(idx, flat, ahead, back, sems):
    z = idx[Z]
    copies = []
    for way, out in enumerate((ahead, back)):
        at = 0
        for d, first, count in [((1, 3)[way], 0, SUB)] + [(2, *r) for r in RELAYED[way]]:
            source = lax.rem(z + d, ROWS) * (SUB * 64) + first * 64
            copies.append(
                pltpu.make_async_copy(
                    flat.at[pl.ds(pl.multiple_of(source, 64), count * 64)],
                    out.at[pl.ds(at * 64, count * 64)],
                    sems.at[len(copies)],
                )
            )
            at += count
    for copy in copies:
        copy.start()
    for copy in copies:
        copy.wait()


def relay_kernel(idx, prev, after, p1, a1, p2, a2):
    cut = SUB + RELAYED[0][0][1]
    p1[...] = prev[SUB * 64 : cut * 64, :]
    a1[...] = after[SUB * 64 : cut * 64, :]
    p2[...] = prev[cut * 64 :, :]
    a2[...] = after[cut * 64 :, :]


def stage_kernel(idx, gains, info, staged, sem):
    copy = pltpu.make_async_copy(gains, staged, sem)
    copy.start()
    copy.wait()


def sum_kernel(idx, sums, info):
    info[...] = jnp.sum(sums[...], axis=0)


def offset_kernel(idx, g, i0, r1, r2, r3, o0, o1, o2, o3, info_s, off_s):
    z = idx[Z]
    info_s[z] = i0[...]
    for d, r in ((1, r1), (2, r2), (3, r3)):
        info_s[lax.rem(z - d + ROWS, ROWS)] = r[...]
    lane = lax.broadcasted_iota(jnp.int32, (64, 128), 1)
    for q in range(4):
        full = jnp.concatenate([info_s[i, :, q * 64 : (q + 1) * 64] for i in range(ROWS)], axis=1)
        acc = jnp.zeros((64, 128), F32)
        for k in range(16):
            col = jnp.sum(g[16 * q + k] * full[k : k + 1, :], axis=1, keepdims=True)
            acc = jnp.where(lane == k, col, acc)
        off_s[q] = jnp.concatenate([acc, jnp.zeros((64, 128), F32)], axis=0).T[:16, :]
    for d, o in enumerate((o0, o1, o2, o3)):
        o[:, :128] = off_s[lax.rem(z + d, ROWS)]
        o[:, 128:] = jnp.zeros((16, 128), F32)


def place_kernel(idx, r0, r1, r2, r3, out):
    z = idx[Z]
    for d, r in enumerate((r0, r1, r2, r3)):
        slot = lax.rem(z - d + ROWS, ROWS)
        out[pl.ds(pl.multiple_of(slot * SUB, SUB), SUB), :] = r[...]


def along_row(x, d):
    return lax.ppermute(x, "row", [(i, (i + d) % ROWS) for i in range(ROWS)])


def shards(prior, dynamics, gains, observed, owner, step):
    tm = lax.axis_index("tm").astype(jnp.int32)
    z = lax.axis_index("row").astype(jnp.int32)
    idx = jnp.stack([z, tm & 1, (tm >> 1) & 3, tm >> 3])
    prior = prior.reshape(1, N)
    flat = dynamics.reshape(ROWS * SUB * 64, N)

    def along_rows(blocks):
        return [along_row(b, d) for d, b in enumerate(blocks, 1)]

    ahead, back = call(
        send_kernel, [(SENT * 64, N)] * 2, idx, (), [pltpu.SemaphoreType.DMA((6,))], far=(flat,)
    )
    prev, after = along_row(ahead, 1), along_row(back, 3)

    rid = owner[:, 0] * 16 + step % 16 + 512 * (step // 16)
    partial = binned(rid.reshape(1, -1), observed.T)
    sums = lax.all_to_all(partial, "tm", 0, 0, tiled=True).reshape(32, 16, N)
    (info,) = call(sum_kernel, [(16, N)], idx, (sums,))
    infos = along_rows([info] * 3)
    (staged,) = call(stage_kernel, [gains.shape], idx, (info,), [pltpu.SemaphoreType.DMA], far=(gains,))
    infos, staged, prev, after, idx, prior = lax.optimization_barrier((infos, staged, prev, after, idx, prior))
    pieces = call(relay_kernel, [(n * 64, N) for n in (5, 5, 3, 3)], idx, (prev, after))
    pieces, infos = lax.optimization_barrier((pieces, infos))
    relayed = [along_row(p, d) for p, d in zip(pieces, (1, 3, 1, 3))]
    p01, ah01, al01, tail = call(
        first_kernel,
        [(SIZES[0], N, N), ((SIZES[0], N, N), BF16), ((SIZES[0], N, N), BF16), (N, N)],
        idx,
        (prev, after, *relayed[:2]),
        [pltpu.VMEM((SIZES[0] * 64, N), F32), pltpu.SemaphoreType.DMA],
        far=(flat,),
    )
    offs = call(
        offset_kernel,
        [(16, N)] * 4,
        idx,
        (staged, info, *infos),
        [pltpu.VMEM((ROWS, 16, N), F32), pltpu.VMEM((ROWS, 16, 128), F32)],
    )
    offs = [offs[0], *along_rows(offs[1:])]
    p23, ah23, al23, last = call(
        second_kernel,
        [(SIZES[1], N, N), ((SIZES[1], N, N), BF16), ((SIZES[1], N, N), BF16), (2, N, N)],
        idx,
        (prev, after, *relayed[2:], tail),
        [pltpu.VMEM((SIZES[1] * 64, N), F32), pltpu.SemaphoreType.DMA],
        far=(flat,),
    )
    shifts, whole = call(
        third_kernel,
        [(SUB, N), (R, N)],
        idx,
        (*offs, p01, ah01, al01, p23, ah23, al23, last),
        [pltpu.VMEM((ROWS, 16, N), F32)],
    )

    block, before = call(
        four_kernel,
        [(R, N), (R, N)],
        idx,
        (whole, *[along_row(whole, d) for d in (1, 2, 3)]),
        [pltpu.VMEM((4, R, N), F32)],
    )

    def other_core(m):
        return lax.ppermute(m, "tm", [(i, i ^ 1) for i in range(32)])

    def along_tm(m, stride, moves):
        n = 4 * stride
        return lax.ppermute(m, "tm", [(i, i - i % n + (i + moves[i % 2] * stride) % n) for i in range(32)])

    def gathered(mine, rest, stride):
        near_mine = along_tm(mine, stride, (1, 3))
        got = near_mine, along_tm(rest, stride, (1, 3)), along_tm(near_mine, stride, (1, 3))
        return *got, *[other_core(g) for g in got]

    column, *halves, before = call(
        pair_kernel, [(R, N), (HALF, N), (HALF, N), (R, N)], idx, (block, other_core(block), before)
    )
    *halves, ybefore = call(
        plane_kernel,
        [(HALF, N), (HALF, N), (R, N)],
        idx,
        (column, *gathered(*halves, 2)),
        [pltpu.VMEM((4, R, N), F32), pltpu.VMEM((R, N), F32)],
    )
    (before,) = call(fold_kernel, [(R, N)], idx, (ybefore, before))
    outs = call(
        states_kernel,
        [(SUB, 64)] * 4,
        idx,
        (prior, *gathered(*halves, 8), before, p01, p23, shifts),
        [pltpu.VMEM((ROWS, SUB, 64), F32), pltpu.VMEM((4, R, N), F32), pltpu.VMEM((PAD, N), F32)],
    )
    got = [outs[0], *along_rows(outs[1:])]
    return pl.pallas_call(
        place_kernel,
        out_shape=jax.ShapeDtypeStruct((64, 64), F32),
        in_specs=[SM] + [VM] * 4,
        out_specs=VM,
        compiler_params=pltpu.CompilerParams(vmem_limit_bytes=4 * MIB),
    )(idx, *[near(g) for g in got])


def solution(mesh):
    return jax.shard_map(
        shards,
        mesh=mesh,
        in_specs=(
            P(),
            P("tm", "row", None),
            P("tm", "row", None),
            P("tm", "row"),
            P("tm", None),
            P("tm"),
        ),
        out_specs=P("tm", "row"),
        check_vma=False,
    )
```

```python
import jax
import jax.numpy as jnp
from jax import lax
from jax.experimental import pallas as pl
from jax.experimental.pallas import tpu as pltpu
from jax.sharding import PartitionSpec as P

F32 = jnp.float32
BF16 = jnp.bfloat16
MIB = 1024 * 1024
VM = pl.BlockSpec(memory_space=pltpu.VMEM)
SM = pl.BlockSpec(memory_space=pltpu.SMEM)
N = 256
PAD = 16
R = N + PAD
Z, C, Y, X = range(4)
HALF = R // 2
ROWS = 4
SUB = 16
SEG = 4
HALF_SUB = SUB // 2
Z, C, Y, X = range(4)
HALF = R // 2
ROWS = 4
SUB = 16
CHUNKS = ((5, 5), (3, 3))
SEGS = tuple(n for chunk in CHUNKS for n in chunk)
SIZES = tuple(sum(chunk) for chunk in CHUNKS)
ENDS = tuple(sum(SEGS[: i + 1]) for i in range(len(SEGS)))


def split(x):
    hi = x.astype(BF16)
    return hi, (x - hi.astype(F32)).astype(BF16)


def dot_nn(a, b):
    return lax.dot_general(a, b, (((1,), (0,)), ((), ())), preferred_element_type=F32)


def dot_nt(a, b):
    return lax.dot_general(a, b, (((1,), (1,)), ((), ())), preferred_element_type=F32)


def mm(a, b, dot=dot_nn):
    ah, al = split(a)
    bh, bl = split(b)
    return dot(ah, bh) + dot(al, bh) + dot(ah, bl)


def then(first, second):
    out = mm(first, second[:N])
    return jnp.concatenate([out[:N], out[N:] + second[N:]], axis=0)


def apply(s, m):
    return mm(s, m[:N]) + m[N:]


def eye_map():
    r = lax.broadcasted_iota(jnp.int32, (R, N), 0)
    c = lax.broadcasted_iota(jnp.int32, (R, N), 1)
    return jnp.where(r == c, 1.0, 0.0).astype(F32)


FAR = pl.BlockSpec(memory_space=pltpu.HBM)


def near(x):
    return pltpu.with_memory_space_constraint(x, pltpu.VMEM)


def call(kernel, outs, idx, args, scratch=(), far=(), mib=8):
    outs = [o if isinstance(o[0], tuple) else (o, F32) for o in outs]
    return pl.pallas_call(
        kernel,
        out_shape=[pltpu.VMEM(s, t) for s, t in outs],
        in_specs=[SM] + [FAR] * len(far) + [VM] * len(args),
        out_specs=[VM] * len(outs),
        scratch_shapes=list(scratch),
        compiler_params=pltpu.CompilerParams(vmem_limit_bytes=mib * MIB),
    )(idx, *[pltpu.with_memory_space_constraint(f, pltpu.HBM) for f in far], *[near(a) for a in args])


BIN_M = 256


def bin_kernel(rid_ref, obs_ref, out_ref, rhs, acc):
    i = pl.program_id(0)
    n_m = pl.num_programs(0)

    @pl.when(i == 0)
    def _():
        x = obs_ref[...]
        hi = x.astype(BF16)
        rest = x - hi.astype(F32)
        mid = rest.astype(BF16)
        low = (rest - mid.astype(F32)).astype(BF16)
        rhs[...] = jnp.concatenate([hi, mid, low, jnp.zeros_like(hi)], axis=0)

    rows = lax.broadcasted_iota(jnp.int32, (BIN_M, rid_ref.shape[1]), 0) + i * BIN_M
    onehot = jnp.where(rows == rid_ref[...], 1.0, 0.0).astype(BF16)
    got = dot_nt(onehot, rhs[...])
    a = got[:, :128] + got[:, 128:]
    acc[pl.ds(pl.multiple_of(i * BIN_M, BIN_M), BIN_M), :] = a + pltpu.roll(a, 64, 1)

    @pl.when(i == n_m - 1)
    def _():
        part = out_ref.shape[0]
        low_half = lax.broadcasted_iota(jnp.int32, (part, 128), 1) < 64
        for h in range(2):
            even = acc[2 * h * part : (2 * h + 1) * part, :]
            odd = acc[(2 * h + 1) * part : (2 * h + 2) * part, :]
            out_ref[:, h * 128 : (h + 1) * 128] = jnp.where(low_half, even, odd)


def binned(rid, observed):
    n_bins = 2048
    width, obs_rows = observed.shape
    return pl.pallas_call(
        bin_kernel,
        out_shape=jax.ShapeDtypeStruct((n_bins // 4, N), F32),
        grid=(n_bins // BIN_M,),
        in_specs=[
            pl.BlockSpec((1, obs_rows), lambda i: (0, 0)),
            pl.BlockSpec((width, obs_rows), lambda i: (0, 0)),
        ],
        out_specs=pl.BlockSpec((n_bins // 4, N), lambda i: (0, 0)),
        scratch_shapes=[pltpu.VMEM((4 * width, obs_rows), BF16), pltpu.VMEM((n_bins, 128), F32)],
        compiler_params=pltpu.CompilerParams(vmem_limit_bytes=24 * MIB),
    )(rid, observed)


def assemble(z, own, prev, after, opposite, ah, al):
    for d in range(ROWS):
        slot = lax.rem(z - d + ROWS, ROWS)
        rows = pl.ds(pl.multiple_of(slot * 64, 64), 64)
        for k in range(SUB):
            ref, at = ((own, k), (prev, k), (opposite[k // HALF_SUB], k % HALF_SUB), (after, k))[d]
            hi, lo = split(ref[at * 64 : (at + 1) * 64, :])
            ah[k, rows, :] = hi
            al[k, rows, :] = lo


def compose_kernel(idx, own, prev, after, q1, q2, b0, b1, b2, b3, pref, whole, ah, al, b_s):
    z = idx[Z]
    assemble(z, own, prev, after, (q1, q2), ah, al)
    for d, b in enumerate((b0, b1, b2, b3)):
        b_s[lax.rem(z - d + ROWS, ROWS)] = b[...]
    b = jnp.concatenate([b_s[i, :, :64] for i in range(ROWS)], axis=1)
    first = lax.broadcasted_iota(jnp.int32, (PAD, N), 0) == 0
    eye = lax.broadcasted_iota(jnp.int32, (N, N), 0) == lax.broadcasted_iota(jnp.int32, (N, N), 1)
    eye = jnp.where(eye, 1.0, 0.0).astype(BF16)
    chains = range(SUB // SEG)
    for t in range(SEG):
        for c in chains:
            k = c * SEG + t
            shift = jnp.where(first, b[k : k + 1, :], 0.0)
            if t == 0:
                pref[k, :N, :] = dot_nt(eye, ah[k]) + dot_nt(eye, al[k])
                pref[k, N:, :] = shift
            else:
                hi, lo = split(pref[k - 1])
                out = dot_nt(hi, ah[k]) + dot_nt(lo, ah[k]) + dot_nt(hi, al[k])
                pref[k, :N, :] = out[:N]
                pref[k, N:, :] = out[N:] + shift
    ends = [pref[c * SEG + SEG - 1] for c in chains]
    whole[...] = then(then(ends[0], ends[1]), then(ends[2], ends[3]))


def combine(pos, m_s, before):
    m01 = then(m_s[0], m_s[1])
    m23 = then(m_s[2], m_s[3])
    before[...] = eye_map()

    @pl.when(pos == 1)
    def _():
        before[...] = m_s[0]

    @pl.when(pos == 2)
    def _():
        before[...] = m01

    @pl.when(pos == 3)
    def _():
        before[...] = then(m01, m_s[2])

    return then(m01, m23)


def four_kernel(idx, m0, m1, m2, m3, total, before, m_s):
    pos = idx[Z]
    for d, m in enumerate((m0, m1, m2, m3)):
        m_s[lax.rem(pos - d + 4, 4)] = m[...]
    total[...] = combine(pos, m_s, before)


def half_rows(c):
    return pl.ds(pl.multiple_of(c * HALF, 8), HALF)


def join(pos, c, mine, others, m_s):
    for d, (m, o) in enumerate(zip(mine, others), 1):
        slot = lax.rem(pos - d + 4, 4)
        m_s[slot, half_rows(c), :] = m[...]
        m_s[slot, half_rows(1 - c), :] = o[...]


def plane_kernel(idx, own, h1, h2, h3, o1, o2, o3, half, before, m_s, all_s):
    pos, c = idx[Y], idx[C]
    m_s[pos] = own[...]
    join(pos, c, (h1, h2, h3), (o1, o2, o3), m_s)
    all_s[...] = combine(pos, m_s, before)
    half[...] = all_s[half_rows(c), :]


def pair_kernel(idx, own, other, before_in, total, half, before):
    c = idx[C]
    swap = c == 1

    @pl.when(swap)
    def _():
        total[...] = then(other[...], own[...])
        before[...] = then(other[...], before_in[...])

    @pl.when(jnp.logical_not(swap))
    def _():
        total[...] = then(own[...], other[...])
        before[...] = before_in[...]

    half[...] = total[half_rows(c), :]


def fold_kernel(idx, first, second, out):
    out[...] = then(first[...], second[...])


def states_kernel(idx, prior, h1, h2, h3, g1, g2, g3, before, pref, o0, o1, o2, o3, st_s, m_s, s_s):
    z, pos = idx[Z], idx[X]
    join(pos, idx[C], (h1, h2, h3), (g1, g2, g3), m_s)
    s_s[...] = jnp.where(lax.broadcasted_iota(jnp.int32, (PAD, N), 0) == 0, prior[...], 0.0)
    for i in range(3):

        @pl.when(i < pos)
        def _(i=i):
            s_s[...] = apply(s_s[...], m_s[i])

    s = apply(s_s[...], before[...])
    eye = lax.broadcasted_iota(jnp.int32, (N, N), 0) == lax.broadcasted_iota(jnp.int32, (N, N), 1)
    for end in range(SEG, SUB + 1, SEG):
        col = jnp.sum(jnp.where(eye, s[0:1, :], 0.0), axis=1, keepdims=True)
        for k in range(end - SEG, end):
            row = jnp.sum(pref[k, :N, :] * col, axis=0, keepdims=True) + pref[k, N : N + 1, :]
            for j in range(ROWS):
                st_s[j, k : k + 1, :] = row[:, j * 64 : (j + 1) * 64]
        if end < SUB:
            s = apply(s, pref[end - 1])
    for d, o in enumerate((o0, o1, o2, o3)):
        o[...] = st_s[lax.rem(z + d, ROWS)]


SENT = SUB + HALF_SUB
COPIED = 4


def send_kernel(idx, flat, ahead, back, sems):
    z = idx[Z]
    copies = []
    for way, out in enumerate((ahead, back)):
        for at in range(0, SENT, COPIED):
            d, first = ((1, 3)[way], at) if at < SUB else (2, at - SUB + way * HALF_SUB)
            source = lax.rem(z + d, ROWS) * (SUB * 64) + first * 64
            copies.append(
                pltpu.make_async_copy(
                    flat.at[pl.ds(pl.multiple_of(source, 64), COPIED * 64)],
                    out.at[pl.ds(at * 64, COPIED * 64)],
                    sems.at[len(copies)],
                )
            )
    for copy in copies:
        copy.start()
    for copy in copies:
        copy.wait()


def relay_kernel(idx, prev, after, p, a):
    p[...] = prev[SUB * 64 :, :]
    a[...] = after[SUB * 64 :, :]


def stage_kernel(idx, gains, flat, info, staged, own, sems):
    copies = [
        pltpu.make_async_copy(gains, staged, sems.at[0]),
        pltpu.make_async_copy(flat.at[pl.ds(pl.multiple_of(idx[Z] * (SUB * 64), 64), SUB * 64)], own, sems.at[1]),
    ]
    for copy in copies:
        copy.start()
    for copy in copies:
        copy.wait()


def sum_kernel(idx, sums, info):
    info[...] = jnp.sum(sums[...], axis=0)


def offset_kernel(idx, g, i0, r1, r2, r3, o0, o1, o2, o3, info_s, off_s):
    z = idx[Z]
    info_s[z] = i0[...]
    for d, r in ((1, r1), (2, r2), (3, r3)):
        info_s[lax.rem(z - d + ROWS, ROWS)] = r[...]
    lane = lax.broadcasted_iota(jnp.int32, (64, 128), 1)
    for q in range(4):
        full = jnp.concatenate([info_s[i, :, q * 64 : (q + 1) * 64] for i in range(ROWS)], axis=1)
        acc = jnp.zeros((64, 128), F32)
        for k in range(16):
            col = jnp.sum(g[16 * q + k] * full[k : k + 1, :], axis=1, keepdims=True)
            acc = jnp.where(lane == k, col, acc)
        off_s[q] = jnp.concatenate([acc, jnp.zeros((64, 128), F32)], axis=0).T[:16, :]
    for d, o in enumerate((o0, o1, o2, o3)):
        o[:, :128] = off_s[lax.rem(z + d, ROWS)]
        o[:, 128:] = jnp.zeros((16, 128), F32)


def place_kernel(idx, r0, r1, r2, r3, out):
    z = idx[Z]
    for d, r in enumerate((r0, r1, r2, r3)):
        slot = lax.rem(z - d + ROWS, ROWS)
        out[pl.ds(pl.multiple_of(slot * SUB, SUB), SUB), :] = r[...]


def along_row(x, d):
    return lax.ppermute(x, "row", [(i, (i + d) % ROWS) for i in range(ROWS)])


def shards(prior, dynamics, gains, observed, owner, step):
    tm = lax.axis_index("tm").astype(jnp.int32)
    z = lax.axis_index("row").astype(jnp.int32)
    idx = jnp.stack([z, tm & 1, (tm >> 1) & 3, tm >> 3])
    prior = prior.reshape(1, N)
    flat = dynamics.reshape(ROWS * SUB * 64, N)

    def along_rows(blocks):
        return [along_row(b, d) for d, b in enumerate(blocks, 1)]

    ahead, back = call(
        send_kernel, [(SENT * 64, N)] * 2, idx, (), [pltpu.SemaphoreType.DMA((2 * SENT // COPIED,))], far=(flat,)
    )
    prev, after = along_row(ahead, 1), along_row(back, 3)

    rid = owner[:, 0] * 16 + step % 16 + 512 * (step // 16)
    partial = binned(rid.reshape(1, -1), observed.T)
    sums = lax.all_to_all(partial, "tm", 0, 0, tiled=True).reshape(32, 16, N)
    (info,) = call(sum_kernel, [(16, N)], idx, (sums,))
    infos = along_rows([info] * 3)
    staged, own = call(
        stage_kernel,
        [gains.shape, (SUB * 64, N)],
        idx,
        (info,),
        [pltpu.SemaphoreType.DMA((2,))],
        far=(gains, flat),
    )
    infos, staged, own, prev, after, idx, prior = lax.optimization_barrier(
        (infos, staged, own, prev, after, idx, prior)
    )
    pieces = call(relay_kernel, [(HALF_SUB * 64, N)] * 2, idx, (prev, after))
    pieces, infos = lax.optimization_barrier((pieces, infos))
    relayed = [along_row(p, d) for p, d in zip(pieces, (1, 3))]
    offs = call(
        offset_kernel,
        [(16, N)] * 4,
        idx,
        (staged, info, *infos),
        [pltpu.VMEM((ROWS, 16, N), F32), pltpu.VMEM((ROWS, 16, 128), F32)],
    )
    offs = [offs[0], *along_rows(offs[1:])]
    pref, whole = call(
        compose_kernel,
        [(SUB, R, N), (R, N)],
        idx,
        (own, prev, after, *relayed, *offs),
        [pltpu.VMEM((SUB, N, N), BF16)] * 2 + [pltpu.VMEM((ROWS, 16, N), F32)],
        mib=16,
    )

    block, before = call(
        four_kernel,
        [(R, N), (R, N)],
        idx,
        (whole, *[along_row(whole, d) for d in (1, 2, 3)]),
        [pltpu.VMEM((4, R, N), F32)],
    )

    def other_core(m):
        return lax.ppermute(m, "tm", [(i, i ^ 1) for i in range(32)])

    def gathered(half, stride):
        n = 4 * stride
        got = [
            lax.ppermute(half, "tm", [(i, i - i % n + (i + d * stride) % n) for i in range(32)]) for d in (1, 2, 3)
        ]
        return *got, *[other_core(g) for g in got]

    column, half, before = call(
        pair_kernel, [(R, N), (HALF, N), (R, N)], idx, (block, other_core(block), before)
    )
    half, ybefore = call(
        plane_kernel,
        [(HALF, N), (R, N)],
        idx,
        (column, *gathered(half, 2)),
        [pltpu.VMEM((4, R, N), F32), pltpu.VMEM((R, N), F32)],
    )
    (before,) = call(fold_kernel, [(R, N)], idx, (ybefore, before))
    outs = call(
        states_kernel,
        [(SUB, 64)] * 4,
        idx,
        (prior, *gathered(half, 8), before, pref),
        [pltpu.VMEM((ROWS, SUB, 64), F32), pltpu.VMEM((4, R, N), F32), pltpu.VMEM((PAD, N), F32)],
    )
    got = [outs[0], *along_rows(outs[1:])]
    return pl.pallas_call(
        place_kernel,
        out_shape=jax.ShapeDtypeStruct((64, 64), F32),
        in_specs=[SM] + [VM] * 4,
        out_specs=VM,
        compiler_params=pltpu.CompilerParams(vmem_limit_bytes=4 * MIB),
    )(idx, *[near(g) for g in got])


def solution(mesh):
    return jax.shard_map(
        shards,
        mesh=mesh,
        in_specs=(
            P(),
            P("tm", "row", None),
            P("tm", "row", None),
            P("tm", "row"),
            P("tm", None),
            P("tm"),
        ),
        out_specs=P("tm", "row"),
        check_vma=False,
    )
```

```python
import jax
import jax.numpy as jnp
from jax import lax
from jax.experimental import pallas as pl
from jax.experimental.pallas import tpu as pltpu
from jax.sharding import PartitionSpec as P

F32 = jnp.float32
BF16 = jnp.bfloat16
MIB = 1024 * 1024
VM = pl.BlockSpec(memory_space=pltpu.VMEM)
SM = pl.BlockSpec(memory_space=pltpu.SMEM)
N = 256
PAD = 16
R = N + PAD
Z, C, Y, X = range(4)
HALF = R // 2
ROWS = 4
SUB = 16
SEG = 4
HALF_SUB = SUB // 2
Z, C, Y, X = range(4)
HALF = R // 2
ROWS = 4
SUB = 16
CHUNKS = ((5, 5), (3, 3))
SEGS = tuple(n for chunk in CHUNKS for n in chunk)
SIZES = tuple(sum(chunk) for chunk in CHUNKS)
ENDS = tuple(sum(SEGS[: i + 1]) for i in range(len(SEGS)))


def split(x):
    hi = x.astype(BF16)
    return hi, (x - hi.astype(F32)).astype(BF16)


def dot_nn(a, b):
    return lax.dot_general(a, b, (((1,), (0,)), ((), ())), preferred_element_type=F32)


def dot_nt(a, b):
    return lax.dot_general(a, b, (((1,), (1,)), ((), ())), preferred_element_type=F32)


def mm(a, b, dot=dot_nn):
    ah, al = split(a)
    bh, bl = split(b)
    return dot(ah, bh) + dot(al, bh) + dot(ah, bl)


def then(first, second):
    out = mm(first, second[:N])
    return jnp.concatenate([out[:N], out[N:] + second[N:]], axis=0)


def apply(s, m):
    return mm(s, m[:N]) + m[N:]


def eye_map():
    r = lax.broadcasted_iota(jnp.int32, (R, N), 0)
    c = lax.broadcasted_iota(jnp.int32, (R, N), 1)
    return jnp.where(r == c, 1.0, 0.0).astype(F32)


FAR = pl.BlockSpec(memory_space=pltpu.HBM)


def near(x):
    return pltpu.with_memory_space_constraint(x, pltpu.VMEM)


def call(kernel, outs, idx, args, scratch=(), far=(), mib=8):
    outs = [o if isinstance(o[0], tuple) else (o, F32) for o in outs]
    return pl.pallas_call(
        kernel,
        out_shape=[pltpu.VMEM(s, t) for s, t in outs],
        in_specs=[SM] + [FAR] * len(far) + [VM] * len(args),
        out_specs=[VM] * len(outs),
        scratch_shapes=list(scratch),
        compiler_params=pltpu.CompilerParams(vmem_limit_bytes=mib * MIB),
    )(idx, *[pltpu.with_memory_space_constraint(f, pltpu.HBM) for f in far], *[near(a) for a in args])


BIN_M = 256


def bin_kernel(rid_ref, obs_ref, out_ref, rhs, acc):
    i = pl.program_id(0)
    n_m = pl.num_programs(0)

    @pl.when(i == 0)
    def _():
        x = obs_ref[...]
        hi = x.astype(BF16)
        rest = x - hi.astype(F32)
        mid = rest.astype(BF16)
        low = (rest - mid.astype(F32)).astype(BF16)
        rhs[...] = jnp.concatenate([hi, mid, low, jnp.zeros_like(hi)], axis=0)

    rows = lax.broadcasted_iota(jnp.int32, (BIN_M, rid_ref.shape[1]), 0) + i * BIN_M
    onehot = jnp.where(rows == rid_ref[...], 1.0, 0.0).astype(BF16)
    got = dot_nt(onehot, rhs[...])
    a = got[:, :128] + got[:, 128:]
    acc[pl.ds(pl.multiple_of(i * BIN_M, BIN_M), BIN_M), :] = a + pltpu.roll(a, 64, 1)

    @pl.when(i == n_m - 1)
    def _():
        part = out_ref.shape[0]
        low_half = lax.broadcasted_iota(jnp.int32, (part, 128), 1) < 64
        for h in range(2):
            even = acc[2 * h * part : (2 * h + 1) * part, :]
            odd = acc[(2 * h + 1) * part : (2 * h + 2) * part, :]
            out_ref[:, h * 128 : (h + 1) * 128] = jnp.where(low_half, even, odd)


def binned(rid, observed):
    n_bins = 2048
    width, obs_rows = observed.shape
    return pl.pallas_call(
        bin_kernel,
        out_shape=jax.ShapeDtypeStruct((n_bins // 4, N), F32),
        grid=(n_bins // BIN_M,),
        in_specs=[
            pl.BlockSpec((1, obs_rows), lambda i: (0, 0)),
            pl.BlockSpec((width, obs_rows), lambda i: (0, 0)),
        ],
        out_specs=pl.BlockSpec((n_bins // 4, N), lambda i: (0, 0)),
        scratch_shapes=[pltpu.VMEM((4 * width, obs_rows), BF16), pltpu.VMEM((n_bins, 128), F32)],
        compiler_params=pltpu.CompilerParams(vmem_limit_bytes=24 * MIB),
    )(rid, observed)


def assemble(z, own, prev, after, opposite, ah, al):
    for d in range(ROWS):
        slot = lax.rem(z - d + ROWS, ROWS)
        rows = pl.ds(pl.multiple_of(slot * 64, 64), 64)
        for k in range(SUB):
            ref, at = ((own, k), (prev, k), (opposite[k // HALF_SUB], k % HALF_SUB), (after, k))[d]
            hi, lo = split(ref[at * 64 : (at + 1) * 64, :])
            ah[k, rows, :] = hi
            al[k, rows, :] = lo


def compose_kernel(idx, own, prev, after, q1, q2, b0, b1, b2, b3, pref, top, low, ah, al, b_s):
    z = idx[Z]
    assemble(z, own, prev, after, (q1, q2), ah, al)
    for d, b in enumerate((b0, b1, b2, b3)):
        b_s[lax.rem(z - d + ROWS, ROWS)] = b[...]
    b = jnp.concatenate([b_s[i, :, :64] for i in range(ROWS)], axis=1)
    first = lax.broadcasted_iota(jnp.int32, (PAD, N), 0) == 0
    eye = lax.broadcasted_iota(jnp.int32, (N, N), 0) == lax.broadcasted_iota(jnp.int32, (N, N), 1)
    eye = jnp.where(eye, 1.0, 0.0).astype(BF16)
    chains = range(SUB // SEG)
    for t in range(SEG):
        for c in chains:
            k = c * SEG + t
            shift = jnp.where(first, b[k : k + 1, :], 0.0)
            if t == 0:
                pref[k, :N, :] = dot_nt(eye, ah[k]) + dot_nt(eye, al[k])
                pref[k, N:, :] = shift
            else:
                hi, lo = split(pref[k - 1])
                out = dot_nt(hi, ah[k]) + dot_nt(lo, ah[k]) + dot_nt(hi, al[k])
                pref[k, :N, :] = out[:N]
                pref[k, N:, :] = out[N:] + shift
    ends = [pref[c * SEG + SEG - 1] for c in chains]
    whole = then(then(ends[0], ends[1]), then(ends[2], ends[3]))
    top[...] = whole[:HALF]
    low[...] = whole[HALF:]


def combine(pos, m_s, before):
    m01 = then(m_s[0], m_s[1])
    m23 = then(m_s[2], m_s[3])
    before[...] = eye_map()

    @pl.when(pos == 1)
    def _():
        before[...] = m_s[0]

    @pl.when(pos == 2)
    def _():
        before[...] = m01

    @pl.when(pos == 3)
    def _():
        before[...] = then(m01, m_s[2])

    return then(m01, m23)


def four_kernel(idx, t0, l0, t1, l1, t2, l2, t3, l3, total, before, m_s):
    pos = idx[Z]
    for d, (t, l) in enumerate(((t0, l0), (t1, l1), (t2, l2), (t3, l3))):
        slot = lax.rem(pos - d + 4, 4)
        m_s[slot, :HALF, :] = t[...]
        m_s[slot, HALF:, :] = l[...]
    total[...] = combine(pos, m_s, before)


def half_rows(c):
    return pl.ds(pl.multiple_of(c * HALF, 8), HALF)


def join(pos, c, mine, others, m_s):
    for d, m, o in zip((3, 2, 1), mine, others):
        slot = lax.rem(pos - d + 4, 4)
        m_s[slot, half_rows(c), :] = m[...]
        m_s[slot, half_rows(1 - c), :] = o[...]


def plane_kernel(idx, own, h1, h2, h3, o1, o2, o3, half, before, m_s, all_s):
    pos, c = idx[Y], idx[C]
    m_s[pos] = own[...]
    join(pos, c, (h1, h2, h3), (o1, o2, o3), m_s)
    all_s[...] = combine(pos, m_s, before)
    half[...] = all_s[half_rows(c), :]


def pair_kernel(idx, own, other, before_in, total, half, before):
    c = idx[C]
    swap = c == 1

    @pl.when(swap)
    def _():
        total[...] = then(other[...], own[...])
        before[...] = then(other[...], before_in[...])

    @pl.when(jnp.logical_not(swap))
    def _():
        total[...] = then(own[...], other[...])
        before[...] = before_in[...]

    half[...] = total[half_rows(c), :]


def fold_kernel(idx, first, second, out):
    out[...] = then(first[...], second[...])


def states_kernel(idx, prior, h1, h2, h3, g1, g2, g3, before, pref, o0, o1, o2, o3, st_s, m_s, s_s):
    z, pos = idx[Z], idx[X]
    join(pos, idx[C], (h1, h2, h3), (g1, g2, g3), m_s)
    s_s[...] = jnp.where(lax.broadcasted_iota(jnp.int32, (PAD, N), 0) == 0, prior[...], 0.0)
    for i in range(3):

        @pl.when(i < pos)
        def _(i=i):
            s_s[...] = apply(s_s[...], m_s[i])

    s = apply(s_s[...], before[...])
    eye = lax.broadcasted_iota(jnp.int32, (N, N), 0) == lax.broadcasted_iota(jnp.int32, (N, N), 1)
    for end in range(SEG, SUB + 1, SEG):
        col = jnp.sum(jnp.where(eye, s[0:1, :], 0.0), axis=1, keepdims=True)
        for k in range(end - SEG, end):
            row = jnp.sum(pref[k, :N, :] * col, axis=0, keepdims=True) + pref[k, N : N + 1, :]
            for j in range(ROWS):
                st_s[j, k : k + 1, :] = row[:, j * 64 : (j + 1) * 64]
        if end < SUB:
            s = apply(s, pref[end - 1])
    for d, o in enumerate((o0, o1, o2, o3)):
        o[...] = st_s[lax.rem(z + d, ROWS)]


SENT = SUB + HALF_SUB
COPIED = 4


def send_kernel(idx, flat, ahead, back, sems):
    z = idx[Z]
    copies = []
    for way, out in enumerate((ahead, back)):
        for at in range(0, SENT, COPIED):
            d, first = ((1, 3)[way], at) if at < SUB else (2, at - SUB + way * HALF_SUB)
            source = lax.rem(z + d, ROWS) * (SUB * 64) + first * 64
            copies.append(
                pltpu.make_async_copy(
                    flat.at[pl.ds(pl.multiple_of(source, 64), COPIED * 64)],
                    out.at[pl.ds(at * 64, COPIED * 64)],
                    sems.at[len(copies)],
                )
            )
    for copy in copies:
        copy.start()
    for copy in copies:
        copy.wait()


def relay_kernel(idx, prev, after, p, a):
    p[...] = prev[SUB * 64 :, :]
    a[...] = after[SUB * 64 :, :]


def stage_kernel(idx, gains, flat, info, staged, own, sems):
    copies = [
        pltpu.make_async_copy(gains, staged, sems.at[0]),
        pltpu.make_async_copy(flat.at[pl.ds(pl.multiple_of(idx[Z] * (SUB * 64), 64), SUB * 64)], own, sems.at[1]),
    ]
    for copy in copies:
        copy.start()
    for copy in copies:
        copy.wait()


def sum_kernel(idx, sums, info):
    info[...] = jnp.sum(sums[...], axis=0)


def offset_kernel(idx, g, i0, r1, r2, r3, o0, o1, o2, o3, info_s, off_s):
    z = idx[Z]
    info_s[z] = i0[...]
    for d, r in ((1, r1), (2, r2), (3, r3)):
        info_s[lax.rem(z - d + ROWS, ROWS)] = r[...]
    lane = lax.broadcasted_iota(jnp.int32, (64, 128), 1)
    for q in range(4):
        full = jnp.concatenate([info_s[i, :, q * 64 : (q + 1) * 64] for i in range(ROWS)], axis=1)
        acc = jnp.zeros((64, 128), F32)
        for k in range(16):
            col = jnp.sum(g[16 * q + k] * full[k : k + 1, :], axis=1, keepdims=True)
            acc = jnp.where(lane == k, col, acc)
        off_s[q] = jnp.concatenate([acc, jnp.zeros((64, 128), F32)], axis=0).T[:16, :]
    for d, o in enumerate((o0, o1, o2, o3)):
        o[:, :128] = off_s[lax.rem(z + d, ROWS)]
        o[:, 128:] = jnp.zeros((16, 128), F32)


def place_kernel(idx, r0, r1, r2, r3, out):
    z = idx[Z]
    for d, r in enumerate((r0, r1, r2, r3)):
        slot = lax.rem(z - d + ROWS, ROWS)
        out[pl.ds(pl.multiple_of(slot * SUB, SUB), SUB), :] = r[...]


def along_row(x, d):
    return lax.ppermute(x, "row", [(i, (i + d) % ROWS) for i in range(ROWS)])


def shards(prior, dynamics, gains, observed, owner, step):
    tm = lax.axis_index("tm").astype(jnp.int32)
    z = lax.axis_index("row").astype(jnp.int32)
    idx = jnp.stack([z, tm & 1, (tm >> 1) & 3, tm >> 3])
    prior = prior.reshape(1, N)
    flat = dynamics.reshape(ROWS * SUB * 64, N)

    def along_rows(blocks):
        return [along_row(b, d) for d, b in enumerate(blocks, 1)]

    ahead, back = call(
        send_kernel, [(SENT * 64, N)] * 2, idx, (), [pltpu.SemaphoreType.DMA((2 * SENT // COPIED,))], far=(flat,)
    )
    prev, after = along_row(ahead, 1), along_row(back, 3)

    rid = owner[:, 0] * 16 + step % 16 + 512 * (step // 16)
    partial = binned(rid.reshape(1, -1), observed.T)
    sums = lax.all_to_all(partial, "tm", 0, 0, tiled=True).reshape(32, 16, N)
    (info,) = call(sum_kernel, [(16, N)], idx, (sums,))
    infos = along_rows([info] * 3)
    staged, own = call(
        stage_kernel,
        [gains.shape, (SUB * 64, N)],
        idx,
        (info,),
        [pltpu.SemaphoreType.DMA((2,))],
        far=(gains, flat),
    )
    infos[0], infos[2], staged, own, prev, after, idx, prior = lax.optimization_barrier(
        (infos[0], infos[2], staged, own, prev, after, idx, prior)
    )
    pieces = call(relay_kernel, [(HALF_SUB * 64, N)] * 2, idx, (prev, after))
    pieces, infos = lax.optimization_barrier((pieces, infos))
    relayed = [along_row(p, d) for p, d in zip(pieces, (1, 3))]
    offs = call(
        offset_kernel,
        [(16, N)] * 4,
        idx,
        (staged, info, *infos),
        [pltpu.VMEM((ROWS, 16, N), F32), pltpu.VMEM((ROWS, 16, 128), F32)],
    )
    offs = [offs[0], *along_rows(offs[1:])]
    pref, top, low = call(
        compose_kernel,
        [(SUB, R, N), (HALF, N), (HALF, N)],
        idx,
        (own, prev, after, *relayed, *offs),
        [pltpu.VMEM((SUB, N, N), BF16)] * 2 + [pltpu.VMEM((ROWS, 16, N), F32)],
        mib=16,
    )

    prev_top, after_low = along_row(top, 1), along_row(low, 3)
    prev_low, after_top = along_row(low, 1), along_row(top, 3)
    block, before = call(
        four_kernel,
        [(R, N), (R, N)],
        idx,
        (top, low, prev_top, prev_low, along_row(prev_top, 1), along_row(after_low, 3), after_top, after_low),
        [pltpu.VMEM((4, R, N), F32)],
    )

    def other_core(m):
        return lax.ppermute(m, "tm", [(i, i ^ 1) for i in range(32)])

    def gathered(half, stride):
        n = 4 * stride
        got = [
            lax.ppermute(half, "tm", [(i, i - i % n + (i + d * stride) % n) for i in range(32)]) for d in (3, 2, 1)
        ]
        return *got, *[other_core(g) for g in got]

    column, half, before = call(
        pair_kernel, [(R, N), (HALF, N), (R, N)], idx, (block, other_core(block), before)
    )
    half, ybefore = call(
        plane_kernel,
        [(HALF, N), (R, N)],
        idx,
        (column, *gathered(half, 2)),
        [pltpu.VMEM((4, R, N), F32), pltpu.VMEM((R, N), F32)],
    )
    (before,) = call(fold_kernel, [(R, N)], idx, (ybefore, before))
    outs = call(
        states_kernel,
        [(SUB, 64)] * 4,
        idx,
        (prior, *gathered(half, 8), before, pref),
        [pltpu.VMEM((ROWS, SUB, 64), F32), pltpu.VMEM((4, R, N), F32), pltpu.VMEM((PAD, N), F32)],
    )
    got = [outs[0], *along_rows(outs[1:])]
    return pl.pallas_call(
        place_kernel,
        out_shape=jax.ShapeDtypeStruct((64, 64), F32),
        in_specs=[SM] + [VM] * 4,
        out_specs=VM,
        compiler_params=pltpu.CompilerParams(vmem_limit_bytes=4 * MIB),
    )(idx, *[near(g) for g in got])


def solution(mesh):
    return jax.shard_map(
        shards,
        mesh=mesh,
        in_specs=(
            P(),
            P("tm", "row", None),
            P("tm", "row", None),
            P("tm", "row"),
            P("tm", None),
            P("tm"),
        ),
        out_specs=P("tm", "row"),
        check_vma=False,
    )
```

```python
import jax
import jax.numpy as jnp
from jax import lax
from jax.experimental import pallas as pl
from jax.experimental.pallas import tpu as pltpu
from jax.sharding import PartitionSpec as P

F32 = jnp.float32
BF16 = jnp.bfloat16
MIB = 1024 * 1024
VM = pl.BlockSpec(memory_space=pltpu.VMEM)
SM = pl.BlockSpec(memory_space=pltpu.SMEM)
N = 256
PAD = 16
R = N + PAD
Z, C, Y, X = range(4)
HALF = R // 2
UPPER = 72
ROWS = 4
SUB = 16
SEG = 4
HALF_SUB = SUB // 2
Z, C, Y, X = range(4)
HALF = R // 2
UPPER = 72
ROWS = 4
SUB = 16
CHUNKS = ((5, 5), (3, 3))
SEGS = tuple(n for chunk in CHUNKS for n in chunk)
SIZES = tuple(sum(chunk) for chunk in CHUNKS)
ENDS = tuple(sum(SEGS[: i + 1]) for i in range(len(SEGS)))


def split(x):
    hi = x.astype(BF16)
    return hi, (x - hi.astype(F32)).astype(BF16)


def dot_nn(a, b):
    return lax.dot_general(a, b, (((1,), (0,)), ((), ())), preferred_element_type=F32)


def dot_nt(a, b):
    return lax.dot_general(a, b, (((1,), (1,)), ((), ())), preferred_element_type=F32)


def mm(a, b, dot=dot_nn):
    ah, al = split(a)
    bh, bl = split(b)
    return dot(ah, bh) + dot(al, bh) + dot(ah, bl)


def then(first, second):
    out = mm(first, second[:N])
    return jnp.concatenate([out[:N], out[N:] + second[N:]], axis=0)


def apply(s, m):
    return mm(s, m[:N]) + m[N:]


def eye_map():
    r = lax.broadcasted_iota(jnp.int32, (R, N), 0)
    c = lax.broadcasted_iota(jnp.int32, (R, N), 1)
    return jnp.where(r == c, 1.0, 0.0).astype(F32)


FAR = pl.BlockSpec(memory_space=pltpu.HBM)


def near(x):
    return pltpu.with_memory_space_constraint(x, pltpu.VMEM)


def call(kernel, outs, idx, args, scratch=(), far=(), mib=8):
    outs = [o if isinstance(o[0], tuple) else (o, F32) for o in outs]
    return pl.pallas_call(
        kernel,
        out_shape=[pltpu.VMEM(s, t) for s, t in outs],
        in_specs=[SM] + [FAR] * len(far) + [VM] * len(args),
        out_specs=[VM] * len(outs),
        scratch_shapes=list(scratch),
        compiler_params=pltpu.CompilerParams(vmem_limit_bytes=mib * MIB),
    )(idx, *[pltpu.with_memory_space_constraint(f, pltpu.HBM) for f in far], *[near(a) for a in args])


BIN_M = 256


def bin_kernel(rid_ref, obs_ref, out_ref, rhs, acc):
    i = pl.program_id(0)
    n_m = pl.num_programs(0)

    @pl.when(i == 0)
    def _():
        x = obs_ref[...]
        hi = x.astype(BF16)
        rest = x - hi.astype(F32)
        mid = rest.astype(BF16)
        low = (rest - mid.astype(F32)).astype(BF16)
        rhs[...] = jnp.concatenate([hi, mid, low, jnp.zeros_like(hi)], axis=0)

    rows = lax.broadcasted_iota(jnp.int32, (BIN_M, rid_ref.shape[1]), 0) + i * BIN_M
    onehot = jnp.where(rows == rid_ref[...], 1.0, 0.0).astype(BF16)
    got = dot_nt(onehot, rhs[...])
    a = got[:, :128] + got[:, 128:]
    acc[pl.ds(pl.multiple_of(i * BIN_M, BIN_M), BIN_M), :] = a + pltpu.roll(a, 64, 1)

    @pl.when(i == n_m - 1)
    def _():
        part = out_ref.shape[0]
        low_half = lax.broadcasted_iota(jnp.int32, (part, 128), 1) < 64
        for h in range(2):
            even = acc[2 * h * part : (2 * h + 1) * part, :]
            odd = acc[(2 * h + 1) * part : (2 * h + 2) * part, :]
            out_ref[:, h * 128 : (h + 1) * 128] = jnp.where(low_half, even, odd)


def binned(rid, observed):
    n_bins = 2048
    width, obs_rows = observed.shape
    return pl.pallas_call(
        bin_kernel,
        out_shape=jax.ShapeDtypeStruct((n_bins // 4, N), F32),
        grid=(n_bins // BIN_M,),
        in_specs=[
            pl.BlockSpec((1, obs_rows), lambda i: (0, 0)),
            pl.BlockSpec((width, obs_rows), lambda i: (0, 0)),
        ],
        out_specs=pl.BlockSpec((n_bins // 4, N), lambda i: (0, 0)),
        scratch_shapes=[pltpu.VMEM((4 * width, obs_rows), BF16), pltpu.VMEM((n_bins, 128), F32)],
        compiler_params=pltpu.CompilerParams(vmem_limit_bytes=24 * MIB),
    )(rid, observed)


def assemble(z, own, prev, after, opposite, ah, al):
    for d in range(ROWS):
        slot = lax.rem(z - d + ROWS, ROWS)
        rows = pl.ds(pl.multiple_of(slot * 64, 64), 64)
        for k in range(SUB):
            ref, at = ((own, k), (prev, k), (opposite[k // HALF_SUB], k % HALF_SUB), (after, k))[d]
            hi, lo = split(ref[at * 64 : (at + 1) * 64, :])
            ah[k, rows, :] = hi
            al[k, rows, :] = lo


def compose_kernel(idx, own, prev, after, q1, q2, b0, b1, b2, b3, pref, top, low, ah, al, b_s):
    z = idx[Z]
    assemble(z, own, prev, after, (q1, q2), ah, al)
    for d, b in enumerate((b0, b1, b2, b3)):
        b_s[lax.rem(z - d + ROWS, ROWS)] = b[...]
    b = jnp.concatenate([b_s[i, :, :64] for i in range(ROWS)], axis=1)
    first = lax.broadcasted_iota(jnp.int32, (PAD, N), 0) == 0
    eye = lax.broadcasted_iota(jnp.int32, (N, N), 0) == lax.broadcasted_iota(jnp.int32, (N, N), 1)
    eye = jnp.where(eye, 1.0, 0.0).astype(BF16)
    chains = range(SUB // SEG)
    for t in range(SEG):
        for c in chains:
            k = c * SEG + t
            shift = jnp.where(first, b[k : k + 1, :], 0.0)
            if t == 0:
                pref[k, :N, :] = dot_nt(eye, ah[k]) + dot_nt(eye, al[k])
                pref[k, N:, :] = shift
            else:
                hi, lo = split(pref[k - 1])
                out = dot_nt(hi, ah[k]) + dot_nt(lo, ah[k]) + dot_nt(hi, al[k])
                pref[k, :N, :] = out[:N]
                pref[k, N:, :] = out[N:] + shift
    ends = [pref[c * SEG + SEG - 1] for c in chains]
    whole = then(then(ends[0], ends[1]), then(ends[2], ends[3]))
    top[...] = whole[:HALF]
    low[...] = whole[HALF:]


def combine(pos, m_s, before):
    m01 = then(m_s[0], m_s[1])
    m23 = then(m_s[2], m_s[3])
    before[...] = eye_map()

    @pl.when(pos == 1)
    def _():
        before[...] = m_s[0]

    @pl.when(pos == 2)
    def _():
        before[...] = m01

    @pl.when(pos == 3)
    def _():
        before[...] = then(m01, m_s[2])

    return then(m01, m23)


def four_kernel(idx, t0, l0, t1, l1, t2, l2, t3, l3, total, before, m_s):
    pos = idx[Z]
    for d, (t, l) in enumerate(((t0, l0), (t1, l1), (t2, l2), (t3, l3))):
        slot = lax.rem(pos - d + 4, 4)
        m_s[slot, :HALF, :] = t[...]
        m_s[slot, HALF:, :] = l[...]
    total[...] = combine(pos, m_s, before)


def cut_half(c, whole, upper, lower):
    at = pl.multiple_of(c * HALF, 8)
    upper[...] = whole[pl.ds(at, UPPER), :]
    lower[...] = whole[pl.ds(at + UPPER, HALF - UPPER), :]


def join(pos, c, mine, others, m_s):
    for side, parts in ((c, mine), (1 - c, others)):
        at = pl.multiple_of(side * HALF, 8)
        for d, (u, l) in zip((1, 3, 2), zip(parts[::2], parts[1::2])):
            slot = lax.rem(pos - d + 4, 4)
            m_s[slot, pl.ds(at, UPPER), :] = u[...]
            m_s[slot, pl.ds(at + UPPER, HALF - UPPER), :] = l[...]


def plane_kernel(idx, own, *refs):
    mine, others, (upper, lower, before, m_s, all_s) = refs[:6], refs[6:12], refs[12:]
    pos, c = idx[Y], idx[C]
    m_s[pos] = own[...]
    join(pos, c, mine, others, m_s)
    all_s[...] = combine(pos, m_s, before)
    cut_half(c, all_s, upper, lower)


def pair_kernel(idx, own, other, before_in, total, upper, lower, before):
    c = idx[C]
    swap = c == 1

    @pl.when(swap)
    def _():
        total[...] = then(other[...], own[...])
        before[...] = then(other[...], before_in[...])

    @pl.when(jnp.logical_not(swap))
    def _():
        total[...] = then(own[...], other[...])
        before[...] = before_in[...]

    cut_half(c, total, upper, lower)


def fold_kernel(idx, first, second, out):
    out[...] = then(first[...], second[...])


def states_kernel(idx, prior, *refs):
    mine, others, (before, pref, o0, o1, o2, o3, st_s, m_s, s_s) = refs[:6], refs[6:12], refs[12:]
    z, pos = idx[Z], idx[X]
    join(pos, idx[C], mine, others, m_s)
    s_s[...] = jnp.where(lax.broadcasted_iota(jnp.int32, (PAD, N), 0) == 0, prior[...], 0.0)
    for i in range(3):

        @pl.when(i < pos)
        def _(i=i):
            s_s[...] = apply(s_s[...], m_s[i])

    s = apply(s_s[...], before[...])
    eye = lax.broadcasted_iota(jnp.int32, (N, N), 0) == lax.broadcasted_iota(jnp.int32, (N, N), 1)
    for end in range(SEG, SUB + 1, SEG):
        col = jnp.sum(jnp.where(eye, s[0:1, :], 0.0), axis=1, keepdims=True)
        for k in range(end - SEG, end):
            row = jnp.sum(pref[k, :N, :] * col, axis=0, keepdims=True) + pref[k, N : N + 1, :]
            for j in range(ROWS):
                st_s[j, k : k + 1, :] = row[:, j * 64 : (j + 1) * 64]
        if end < SUB:
            s = apply(s, pref[end - 1])
    for d, o in enumerate((o0, o1, o2, o3)):
        o[...] = st_s[lax.rem(z + d, ROWS)]


SENT = SUB + HALF_SUB
COPIED = 4


def send_kernel(idx, flat, ahead, back, sems):
    z = idx[Z]
    copies = []
    for way, out in enumerate((ahead, back)):
        for at in range(0, SENT, COPIED):
            d, first = ((1, 3)[way], at) if at < SUB else (2, at - SUB + way * HALF_SUB)
            source = lax.rem(z + d, ROWS) * (SUB * 64) + first * 64
            copies.append(
                pltpu.make_async_copy(
                    flat.at[pl.ds(pl.multiple_of(source, 64), COPIED * 64)],
                    out.at[pl.ds(at * 64, COPIED * 64)],
                    sems.at[len(copies)],
                )
            )
    for copy in copies:
        copy.start()
    for copy in copies:
        copy.wait()


def relay_kernel(idx, prev, after, p, a):
    p[...] = prev[SUB * 64 :, :]
    a[...] = after[SUB * 64 :, :]


def stage_kernel(idx, gains, flat, info, staged, own, sems):
    copies = [
        pltpu.make_async_copy(gains, staged, sems.at[0]),
        pltpu.make_async_copy(flat.at[pl.ds(pl.multiple_of(idx[Z] * (SUB * 64), 64), SUB * 64)], own, sems.at[1]),
    ]
    for copy in copies:
        copy.start()
    for copy in copies:
        copy.wait()


def sum_kernel(idx, sums, info):
    info[...] = jnp.sum(sums[...], axis=0)


def offset_kernel(idx, g, i0, r1, r2, r3, o0, o1, o2, o3, info_s, off_s):
    z = idx[Z]
    info_s[z] = i0[...]
    for d, r in ((1, r1), (2, r2), (3, r3)):
        info_s[lax.rem(z - d + ROWS, ROWS)] = r[...]
    lane = lax.broadcasted_iota(jnp.int32, (64, 128), 1)
    for q in range(4):
        full = jnp.concatenate([info_s[i, :, q * 64 : (q + 1) * 64] for i in range(ROWS)], axis=1)
        acc = jnp.zeros((64, 128), F32)
        for k in range(16):
            col = jnp.sum(g[16 * q + k] * full[k : k + 1, :], axis=1, keepdims=True)
            acc = jnp.where(lane == k, col, acc)
        off_s[q] = jnp.concatenate([acc, jnp.zeros((64, 128), F32)], axis=0).T[:16, :]
    for d, o in enumerate((o0, o1, o2, o3)):
        o[:, :128] = off_s[lax.rem(z + d, ROWS)]
        o[:, 128:] = jnp.zeros((16, 128), F32)


def place_kernel(idx, r0, r2, r1, r3, out):
    z = idx[Z]
    for d, r in enumerate((r0, r1, r2, r3)):
        slot = lax.rem(z - d + ROWS, ROWS)
        out[pl.ds(pl.multiple_of(slot * SUB, SUB), SUB), :] = r[...]


def along_row(x, d):
    return lax.ppermute(x, "row", [(i, (i + d) % ROWS) for i in range(ROWS)])


def shards(prior, dynamics, gains, observed, owner, step):
    tm = lax.axis_index("tm").astype(jnp.int32)
    z = lax.axis_index("row").astype(jnp.int32)
    idx = jnp.stack([z, tm & 1, (tm >> 1) & 3, tm >> 3])
    prior = prior.reshape(1, N)
    flat = dynamics.reshape(ROWS * SUB * 64, N)

    def along_rows(blocks):
        return [along_row(b, d) for d, b in enumerate(blocks, 1)]

    ahead, back = call(
        send_kernel, [(SENT * 64, N)] * 2, idx, (), [pltpu.SemaphoreType.DMA((2 * SENT // COPIED,))], far=(flat,)
    )
    prev, after = along_row(ahead, 1), along_row(back, 3)

    rid = owner[:, 0] * 16 + step % 16 + 512 * (step // 16)
    partial = binned(rid.reshape(1, -1), observed.T)
    sums = lax.all_to_all(partial, "tm", 0, 0, tiled=True).reshape(32, 16, N)
    (info,) = call(sum_kernel, [(16, N)], idx, (sums,))
    infos = along_rows([info] * 3)
    staged, own = call(
        stage_kernel,
        [gains.shape, (SUB * 64, N)],
        idx,
        (info,),
        [pltpu.SemaphoreType.DMA((2,))],
        far=(gains, flat),
    )
    infos[0], infos[2], staged, own, prev, after, idx, prior = lax.optimization_barrier(
        (infos[0], infos[2], staged, own, prev, after, idx, prior)
    )
    pieces = call(relay_kernel, [(HALF_SUB * 64, N)] * 2, idx, (prev, after))
    pieces, infos = lax.optimization_barrier((pieces, infos))
    relayed = [along_row(p, d) for p, d in zip(pieces, (1, 3))]
    offs = call(
        offset_kernel,
        [(16, N)] * 4,
        idx,
        (staged, info, *infos),
        [pltpu.VMEM((ROWS, 16, N), F32), pltpu.VMEM((ROWS, 16, 128), F32)],
    )
    offs = [offs[0], *along_rows(offs[1:])]
    pref, top, low = call(
        compose_kernel,
        [(SUB, R, N), (HALF, N), (HALF, N)],
        idx,
        (own, prev, after, *relayed, *offs),
        [pltpu.VMEM((SUB, N, N), BF16)] * 2 + [pltpu.VMEM((ROWS, 16, N), F32)],
        mib=16,
    )

    prev_top, after_low = along_row(top, 1), along_row(low, 3)
    prev_low, after_top = along_row(low, 1), along_row(top, 3)
    block, before = call(
        four_kernel,
        [(R, N), (R, N)],
        idx,
        (top, low, prev_top, prev_low, along_row(prev_top, 1), along_row(after_low, 3), after_top, after_low),
        [pltpu.VMEM((4, R, N), F32)],
    )

    def other_core(m):
        return lax.ppermute(m, "tm", [(i, i ^ 1) for i in range(32)])

    def gathered(upper, lower, stride):
        n = 4 * stride

        def along(m, d):
            return lax.ppermute(m, "tm", [(i, i - i % n + (i + d * stride) % n) for i in range(32)])

        prev_upper, after_lower = along(upper, 1), along(lower, 3)
        got = prev_upper, along(lower, 1), along(upper, 3), after_lower, along(prev_upper, 1), along(after_lower, 3)
        return *got, *[other_core(g) for g in got]

    quarters = [(UPPER, N), (HALF - UPPER, N)]
    column, *cut, before = call(
        pair_kernel, [(R, N), *quarters, (R, N)], idx, (block, other_core(block), before)
    )
    *cut, ybefore = call(
        plane_kernel,
        [*quarters, (R, N)],
        idx,
        (column, *gathered(*cut, 2)),
        [pltpu.VMEM((4, R, N), F32), pltpu.VMEM((R, N), F32)],
    )
    (before,) = call(fold_kernel, [(R, N)], idx, (ybefore, before))
    outs = call(
        states_kernel,
        [(SUB, 64)] * 4,
        idx,
        (prior, *gathered(*cut, 8), before, pref),
        [pltpu.VMEM((ROWS, SUB, 64), F32), pltpu.VMEM((4, R, N), F32), pltpu.VMEM((PAD, N), F32)],
    )
    got = [outs[0], along_row(outs[2], 2), along_row(outs[1], 1), along_row(outs[3], 3)]
    return pl.pallas_call(
        place_kernel,
        out_shape=jax.ShapeDtypeStruct((64, 64), F32),
        in_specs=[SM] + [VM] * 4,
        out_specs=VM,
        compiler_params=pltpu.CompilerParams(vmem_limit_bytes=4 * MIB),
    )(idx, *[near(g) for g in got])


def solution(mesh):
    return jax.shard_map(
        shards,
        mesh=mesh,
        in_specs=(
            P(),
            P("tm", "row", None),
            P("tm", "row", None),
            P("tm", "row"),
            P("tm", None),
            P("tm"),
        ),
        out_specs=P("tm", "row"),
        check_vma=False,
    )
```

```python
import jax
import jax.numpy as jnp
from jax import lax
from jax.experimental import pallas as pl
from jax.experimental.pallas import tpu as pltpu
from jax.sharding import PartitionSpec as P

F32 = jnp.float32
BF16 = jnp.bfloat16
MIB = 1024 * 1024
VM = pl.BlockSpec(memory_space=pltpu.VMEM)
SM = pl.BlockSpec(memory_space=pltpu.SMEM)
N = 256
PAD = 16
R = N + PAD
Z, C, Y, X = range(4)
HALF = R // 2
ROWS = 4
SUB = 16
SEG = 4
HALF_SUB = SUB // 2
Z, C, Y, X = range(4)
HALF = R // 2
ROWS = 4
SUB = 16
CHUNKS = ((5, 5), (3, 3))
SEGS = tuple(n for chunk in CHUNKS for n in chunk)
SIZES = tuple(sum(chunk) for chunk in CHUNKS)
ENDS = tuple(sum(SEGS[: i + 1]) for i in range(len(SEGS)))


def split(x):
    hi = x.astype(BF16)
    return hi, (x - hi.astype(F32)).astype(BF16)


def dot_nn(a, b):
    return lax.dot_general(a, b, (((1,), (0,)), ((), ())), preferred_element_type=F32)


def dot_nt(a, b):
    return lax.dot_general(a, b, (((1,), (1,)), ((), ())), preferred_element_type=F32)


def mm(a, b, dot=dot_nn):
    ah, al = split(a)
    bh, bl = split(b)
    return dot(ah, bh) + dot(al, bh) + dot(ah, bl)


def then(first, second):
    out = mm(first, second[:N])
    return jnp.concatenate([out[:N], out[N:] + second[N:]], axis=0)


def apply(s, m):
    return mm(s, m[:N]) + m[N:]


def eye_map():
    r = lax.broadcasted_iota(jnp.int32, (R, N), 0)
    c = lax.broadcasted_iota(jnp.int32, (R, N), 1)
    return jnp.where(r == c, 1.0, 0.0).astype(F32)


FAR = pl.BlockSpec(memory_space=pltpu.HBM)


def near(x):
    return pltpu.with_memory_space_constraint(x, pltpu.VMEM)


def call(kernel, outs, idx, args, scratch=(), far=(), mib=8):
    outs = [o if isinstance(o[0], tuple) else (o, F32) for o in outs]
    return pl.pallas_call(
        kernel,
        out_shape=[pltpu.VMEM(s, t) for s, t in outs],
        in_specs=[SM] + [FAR] * len(far) + [VM] * len(args),
        out_specs=[VM] * len(outs),
        scratch_shapes=list(scratch),
        compiler_params=pltpu.CompilerParams(vmem_limit_bytes=mib * MIB),
    )(idx, *[pltpu.with_memory_space_constraint(f, pltpu.HBM) for f in far], *[near(a) for a in args])


BIN_M = 256


def bin_kernel(rid_ref, obs_ref, out_ref, rhs, acc):
    i = pl.program_id(0)
    n_m = pl.num_programs(0)

    @pl.when(i == 0)
    def _():
        x = obs_ref[...]
        hi = x.astype(BF16)
        rest = x - hi.astype(F32)
        mid = rest.astype(BF16)
        low = (rest - mid.astype(F32)).astype(BF16)
        rhs[...] = jnp.concatenate([hi, mid, low, jnp.zeros_like(hi)], axis=0)

    rows = lax.broadcasted_iota(jnp.int32, (BIN_M, rid_ref.shape[1]), 0) + i * BIN_M
    onehot = jnp.where(rows == rid_ref[...], 1.0, 0.0).astype(BF16)
    got = dot_nt(onehot, rhs[...])
    a = got[:, :128] + got[:, 128:]
    acc[pl.ds(pl.multiple_of(i * BIN_M, BIN_M), BIN_M), :] = a + pltpu.roll(a, 64, 1)

    @pl.when(i == n_m - 1)
    def _():
        part = out_ref.shape[0]
        low_half = lax.broadcasted_iota(jnp.int32, (part, 128), 1) < 64
        for h in range(2):
            even = acc[2 * h * part : (2 * h + 1) * part, :]
            odd = acc[(2 * h + 1) * part : (2 * h + 2) * part, :]
            out_ref[:, h * 128 : (h + 1) * 128] = jnp.where(low_half, even, odd)


def binned(rid, observed):
    n_bins = 2048
    width, obs_rows = observed.shape
    return pl.pallas_call(
        bin_kernel,
        out_shape=jax.ShapeDtypeStruct((n_bins // 4, N), F32),
        grid=(n_bins // BIN_M,),
        in_specs=[
            pl.BlockSpec((1, obs_rows), lambda i: (0, 0)),
            pl.BlockSpec((width, obs_rows), lambda i: (0, 0)),
        ],
        out_specs=pl.BlockSpec((n_bins // 4, N), lambda i: (0, 0)),
        scratch_shapes=[pltpu.VMEM((4 * width, obs_rows), BF16), pltpu.VMEM((n_bins, 128), F32)],
        compiler_params=pltpu.CompilerParams(vmem_limit_bytes=24 * MIB),
    )(rid, observed)


def assemble(z, own, prev, after, opposite, ah, al):
    for d in range(ROWS):
        slot = lax.rem(z - d + ROWS, ROWS)
        rows = pl.ds(pl.multiple_of(slot * 64, 64), 64)
        for k in range(SUB):
            ref, at = ((own, k), (prev, k), (opposite[k // HALF_SUB], k % HALF_SUB), (after, k))[d]
            hi, lo = split(ref[at * 64 : (at + 1) * 64, :])
            ah[k, rows, :] = hi
            al[k, rows, :] = lo


def compose_kernel(idx, own, prev, after, q1, q2, b0, b1, b2, b3, pref, top, low, ah, al, b_s):
    z = idx[Z]
    assemble(z, own, prev, after, (q1, q2), ah, al)
    for d, b in enumerate((b0, b1, b2, b3)):
        b_s[lax.rem(z - d + ROWS, ROWS)] = b[...]
    b = jnp.concatenate([b_s[i, :, :64] for i in range(ROWS)], axis=1)
    first = lax.broadcasted_iota(jnp.int32, (PAD, N), 0) == 0
    eye = lax.broadcasted_iota(jnp.int32, (N, N), 0) == lax.broadcasted_iota(jnp.int32, (N, N), 1)
    eye = jnp.where(eye, 1.0, 0.0).astype(BF16)
    chains = range(SUB // SEG)
    for t in range(SEG):
        for c in chains:
            k = c * SEG + t
            shift = jnp.where(first, b[k : k + 1, :], 0.0)
            if t == 0:
                pref[k, :N, :] = dot_nt(eye, ah[k]) + dot_nt(eye, al[k])
                pref[k, N:, :] = shift
            else:
                hi, lo = split(pref[k - 1])
                out = dot_nt(hi, ah[k]) + dot_nt(lo, ah[k]) + dot_nt(hi, al[k])
                pref[k, :N, :] = out[:N]
                pref[k, N:, :] = out[N:] + shift
    ends = [pref[c * SEG + SEG - 1] for c in chains]
    whole = then(then(ends[0], ends[1]), then(ends[2], ends[3]))
    top[...] = whole[:HALF]
    low[...] = whole[HALF:]


def combine(pos, m_s, before):
    m01 = then(m_s[0], m_s[1])
    m23 = then(m_s[2], m_s[3])
    before[...] = eye_map()

    @pl.when(pos == 1)
    def _():
        before[...] = m_s[0]

    @pl.when(pos == 2)
    def _():
        before[...] = m01

    @pl.when(pos == 3)
    def _():
        before[...] = then(m01, m_s[2])

    return then(m01, m23)


def four_kernel(idx, t0, l0, t1, l1, t2, l2, t3, l3, total, before, m_s):
    pos = idx[Z]
    for d, (t, l) in enumerate(((t0, l0), (t1, l1), (t2, l2), (t3, l3))):
        slot = lax.rem(pos - d + 4, 4)
        m_s[slot, :HALF, :] = t[...]
        m_s[slot, HALF:, :] = l[...]
    total[...] = combine(pos, m_s, before)


def half_rows(c):
    return pl.ds(pl.multiple_of(c * HALF, 8), HALF)


def join(pos, c, mine, others, m_s):
    for d, m, o in zip((3, 1, 2), mine, others):
        slot = lax.rem(pos - d + 4, 4)
        m_s[slot, half_rows(c), :] = m[...]
        m_s[slot, half_rows(1 - c), :] = o[...]


def plane_kernel(idx, own, h1, h2, h3, o1, o2, o3, half, before, m_s, all_s):
    pos, c = idx[Y], idx[C]
    m_s[pos] = own[...]
    join(pos, c, (h1, h2, h3), (o1, o2, o3), m_s)
    all_s[...] = combine(pos, m_s, before)
    half[...] = all_s[half_rows(c), :]


def pair_kernel(idx, own, other, before_in, total, half, before):
    c = idx[C]
    swap = c == 1

    @pl.when(swap)
    def _():
        total[...] = then(other[...], own[...])
        before[...] = then(other[...], before_in[...])

    @pl.when(jnp.logical_not(swap))
    def _():
        total[...] = then(own[...], other[...])
        before[...] = before_in[...]

    half[...] = total[half_rows(c), :]


def fold_kernel(idx, first, second, out):
    out[...] = then(first[...], second[...])


def states_kernel(idx, prior, h1, h2, h3, g1, g2, g3, before, pref, o0, o1, o2, o3, st_s, m_s, s_s):
    z, pos = idx[Z], idx[X]
    join(pos, idx[C], (h1, h2, h3), (g1, g2, g3), m_s)
    s_s[...] = jnp.where(lax.broadcasted_iota(jnp.int32, (PAD, N), 0) == 0, prior[...], 0.0)
    for i in range(3):

        @pl.when(i < pos)
        def _(i=i):
            s_s[...] = apply(s_s[...], m_s[i])

    s = apply(s_s[...], before[...])
    eye = lax.broadcasted_iota(jnp.int32, (N, N), 0) == lax.broadcasted_iota(jnp.int32, (N, N), 1)
    for end in range(SEG, SUB + 1, SEG):
        col = jnp.sum(jnp.where(eye, s[0:1, :], 0.0), axis=1, keepdims=True)
        for k in range(end - SEG, end):
            row = jnp.sum(pref[k, :N, :] * col, axis=0, keepdims=True) + pref[k, N : N + 1, :]
            for j in range(ROWS):
                st_s[j, k : k + 1, :] = row[:, j * 64 : (j + 1) * 64]
        if end < SUB:
            s = apply(s, pref[end - 1])
    for d, o in enumerate((o0, o1, o2, o3)):
        o[...] = st_s[lax.rem(z + d, ROWS)]


COPIED = 4


def send_kernel(idx, flat, ahead_far, back_far, ahead, back, sems):
    z = idx[Z]
    copies = []
    for out, d, first, count in (
        (ahead_far, 2, 0, HALF_SUB),
        (back_far, 2, HALF_SUB, HALF_SUB),
        (ahead, 1, 0, SUB),
        (back, 3, 0, SUB),
    ):
        for at in range(0, count, COPIED):
            source = lax.rem(z + d, ROWS) * (SUB * 64) + (first + at) * 64
            copies.append(
                pltpu.make_async_copy(
                    flat.at[pl.ds(pl.multiple_of(source, 64), COPIED * 64)],
                    out.at[pl.ds(at * 64, COPIED * 64)],
                    sems.at[len(copies)],
                )
            )
    for copy in copies:
        copy.start()
    for copy in copies:
        copy.wait()


def stage_kernel(idx, gains, flat, info, staged, own, sems):
    copies = [
        pltpu.make_async_copy(gains, staged, sems.at[0]),
        pltpu.make_async_copy(flat.at[pl.ds(pl.multiple_of(idx[Z] * (SUB * 64), 64), SUB * 64)], own, sems.at[1]),
    ]
    for copy in copies:
        copy.start()
    for copy in copies:
        copy.wait()


def sum_kernel(idx, sums, info):
    info[...] = jnp.sum(sums[...], axis=0)


def offset_kernel(idx, g, i0, r1, r2, r3, o0, o1, o2, o3, info_s, off_s):
    z = idx[Z]
    info_s[z] = i0[...]
    for d, r in ((1, r1), (2, r2), (3, r3)):
        info_s[lax.rem(z - d + ROWS, ROWS)] = r[...]
    lane = lax.broadcasted_iota(jnp.int32, (64, 128), 1)
    for q in range(4):
        full = jnp.concatenate([info_s[i, :, q * 64 : (q + 1) * 64] for i in range(ROWS)], axis=1)
        acc = jnp.zeros((64, 128), F32)
        for k in range(16):
            col = jnp.sum(g[16 * q + k] * full[k : k + 1, :], axis=1, keepdims=True)
            acc = jnp.where(lane == k, col, acc)
        off_s[q] = jnp.concatenate([acc, jnp.zeros((64, 128), F32)], axis=0).T[:16, :]
    for d, o in enumerate((o0, o1, o2, o3)):
        o[:, :128] = off_s[lax.rem(z + d, ROWS)]
        o[:, 128:] = jnp.zeros((16, 128), F32)


def place_kernel(idx, r0, r2, r1, r3, out):
    z = idx[Z]
    for d, r in enumerate((r0, r1, r2, r3)):
        slot = lax.rem(z - d + ROWS, ROWS)
        out[pl.ds(pl.multiple_of(slot * SUB, SUB), SUB), :] = r[...]


def along_row(x, d):
    return lax.ppermute(x, "row", [(i, (i + d) % ROWS) for i in range(ROWS)])


def shards(prior, dynamics, gains, observed, owner, step):
    tm = lax.axis_index("tm").astype(jnp.int32)
    z = lax.axis_index("row").astype(jnp.int32)
    idx = jnp.stack([z, tm & 1, (tm >> 1) & 3, tm >> 3])
    prior = prior.reshape(1, N)
    flat = dynamics.reshape(ROWS * SUB * 64, N)

    def along_rows(blocks):
        return [along_row(b, d) for d, b in enumerate(blocks, 1)]

    *far, ahead, back = call(
        send_kernel,
        [(HALF_SUB * 64, N)] * 2 + [(SUB * 64, N)] * 2,
        idx,
        (),
        [pltpu.SemaphoreType.DMA((3 * SUB // COPIED,))],
        far=(flat,),
    )
    far = [along_row(f, d) for f, d in zip(far, (1, 3))]
    prev, after = along_row(ahead, 1), along_row(back, 3)

    rid = owner[:, 0] * 16 + step % 16 + 512 * (step // 16)
    partial = binned(rid.reshape(1, -1), observed.T)
    sums = lax.all_to_all(partial, "tm", 0, 0, tiled=True).reshape(32, 16, N)
    (info,) = call(sum_kernel, [(16, N)], idx, (sums,))
    infos = along_rows([info] * 3)
    staged, own = call(
        stage_kernel,
        [gains.shape, (SUB * 64, N)],
        idx,
        (info,),
        [pltpu.SemaphoreType.DMA((2,))],
        far=(gains, flat),
    )
    infos, staged, own, prev, after, far, idx, prior = lax.optimization_barrier(
        (infos, staged, own, prev, after, far, idx, prior)
    )
    relayed = [along_row(f, d) for f, d in zip(far, (1, 3))]
    offs = call(
        offset_kernel,
        [(16, N)] * 4,
        idx,
        (staged, info, *infos),
        [pltpu.VMEM((ROWS, 16, N), F32), pltpu.VMEM((ROWS, 16, 128), F32)],
    )
    offs = [offs[0], *along_rows(offs[1:])]
    pref, top, low = call(
        compose_kernel,
        [(SUB, R, N), (HALF, N), (HALF, N)],
        idx,
        (own, prev, after, *relayed, *offs),
        [pltpu.VMEM((SUB, N, N), BF16)] * 2 + [pltpu.VMEM((ROWS, 16, N), F32)],
        mib=16,
    )

    prev_top, after_low = along_row(top, 1), along_row(low, 3)
    prev_low, after_top = along_row(low, 1), along_row(top, 3)
    block, before = call(
        four_kernel,
        [(R, N), (R, N)],
        idx,
        (top, low, prev_top, prev_low, along_row(prev_top, 1), along_row(after_low, 3), after_top, after_low),
        [pltpu.VMEM((4, R, N), F32)],
    )

    def other_core(m):
        return lax.ppermute(m, "tm", [(i, i ^ 1) for i in range(32)])

    def gathered(half, stride):
        n = 4 * stride
        got = [
            lax.ppermute(half, "tm", [(i, i - i % n + (i + d * stride) % n) for i in range(32)]) for d in (3, 1, 2)
        ]
        return *got, *[other_core(g) for g in got]

    column, half, before = call(
        pair_kernel, [(R, N), (HALF, N), (R, N)], idx, (block, other_core(block), before)
    )
    half, ybefore = call(
        plane_kernel,
        [(HALF, N), (R, N)],
        idx,
        (column, *gathered(half, 2)),
        [pltpu.VMEM((4, R, N), F32), pltpu.VMEM((R, N), F32)],
    )
    (before,) = call(fold_kernel, [(R, N)], idx, (ybefore, before))
    outs = call(
        states_kernel,
        [(SUB, 64)] * 4,
        idx,
        (prior, *gathered(half, 8), before, pref),
        [pltpu.VMEM((ROWS, SUB, 64), F32), pltpu.VMEM((4, R, N), F32), pltpu.VMEM((PAD, N), F32)],
    )
    got = [outs[0], along_row(outs[2], 2), along_row(outs[1], 1), along_row(outs[3], 3)]
    return pl.pallas_call(
        place_kernel,
        out_shape=jax.ShapeDtypeStruct((64, 64), F32),
        in_specs=[SM] + [VM] * 4,
        out_specs=VM,
        compiler_params=pltpu.CompilerParams(vmem_limit_bytes=4 * MIB),
    )(idx, *[near(g) for g in got])


def solution(mesh):
    return jax.shard_map(
        shards,
        mesh=mesh,
        in_specs=(
            P(),
            P("tm", "row", None),
            P("tm", "row", None),
            P("tm", "row"),
            P("tm", None),
            P("tm"),
        ),
        out_specs=P("tm", "row"),
        check_vma=False,
    )
```

```python
import jax
import jax.numpy as jnp
from jax import lax
from jax.experimental import pallas as pl
from jax.experimental.pallas import tpu as pltpu
from jax.sharding import PartitionSpec as P

F32 = jnp.float32
BF16 = jnp.bfloat16
MIB = 1024 * 1024
VM = pl.BlockSpec(memory_space=pltpu.VMEM)
SM = pl.BlockSpec(memory_space=pltpu.SMEM)
N = 256
PAD = 16
R = N + PAD
Z, C, Y, X = range(4)
HALF = R // 2
ROWS = 4
SUB = 16
SEG = 4
HALF_SUB = SUB // 2
Z, C, Y, X = range(4)
HALF = R // 2
ROWS = 4
SUB = 16
CHUNKS = ((5, 5), (3, 3))
SEGS = tuple(n for chunk in CHUNKS for n in chunk)
SIZES = tuple(sum(chunk) for chunk in CHUNKS)
ENDS = tuple(sum(SEGS[: i + 1]) for i in range(len(SEGS)))


def split(x):
    hi = x.astype(BF16)
    return hi, (x - hi.astype(F32)).astype(BF16)


def dot_nn(a, b):
    return lax.dot_general(a, b, (((1,), (0,)), ((), ())), preferred_element_type=F32)


def dot_nt(a, b):
    return lax.dot_general(a, b, (((1,), (1,)), ((), ())), preferred_element_type=F32)


def mm(a, b, dot=dot_nn):
    ah, al = split(a)
    bh, bl = split(b)
    return dot(ah, bh) + dot(al, bh) + dot(ah, bl)


def then(first, second):
    out = mm(first, second[:N])
    return jnp.concatenate([out[:N], out[N:] + second[N:]], axis=0)


def apply(s, m):
    return mm(s, m[:N]) + m[N:]


def eye_map():
    r = lax.broadcasted_iota(jnp.int32, (R, N), 0)
    c = lax.broadcasted_iota(jnp.int32, (R, N), 1)
    return jnp.where(r == c, 1.0, 0.0).astype(F32)


FAR = pl.BlockSpec(memory_space=pltpu.HBM)


def near(x):
    return pltpu.with_memory_space_constraint(x, pltpu.VMEM)


def call(kernel, outs, idx, args, scratch=(), far=(), mib=8):
    outs = [o if isinstance(o[0], tuple) else (o, F32) for o in outs]
    return pl.pallas_call(
        kernel,
        out_shape=[pltpu.VMEM(s, t) for s, t in outs],
        in_specs=[SM] + [FAR] * len(far) + [VM] * len(args),
        out_specs=[VM] * len(outs),
        scratch_shapes=list(scratch),
        compiler_params=pltpu.CompilerParams(vmem_limit_bytes=mib * MIB),
    )(idx, *[pltpu.with_memory_space_constraint(f, pltpu.HBM) for f in far], *[near(a) for a in args])


BIN_M = 256


def bin_kernel(rid_ref, obs_ref, out_ref, rhs, acc):
    i = pl.program_id(0)
    n_m = pl.num_programs(0)

    @pl.when(i == 0)
    def _():
        x = obs_ref[...]
        hi = x.astype(BF16)
        rest = x - hi.astype(F32)
        mid = rest.astype(BF16)
        low = (rest - mid.astype(F32)).astype(BF16)
        rhs[...] = jnp.concatenate([hi, mid, low, jnp.zeros_like(hi)], axis=0)

    rows = lax.broadcasted_iota(jnp.int32, (BIN_M, rid_ref.shape[1]), 0) + i * BIN_M
    onehot = jnp.where(rows == rid_ref[...], 1.0, 0.0).astype(BF16)
    got = dot_nt(onehot, rhs[...])
    a = got[:, :128] + got[:, 128:]
    acc[pl.ds(pl.multiple_of(i * BIN_M, BIN_M), BIN_M), :] = a + pltpu.roll(a, 64, 1)

    @pl.when(i == n_m - 1)
    def _():
        part = out_ref.shape[0]
        low_half = lax.broadcasted_iota(jnp.int32, (part, 128), 1) < 64
        for h in range(2):
            even = acc[2 * h * part : (2 * h + 1) * part, :]
            odd = acc[(2 * h + 1) * part : (2 * h + 2) * part, :]
            out_ref[:, h * 128 : (h + 1) * 128] = jnp.where(low_half, even, odd)


def binned(rid, observed):
    n_bins = 2048
    width, obs_rows = observed.shape
    return pl.pallas_call(
        bin_kernel,
        out_shape=jax.ShapeDtypeStruct((n_bins // 4, N), F32),
        grid=(n_bins // BIN_M,),
        in_specs=[
            pl.BlockSpec((1, obs_rows), lambda i: (0, 0)),
            pl.BlockSpec((width, obs_rows), lambda i: (0, 0)),
        ],
        out_specs=pl.BlockSpec((n_bins // 4, N), lambda i: (0, 0)),
        scratch_shapes=[pltpu.VMEM((4 * width, obs_rows), BF16), pltpu.VMEM((n_bins, 128), F32)],
        compiler_params=pltpu.CompilerParams(vmem_limit_bytes=24 * MIB),
    )(rid, observed)


def assemble(z, k, own, prev, after, opposite, ah, al):
    for d in range(ROWS):
        rows = pl.ds(pl.multiple_of(lax.rem(z - d + ROWS, ROWS) * 64, 64), 64)
        ref, at = ((own, k), (prev, k), (opposite[k // HALF_SUB], k % HALF_SUB), (after, k))[d]
        hi, lo = split(ref[at * 64 : (at + 1) * 64, :])
        ah[k, rows, :] = hi
        al[k, rows, :] = lo


def compose_kernel(idx, own, prev, after, q1, q2, b0, b1, b2, b3, pref, top, low, ah, al, b_s):
    z = idx[Z]
    for d, b in enumerate((b0, b1, b2, b3)):
        b_s[lax.rem(z - d + ROWS, ROWS)] = b[...]
    b = jnp.concatenate([b_s[i, :, :64] for i in range(ROWS)], axis=1)
    first = lax.broadcasted_iota(jnp.int32, (PAD, N), 0) == 0
    eye = lax.broadcasted_iota(jnp.int32, (N, N), 0) == lax.broadcasted_iota(jnp.int32, (N, N), 1)
    eye = jnp.where(eye, 1.0, 0.0).astype(BF16)
    chains = range(SUB // SEG)
    for c in chains:
        assemble(z, c * SEG, own, prev, after, (q1, q2), ah, al)
    for t in range(SEG):
        for c in chains:
            k = c * SEG + t
            if t + 1 < SEG:
                assemble(z, k + 1, own, prev, after, (q1, q2), ah, al)
            shift = jnp.where(first, b[k : k + 1, :], 0.0)
            if t == 0:
                pref[k, :N, :] = dot_nt(eye, ah[k]) + dot_nt(eye, al[k])
                pref[k, N:, :] = shift
            else:
                hi, lo = split(pref[k - 1])
                out = dot_nt(hi, ah[k]) + dot_nt(lo, ah[k]) + dot_nt(hi, al[k])
                pref[k, :N, :] = out[:N]
                pref[k, N:, :] = out[N:] + shift
    ends = [pref[c * SEG + SEG - 1] for c in chains]
    whole = then(then(ends[0], ends[1]), then(ends[2], ends[3]))
    top[...] = whole[:HALF]
    low[...] = whole[HALF:]


def combine(pos, m_s, before):
    m0, m2 = m_s[0], m_s[2]
    m01, m23 = then(m0, m_s[1]), then(m2, m_s[3])
    total, m012 = then(m01, m23), then(m01, m2)
    before[...] = jnp.where(pos == 0, eye_map(), jnp.where(pos == 1, m0, jnp.where(pos == 2, m01, m012)))
    return total


def four_kernel(idx, t0, l0, t1, l1, t2, l2, t3, l3, total, before, m_s):
    pos = idx[Z]
    for d, (t, l) in enumerate(((t0, l0), (t1, l1), (t2, l2), (t3, l3))):
        slot = lax.rem(pos - d + 4, 4)
        m_s[slot, :HALF, :] = t[...]
        m_s[slot, HALF:, :] = l[...]
    total[...] = combine(pos, m_s, before)


def half_rows(c):
    return pl.ds(pl.multiple_of(c * HALF, 8), HALF)


def join(pos, c, mine, others, m_s):
    for d, m, o in zip((3, 1, 2), mine, others):
        slot = lax.rem(pos - d + 4, 4)
        m_s[slot, half_rows(c), :] = m[...]
        m_s[slot, half_rows(1 - c), :] = o[...]


def plane_kernel(idx, own, h1, h2, h3, o1, o2, o3, half, before, m_s, all_s):
    pos, c = idx[Y], idx[C]
    m_s[pos] = own[...]
    join(pos, c, (h1, h2, h3), (o1, o2, o3), m_s)
    all_s[...] = combine(pos, m_s, before)
    half[...] = all_s[half_rows(c), :]


def pair_kernel(idx, own, other, before_in, total, half, before):
    c = idx[C]
    swap = c == 1

    @pl.when(swap)
    def _():
        total[...] = then(other[...], own[...])
        before[...] = then(other[...], before_in[...])

    @pl.when(jnp.logical_not(swap))
    def _():
        total[...] = then(own[...], other[...])
        before[...] = before_in[...]

    half[...] = total[half_rows(c), :]


def states_kernel(idx, prior, h1, h2, h3, g1, g2, g3, ybefore, before, pref, o0, o1, o2, o3, st_s, m_s, s_s):
    z, pos = idx[Z], idx[X]
    join(pos, idx[C], (h1, h2, h3), (g1, g2, g3), m_s)
    s_s[...] = jnp.where(lax.broadcasted_iota(jnp.int32, (PAD, N), 0) == 0, prior[...], 0.0)
    for i in range(3):

        @pl.when(i < pos)
        def _(i=i):
            s_s[...] = apply(s_s[...], m_s[i])

    s = apply(apply(s_s[...], ybefore[...]), before[...])
    eye = lax.broadcasted_iota(jnp.int32, (N, N), 0) == lax.broadcasted_iota(jnp.int32, (N, N), 1)
    for end in range(SEG, SUB + 1, SEG):
        col = jnp.sum(jnp.where(eye, s[0:1, :], 0.0), axis=1, keepdims=True)
        for k in range(end - SEG, end):
            row = jnp.sum(pref[k, :N, :] * col, axis=0, keepdims=True) + pref[k, N : N + 1, :]
            for j in range(ROWS):
                st_s[j, k : k + 1, :] = row[:, j * 64 : (j + 1) * 64]
        if end < SUB:
            s = apply(s, pref[end - 1])
    for d, o in enumerate((o0, o1, o2, o3)):
        o[...] = st_s[lax.rem(z + d, ROWS)]


COPIED = 4


def send_kernel(idx, flat, ahead_far, back_far, ahead, back, sems):
    z = idx[Z]
    copies = []
    for out, d, first, count in (
        (ahead_far, 2, 0, HALF_SUB),
        (back_far, 2, HALF_SUB, HALF_SUB),
        (ahead, 1, 0, SUB),
        (back, 3, 0, SUB),
    ):
        for at in range(0, count, COPIED):
            source = lax.rem(z + d, ROWS) * (SUB * 64) + (first + at) * 64
            copies.append(
                pltpu.make_async_copy(
                    flat.at[pl.ds(pl.multiple_of(source, 64), COPIED * 64)],
                    out.at[pl.ds(at * 64, COPIED * 64)],
                    sems.at[len(copies)],
                )
            )
    for copy in copies:
        copy.start()
    for copy in copies:
        copy.wait()


def stage_kernel(idx, gains, flat, info, staged, own, sems):
    copies = [
        pltpu.make_async_copy(gains, staged, sems.at[0]),
        pltpu.make_async_copy(flat.at[pl.ds(pl.multiple_of(idx[Z] * (SUB * 64), 64), SUB * 64)], own, sems.at[1]),
    ]
    for copy in copies:
        copy.start()
    for copy in copies:
        copy.wait()


def sum_kernel(idx, sums, info):
    info[...] = jnp.sum(sums[...], axis=0)


def offset_kernel(idx, g, i0, r1, r2, r3, o0, o1, o2, o3, info_s, off_s):
    z = idx[Z]
    info_s[z] = i0[...]
    for d, r in ((1, r1), (2, r2), (3, r3)):
        info_s[lax.rem(z - d + ROWS, ROWS)] = r[...]
    lane = lax.broadcasted_iota(jnp.int32, (64, 128), 1)
    for q in range(4):
        full = jnp.concatenate([info_s[i, :, q * 64 : (q + 1) * 64] for i in range(ROWS)], axis=1)
        acc = jnp.zeros((64, 128), F32)
        for k in range(16):
            col = jnp.sum(g[16 * q + k] * full[k : k + 1, :], axis=1, keepdims=True)
            acc = jnp.where(lane == k, col, acc)
        off_s[q] = jnp.concatenate([acc, jnp.zeros((64, 128), F32)], axis=0).T[:16, :]
    for d, o in enumerate((o0, o1, o2, o3)):
        o[:, :128] = off_s[lax.rem(z + d, ROWS)]
        o[:, 128:] = jnp.zeros((16, 128), F32)


def place_kernel(idx, r0, r2, r1, r3, out):
    z = idx[Z]
    for d, r in enumerate((r0, r1, r2, r3)):
        slot = lax.rem(z - d + ROWS, ROWS)
        out[pl.ds(pl.multiple_of(slot * SUB, SUB), SUB), :] = r[...]


def along_row(x, d):
    return lax.ppermute(x, "row", [(i, (i + d) % ROWS) for i in range(ROWS)])


def shards(prior, dynamics, gains, observed, owner, step):
    tm = lax.axis_index("tm").astype(jnp.int32)
    z = lax.axis_index("row").astype(jnp.int32)
    idx = jnp.stack([z, tm & 1, (tm >> 1) & 3, tm >> 3])
    prior = prior.reshape(1, N)
    flat = dynamics.reshape(ROWS * SUB * 64, N)

    def along_rows(blocks):
        return [along_row(b, d) for d, b in enumerate(blocks, 1)]

    *far, ahead, back = call(
        send_kernel,
        [(HALF_SUB * 64, N)] * 2 + [(SUB * 64, N)] * 2,
        idx,
        (),
        [pltpu.SemaphoreType.DMA((3 * SUB // COPIED,))],
        far=(flat,),
    )
    far = [along_row(f, d) for f, d in zip(far, (1, 3))]
    prev, after = along_row(ahead, 1), along_row(back, 3)

    rid = owner[:, 0] * 16 + step % 16 + 512 * (step // 16)
    partial = binned(rid.reshape(1, -1), observed.T)
    sums = lax.all_to_all(partial, "tm", 0, 0, tiled=True).reshape(32, 16, N)
    (info,) = call(sum_kernel, [(16, N)], idx, (sums,))
    infos = along_rows([info] * 3)
    staged, own = call(
        stage_kernel,
        [gains.shape, (SUB * 64, N)],
        idx,
        (info,),
        [pltpu.SemaphoreType.DMA((2,))],
        far=(gains, flat),
    )
    infos, staged, own, prev, after, far, idx, prior = lax.optimization_barrier(
        (infos, staged, own, prev, after, far, idx, prior)
    )
    relayed = [along_row(f, d) for f, d in zip(far, (1, 3))]
    offs = call(
        offset_kernel,
        [(16, N)] * 4,
        idx,
        (staged, info, *infos),
        [pltpu.VMEM((ROWS, 16, N), F32), pltpu.VMEM((ROWS, 16, 128), F32)],
    )
    offs = [offs[0], *along_rows(offs[1:])]
    pref, top, low = call(
        compose_kernel,
        [(SUB, R, N), (HALF, N), (HALF, N)],
        idx,
        (own, prev, after, *relayed, *offs),
        [pltpu.VMEM((SUB, N, N), BF16)] * 2 + [pltpu.VMEM((ROWS, 16, N), F32)],
        mib=16,
    )

    prev_top, after_low = along_row(top, 1), along_row(low, 3)
    prev_low, after_top = along_row(low, 1), along_row(top, 3)
    block, before = call(
        four_kernel,
        [(R, N), (R, N)],
        idx,
        (top, low, prev_top, prev_low, along_row(prev_top, 1), along_row(after_low, 3), after_top, after_low),
        [pltpu.VMEM((4, R, N), F32)],
    )

    def other_core(m):
        return lax.ppermute(m, "tm", [(i, i ^ 1) for i in range(32)])

    def gathered(half, stride):
        n = 4 * stride
        got = [
            lax.ppermute(half, "tm", [(i, i - i % n + (i + d * stride) % n) for i in range(32)]) for d in (3, 1, 2)
        ]
        return *got, *[other_core(g) for g in got]

    column, half, before = call(
        pair_kernel, [(R, N), (HALF, N), (R, N)], idx, (block, other_core(block), before)
    )
    half, ybefore = call(
        plane_kernel,
        [(HALF, N), (R, N)],
        idx,
        (column, *gathered(half, 2)),
        [pltpu.VMEM((4, R, N), F32), pltpu.VMEM((R, N), F32)],
    )
    outs = call(
        states_kernel,
        [(SUB, 64)] * 4,
        idx,
        (prior, *gathered(half, 8), ybefore, before, pref),
        [pltpu.VMEM((ROWS, SUB, 64), F32), pltpu.VMEM((4, R, N), F32), pltpu.VMEM((PAD, N), F32)],
    )
    got = [outs[0], along_row(outs[2], 2), along_row(outs[1], 1), along_row(outs[3], 3)]
    return pl.pallas_call(
        place_kernel,
        out_shape=jax.ShapeDtypeStruct((64, 64), F32),
        in_specs=[SM] + [VM] * 4,
        out_specs=VM,
        compiler_params=pltpu.CompilerParams(vmem_limit_bytes=4 * MIB),
    )(idx, *[near(g) for g in got])


def solution(mesh):
    return jax.shard_map(
        shards,
        mesh=mesh,
        in_specs=(
            P(),
            P("tm", "row", None),
            P("tm", "row", None),
            P("tm", "row"),
            P("tm", None),
            P("tm"),
        ),
        out_specs=P("tm", "row"),
        check_vma=False,
    )
```

```python
import jax
import jax.numpy as jnp
from jax import lax
from jax.experimental import pallas as pl
from jax.experimental.pallas import tpu as pltpu
from jax.sharding import PartitionSpec as P

F32 = jnp.float32
BF16 = jnp.bfloat16
MIB = 1024 * 1024
VM = pl.BlockSpec(memory_space=pltpu.VMEM)
SM = pl.BlockSpec(memory_space=pltpu.SMEM)
N = 256
PAD = 16
R = N + PAD
Z, C, Y, X = range(4)
HALF = R // 2
ROWS = 4
SUB = 16
SEG = 4
HALF_SUB = SUB // 2
Z, C, Y, X = range(4)
HALF = R // 2
ROWS = 4
SUB = 16
CHUNKS = ((5, 5), (3, 3))
SEGS = tuple(n for chunk in CHUNKS for n in chunk)
SIZES = tuple(sum(chunk) for chunk in CHUNKS)
ENDS = tuple(sum(SEGS[: i + 1]) for i in range(len(SEGS)))


def split(x):
    hi = x.astype(BF16)
    return hi, (x - hi.astype(F32)).astype(BF16)


def dot_nn(a, b):
    return lax.dot_general(a, b, (((1,), (0,)), ((), ())), preferred_element_type=F32)


def dot_nt(a, b):
    return lax.dot_general(a, b, (((1,), (1,)), ((), ())), preferred_element_type=F32)


def mm(a, b, dot=dot_nn):
    ah, al = split(a)
    bh, bl = split(b)
    return dot(ah, bh) + dot(al, bh) + dot(ah, bl)


def then(first, second):
    out = mm(first, second[:N])
    return jnp.concatenate([out[:N], out[N:] + second[N:]], axis=0)


def apply(s, m):
    return mm(s, m[:N]) + m[N:]


def eye_map():
    r = lax.broadcasted_iota(jnp.int32, (R, N), 0)
    c = lax.broadcasted_iota(jnp.int32, (R, N), 1)
    return jnp.where(r == c, 1.0, 0.0).astype(F32)


FAR = pl.BlockSpec(memory_space=pltpu.HBM)


def near(x):
    return pltpu.with_memory_space_constraint(x, pltpu.VMEM)


def call(kernel, outs, idx, args, scratch=(), far=(), mib=8):
    outs = [o if isinstance(o[0], tuple) else (o, F32) for o in outs]
    return pl.pallas_call(
        kernel,
        out_shape=[pltpu.VMEM(s, t) for s, t in outs],
        in_specs=[SM] + [FAR] * len(far) + [VM] * len(args),
        out_specs=[VM] * len(outs),
        scratch_shapes=list(scratch),
        compiler_params=pltpu.CompilerParams(vmem_limit_bytes=mib * MIB),
    )(idx, *[pltpu.with_memory_space_constraint(f, pltpu.HBM) for f in far], *[near(a) for a in args])


BIN_M = 256


def bin_kernel(rid_ref, obs_ref, out_ref, rhs, acc):
    i = pl.program_id(0)
    n_m = pl.num_programs(0)

    @pl.when(i == 0)
    def _():
        x = obs_ref[...]
        hi = x.astype(BF16)
        rest = x - hi.astype(F32)
        mid = rest.astype(BF16)
        low = (rest - mid.astype(F32)).astype(BF16)
        rhs[...] = jnp.concatenate([hi, mid, low, jnp.zeros_like(hi)], axis=0)

    rows = lax.broadcasted_iota(jnp.int32, (BIN_M, rid_ref.shape[1]), 0) + i * BIN_M
    onehot = jnp.where(rows == rid_ref[...], 1.0, 0.0).astype(BF16)
    got = dot_nt(onehot, rhs[...])
    a = got[:, :128] + got[:, 128:]
    acc[pl.ds(pl.multiple_of(i * BIN_M, BIN_M), BIN_M), :] = a + pltpu.roll(a, 64, 1)

    @pl.when(i == n_m - 1)
    def _():
        part = out_ref.shape[0]
        low_half = lax.broadcasted_iota(jnp.int32, (part, 128), 1) < 64
        for h in range(2):
            even = acc[2 * h * part : (2 * h + 1) * part, :]
            odd = acc[(2 * h + 1) * part : (2 * h + 2) * part, :]
            out_ref[:, h * 128 : (h + 1) * 128] = jnp.where(low_half, even, odd)


def binned(rid, observed):
    n_bins = 2048
    width, obs_rows = observed.shape
    return pl.pallas_call(
        bin_kernel,
        out_shape=jax.ShapeDtypeStruct((n_bins // 4, N), F32),
        grid=(n_bins // BIN_M,),
        in_specs=[
            pl.BlockSpec((1, obs_rows), lambda i: (0, 0)),
            pl.BlockSpec((width, obs_rows), lambda i: (0, 0)),
        ],
        out_specs=pl.BlockSpec((n_bins // 4, N), lambda i: (0, 0)),
        scratch_shapes=[pltpu.VMEM((4 * width, obs_rows), BF16), pltpu.VMEM((n_bins, 128), F32)],
        compiler_params=pltpu.CompilerParams(vmem_limit_bytes=24 * MIB),
    )(rid, observed)


def assemble(z, own, prev, after, opposite, ah, al):
    for d in range(ROWS):
        slot = lax.rem(z - d + ROWS, ROWS)
        rows = pl.ds(pl.multiple_of(slot * 64, 64), 64)
        for k in range(SUB):
            ref, at = ((own, k), (prev, k), (opposite[k // HALF_SUB], k % HALF_SUB), (after, k))[d]
            hi, lo = split(ref[at * 64 : (at + 1) * 64, :])
            ah[k, rows, :] = hi
            al[k, rows, :] = lo


def compose_kernel(idx, own, prev, after, q1, q2, b0, b1, b2, b3, pref, top, low, ah, al, b_s):
    z = idx[Z]
    assemble(z, own, prev, after, (q1, q2), ah, al)
    for d, b in enumerate((b0, b1, b2, b3)):
        b_s[lax.rem(z - d + ROWS, ROWS)] = b[...]
    b = jnp.concatenate([b_s[i, :, :64] for i in range(ROWS)], axis=1)
    first = lax.broadcasted_iota(jnp.int32, (PAD, N), 0) == 0
    eye = lax.broadcasted_iota(jnp.int32, (N, N), 0) == lax.broadcasted_iota(jnp.int32, (N, N), 1)
    eye = jnp.where(eye, 1.0, 0.0).astype(BF16)
    chains = range(SUB // SEG)
    for t in range(SEG):
        for c in chains:
            k = c * SEG + t
            shift = jnp.where(first, b[k : k + 1, :], 0.0)
            if t == 0:
                pref[k, :N, :] = dot_nt(eye, ah[k]) + dot_nt(eye, al[k])
                pref[k, N:, :] = shift
            else:
                hi, lo = split(pref[k - 1])
                out = dot_nt(hi, ah[k]) + dot_nt(lo, ah[k]) + dot_nt(hi, al[k])
                pref[k, :N, :] = out[:N]
                pref[k, N:, :] = out[N:] + shift
    ends = [pref[c * SEG + SEG - 1] for c in chains]
    whole = then(then(ends[0], ends[1]), then(ends[2], ends[3]))
    top[...] = whole[:HALF]
    low[...] = whole[HALF:]


def combine(pos, m_s, before):
    m01 = then(m_s[0], m_s[1])
    m23 = then(m_s[2], m_s[3])
    before[...] = eye_map()

    @pl.when(pos == 1)
    def _():
        before[...] = m_s[0]

    @pl.when(pos == 2)
    def _():
        before[...] = m01

    @pl.when(pos == 3)
    def _():
        before[...] = then(m01, m_s[2])

    return then(m01, m23)


def four_kernel(idx, t0, l0, t1, l1, t2, l2, t3, l3, total, before, m_s):
    pos = idx[Z]
    for d, (t, l) in enumerate(((t0, l0), (t1, l1), (t2, l2), (t3, l3))):
        slot = lax.rem(pos - d + 4, 4)
        m_s[slot, :HALF, :] = t[...]
        m_s[slot, HALF:, :] = l[...]
    total[...] = combine(pos, m_s, before)


def half_rows(c):
    return pl.ds(pl.multiple_of(c * HALF, 8), HALF)


def join(pos, c, mine, others, m_s):
    for d, m, o in zip((3, 1, 2), mine, others):
        slot = lax.rem(pos - d + 4, 4)
        m_s[slot, half_rows(c), :] = m[...]
        m_s[slot, half_rows(1 - c), :] = o[...]


def plane_kernel(idx, own, h1, h2, h3, o1, o2, o3, half, before, m_s, all_s):
    pos, c = idx[Y], idx[C]
    m_s[pos] = own[...]
    join(pos, c, (h1, h2, h3), (o1, o2, o3), m_s)
    all_s[...] = combine(pos, m_s, before)
    half[...] = all_s[half_rows(c), :]


def pair_kernel(idx, own, other, before_in, total, half, before):
    c = idx[C]
    swap = c == 1

    @pl.when(swap)
    def _():
        total[...] = then(other[...], own[...])
        before[...] = then(other[...], before_in[...])

    @pl.when(jnp.logical_not(swap))
    def _():
        total[...] = then(own[...], other[...])
        before[...] = before_in[...]

    half[...] = total[half_rows(c), :]


def fold_kernel(idx, first, second, out):
    out[...] = then(first[...], second[...])


def states_kernel(idx, prior, h1, h2, h3, g1, g2, g3, before, pref, o0, o1, o2, o3, st_s, m_s, s_s):
    z, pos = idx[Z], idx[X]
    join(pos, idx[C], (h1, h2, h3), (g1, g2, g3), m_s)
    s_s[...] = jnp.where(lax.broadcasted_iota(jnp.int32, (PAD, N), 0) == 0, prior[...], 0.0)
    for i in range(3):

        @pl.when(i < pos)
        def _(i=i):
            s_s[...] = apply(s_s[...], m_s[i])

    s = apply(s_s[...], before[...])
    eye = lax.broadcasted_iota(jnp.int32, (N, N), 0) == lax.broadcasted_iota(jnp.int32, (N, N), 1)
    for end in range(SEG, SUB + 1, SEG):
        col = jnp.sum(jnp.where(eye, s[0:1, :], 0.0), axis=1, keepdims=True)
        for k in range(end - SEG, end):
            row = jnp.sum(pref[k, :N, :] * col, axis=0, keepdims=True) + pref[k, N : N + 1, :]
            for j in range(ROWS):
                st_s[j, k : k + 1, :] = row[:, j * 64 : (j + 1) * 64]
        if end < SUB:
            s = apply(s, pref[end - 1])
    for d, o in enumerate((o0, o1, o2, o3)):
        o[...] = st_s[lax.rem(z + d, ROWS)]


COPIED = 4


def copied(idx, flat, wanted, sems):
    copies = []
    for out, d, first, count in wanted:
        for at in range(0, count, COPIED):
            source = lax.rem(idx[Z] + d, ROWS) * (SUB * 64) + (first + at) * 64
            copies.append(
                pltpu.make_async_copy(
                    flat.at[pl.ds(pl.multiple_of(source, 64), COPIED * 64)],
                    out.at[pl.ds(at * 64, COPIED * 64)],
                    sems.at[len(copies)],
                )
            )
    for copy in copies:
        copy.start()
    for copy in copies:
        copy.wait()


def far_kernel(idx, flat, ahead, back, sems):
    copied(idx, flat, ((ahead, 2, 0, HALF_SUB), (back, 2, HALF_SUB, HALF_SUB)), sems)


def near_kernel(idx, flat, far_ahead, ahead, back, own, sems):
    copied(idx, flat, ((ahead, 1, 0, SUB), (back, 3, 0, SUB), (own, 0, 0, SUB)), sems)


def stage_kernel(idx, gains, info, staged, sem):
    copy = pltpu.make_async_copy(gains, staged, sem)
    copy.start()
    copy.wait()


def sum_kernel(idx, sums, info):
    info[...] = jnp.sum(sums[...], axis=0)


def offset_kernel(idx, g, i0, r1, r2, r3, o0, o1, o2, o3, info_s, off_s):
    z = idx[Z]
    info_s[z] = i0[...]
    for d, r in ((1, r1), (2, r2), (3, r3)):
        info_s[lax.rem(z - d + ROWS, ROWS)] = r[...]
    lane = lax.broadcasted_iota(jnp.int32, (64, 128), 1)
    for q in range(4):
        full = jnp.concatenate([info_s[i, :, q * 64 : (q + 1) * 64] for i in range(ROWS)], axis=1)
        acc = jnp.zeros((64, 128), F32)
        for k in range(16):
            col = jnp.sum(g[16 * q + k] * full[k : k + 1, :], axis=1, keepdims=True)
            acc = jnp.where(lane == k, col, acc)
        off_s[q] = jnp.concatenate([acc, jnp.zeros((64, 128), F32)], axis=0).T[:16, :]
    for d, o in enumerate((o0, o1, o2, o3)):
        o[:, :128] = off_s[lax.rem(z + d, ROWS)]
        o[:, 128:] = jnp.zeros((16, 128), F32)


def place_kernel(idx, r0, r2, r1, r3, out):
    z = idx[Z]
    for d, r in enumerate((r0, r1, r2, r3)):
        slot = lax.rem(z - d + ROWS, ROWS)
        out[pl.ds(pl.multiple_of(slot * SUB, SUB), SUB), :] = r[...]


def along_row(x, d):
    return lax.ppermute(x, "row", [(i, (i + d) % ROWS) for i in range(ROWS)])


def shards(prior, dynamics, gains, observed, owner, step):
    tm = lax.axis_index("tm").astype(jnp.int32)
    z = lax.axis_index("row").astype(jnp.int32)
    idx = jnp.stack([z, tm & 1, (tm >> 1) & 3, tm >> 3])
    prior = prior.reshape(1, N)
    flat = dynamics.reshape(ROWS * SUB * 64, N)

    def along_rows(blocks):
        return [along_row(b, d) for d, b in enumerate(blocks, 1)]

    dma = pltpu.SemaphoreType.DMA
    far = call(far_kernel, [(HALF_SUB * 64, N)] * 2, idx, (), [dma((SUB // COPIED,))], far=(flat,))
    ahead, back, own = call(
        near_kernel, [(SUB * 64, N)] * 3, idx, far[:1], [dma((3 * SUB // COPIED,))], far=(flat,)
    )
    far = [along_row(f, d) for f, d in zip(far, (1, 3))]
    prev, after = along_row(ahead, 1), along_row(back, 3)

    rid = owner[:, 0] * 16 + step % 16 + 512 * (step // 16)
    partial = binned(rid.reshape(1, -1), observed.T)
    sums = lax.all_to_all(partial, "tm", 0, 0, tiled=True).reshape(32, 16, N)
    (info,) = call(sum_kernel, [(16, N)], idx, (sums,))
    infos = along_rows([info] * 3)
    (staged,) = call(stage_kernel, [gains.shape], idx, (info,), [dma], far=(gains,))
    infos, staged, own, prev, after, far, idx, prior = lax.optimization_barrier(
        (infos, staged, own, prev, after, far, idx, prior)
    )
    relayed = [along_row(f, d) for f, d in zip(far, (1, 3))]
    offs = call(
        offset_kernel,
        [(16, N)] * 4,
        idx,
        (staged, info, *infos),
        [pltpu.VMEM((ROWS, 16, N), F32), pltpu.VMEM((ROWS, 16, 128), F32)],
    )
    offs = [offs[0], *along_rows(offs[1:])]
    pref, top, low = call(
        compose_kernel,
        [(SUB, R, N), (HALF, N), (HALF, N)],
        idx,
        (own, prev, after, *relayed, *offs),
        [pltpu.VMEM((SUB, N, N), BF16)] * 2 + [pltpu.VMEM((ROWS, 16, N), F32)],
        mib=16,
    )

    prev_top, after_low = along_row(top, 1), along_row(low, 3)
    prev_low, after_top = along_row(low, 1), along_row(top, 3)
    block, before = call(
        four_kernel,
        [(R, N), (R, N)],
        idx,
        (top, low, prev_top, prev_low, along_row(prev_top, 1), along_row(after_low, 3), after_top, after_low),
        [pltpu.VMEM((4, R, N), F32)],
    )

    def other_core(m):
        return lax.ppermute(m, "tm", [(i, i ^ 1) for i in range(32)])

    def gathered(half, stride):
        n = 4 * stride
        got = [
            lax.ppermute(half, "tm", [(i, i - i % n + (i + d * stride) % n) for i in range(32)]) for d in (3, 1, 2)
        ]
        return *got, *[other_core(g) for g in got]

    column, half, before = call(
        pair_kernel, [(R, N), (HALF, N), (R, N)], idx, (block, other_core(block), before)
    )
    half, ybefore = call(
        plane_kernel,
        [(HALF, N), (R, N)],
        idx,
        (column, *gathered(half, 2)),
        [pltpu.VMEM((4, R, N), F32), pltpu.VMEM((R, N), F32)],
    )
    (before,) = call(fold_kernel, [(R, N)], idx, (ybefore, before))
    outs = call(
        states_kernel,
        [(SUB, 64)] * 4,
        idx,
        (prior, *gathered(half, 8), before, pref),
        [pltpu.VMEM((ROWS, SUB, 64), F32), pltpu.VMEM((4, R, N), F32), pltpu.VMEM((PAD, N), F32)],
    )
    got = [outs[0], along_row(outs[2], 2), along_row(outs[1], 1), along_row(outs[3], 3)]
    return pl.pallas_call(
        place_kernel,
        out_shape=jax.ShapeDtypeStruct((64, 64), F32),
        in_specs=[SM] + [VM] * 4,
        out_specs=VM,
        compiler_params=pltpu.CompilerParams(vmem_limit_bytes=4 * MIB),
    )(idx, *[near(g) for g in got])


def solution(mesh):
    return jax.shard_map(
        shards,
        mesh=mesh,
        in_specs=(
            P(),
            P("tm", "row", None),
            P("tm", "row", None),
            P("tm", "row"),
            P("tm", None),
            P("tm"),
        ),
        out_specs=P("tm", "row"),
        check_vma=False,
    )
```

```python
import jax
import jax.numpy as jnp
from jax import lax
from jax.experimental import pallas as pl
from jax.experimental.pallas import tpu as pltpu
from jax.sharding import PartitionSpec as P

F32 = jnp.float32
BF16 = jnp.bfloat16
MIB = 1024 * 1024
VM = pl.BlockSpec(memory_space=pltpu.VMEM)
SM = pl.BlockSpec(memory_space=pltpu.SMEM)
N = 256
PAD = 16
R = N + PAD
Z, C, Y, X = range(4)
HALF = R // 2
ROWS = 4
SUB = 16
SEG = 4
HALF_SUB = SUB // 2
Z, C, Y, X = range(4)
HALF = R // 2
ROWS = 4
SUB = 16
CHUNKS = ((5, 5), (3, 3))
SEGS = tuple(n for chunk in CHUNKS for n in chunk)
SIZES = tuple(sum(chunk) for chunk in CHUNKS)
ENDS = tuple(sum(SEGS[: i + 1]) for i in range(len(SEGS)))


def split(x):
    hi = x.astype(BF16)
    return hi, (x - hi.astype(F32)).astype(BF16)


def dot_nn(a, b):
    return lax.dot_general(a, b, (((1,), (0,)), ((), ())), preferred_element_type=F32)


def dot_nt(a, b):
    return lax.dot_general(a, b, (((1,), (1,)), ((), ())), preferred_element_type=F32)


def mm(a, b, dot=dot_nn):
    ah, al = split(a)
    bh, bl = split(b)
    return dot(ah, bh) + dot(al, bh) + dot(ah, bl)


def then(first, second):
    out = mm(first, second[:N])
    return jnp.concatenate([out[:N], out[N:] + second[N:]], axis=0)


def apply(s, m):
    return mm(s, m[:N]) + m[N:]


def eye_map():
    r = lax.broadcasted_iota(jnp.int32, (R, N), 0)
    c = lax.broadcasted_iota(jnp.int32, (R, N), 1)
    return jnp.where(r == c, 1.0, 0.0).astype(F32)


FAR = pl.BlockSpec(memory_space=pltpu.HBM)


def near(x):
    return pltpu.with_memory_space_constraint(x, pltpu.VMEM)


def call(kernel, outs, idx, args, scratch=(), far=(), mib=8):
    outs = [o if isinstance(o[0], tuple) else (o, F32) for o in outs]
    return pl.pallas_call(
        kernel,
        out_shape=[pltpu.VMEM(s, t) for s, t in outs],
        in_specs=[SM] + [FAR] * len(far) + [VM] * len(args),
        out_specs=[VM] * len(outs),
        scratch_shapes=list(scratch),
        compiler_params=pltpu.CompilerParams(vmem_limit_bytes=mib * MIB),
    )(idx, *[pltpu.with_memory_space_constraint(f, pltpu.HBM) for f in far], *[near(a) for a in args])


BIN_M = 512


def bin_kernel(rid_ref, obs_ref, out_ref, rhs, acc):
    i = pl.program_id(0)
    n_m = pl.num_programs(0)

    @pl.when(i == 0)
    def _():
        x = obs_ref[...]
        hi = x.astype(BF16)
        rest = x - hi.astype(F32)
        mid = rest.astype(BF16)
        low = (rest - mid.astype(F32)).astype(BF16)
        rhs[...] = jnp.concatenate([hi, mid, low, jnp.zeros_like(hi)], axis=0)

    rows = lax.broadcasted_iota(jnp.int32, (BIN_M, rid_ref.shape[1]), 0) + i * BIN_M
    onehot = jnp.where(rows == rid_ref[...], 1.0, 0.0).astype(BF16)
    got = dot_nt(onehot, rhs[...])
    a = got[:, :128] + got[:, 128:]
    acc[pl.ds(pl.multiple_of(i * BIN_M, BIN_M), BIN_M), :] = a + pltpu.roll(a, 64, 1)

    @pl.when(i == n_m - 1)
    def _():
        part = out_ref.shape[0]
        low_half = lax.broadcasted_iota(jnp.int32, (part, 128), 1) < 64
        for h in range(2):
            even = acc[2 * h * part : (2 * h + 1) * part, :]
            odd = acc[(2 * h + 1) * part : (2 * h + 2) * part, :]
            out_ref[:, h * 128 : (h + 1) * 128] = jnp.where(low_half, even, odd)


def binned(rid, observed):
    n_bins = 2048
    width, obs_rows = observed.shape
    return pl.pallas_call(
        bin_kernel,
        out_shape=jax.ShapeDtypeStruct((n_bins // 4, N), F32),
        grid=(n_bins // BIN_M,),
        in_specs=[
            pl.BlockSpec((1, obs_rows), lambda i: (0, 0)),
            pl.BlockSpec((width, obs_rows), lambda i: (0, 0)),
        ],
        out_specs=pl.BlockSpec((n_bins // 4, N), lambda i: (0, 0)),
        scratch_shapes=[pltpu.VMEM((4 * width, obs_rows), BF16), pltpu.VMEM((n_bins, 128), F32)],
        compiler_params=pltpu.CompilerParams(vmem_limit_bytes=24 * MIB),
    )(rid, observed)


def assemble(z, own, prev, after, opposite, ah, al):
    for d in range(ROWS):
        slot = lax.rem(z - d + ROWS, ROWS)
        rows = pl.ds(pl.multiple_of(slot * 64, 64), 64)
        for k in range(SUB):
            ref, at = ((own, k), (prev, k), (opposite[k // HALF_SUB], k % HALF_SUB), (after, k))[d]
            hi, lo = split(ref[at * 64 : (at + 1) * 64, :])
            ah[k, rows, :] = hi
            al[k, rows, :] = lo


def compose_kernel(idx, own, prev, after, q1, q2, b0, b1, b2, b3, pref, top, low, ah, al, b_s):
    z = idx[Z]
    assemble(z, own, prev, after, (q1, q2), ah, al)
    for d, b in enumerate((b0, b1, b2, b3)):
        b_s[lax.rem(z - d + ROWS, ROWS)] = b[...]
    b = jnp.concatenate([b_s[i, :, :64] for i in range(ROWS)], axis=1)
    first = lax.broadcasted_iota(jnp.int32, (PAD, N), 0) == 0
    eye = lax.broadcasted_iota(jnp.int32, (N, N), 0) == lax.broadcasted_iota(jnp.int32, (N, N), 1)
    eye = jnp.where(eye, 1.0, 0.0).astype(BF16)
    chains = range(SUB // SEG)
    for t in range(SEG):
        for c in chains:
            k = c * SEG + t
            shift = jnp.where(first, b[k : k + 1, :], 0.0)
            if t == 0:
                pref[k, :N, :] = dot_nt(eye, ah[k]) + dot_nt(eye, al[k])
                pref[k, N:, :] = shift
            else:
                hi, lo = split(pref[k - 1])
                out = dot_nt(hi, ah[k]) + dot_nt(lo, ah[k]) + dot_nt(hi, al[k])
                pref[k, :N, :] = out[:N]
                pref[k, N:, :] = out[N:] + shift
    ends = [pref[c * SEG + SEG - 1] for c in chains]
    whole = then(then(ends[0], ends[1]), then(ends[2], ends[3]))
    top[...] = whole[:HALF]
    low[...] = whole[HALF:]


def combine(pos, m_s, before):
    m01 = then(m_s[0], m_s[1])
    m23 = then(m_s[2], m_s[3])
    before[...] = eye_map()

    @pl.when(pos == 1)
    def _():
        before[...] = m_s[0]

    @pl.when(pos == 2)
    def _():
        before[...] = m01

    @pl.when(pos == 3)
    def _():
        before[...] = then(m01, m_s[2])

    return then(m01, m23)


def four_kernel(idx, t0, l0, t1, l1, t2, l2, t3, l3, total, before, m_s):
    pos = idx[Z]
    for d, (t, l) in enumerate(((t0, l0), (t1, l1), (t2, l2), (t3, l3))):
        slot = lax.rem(pos - d + 4, 4)
        m_s[slot, :HALF, :] = t[...]
        m_s[slot, HALF:, :] = l[...]
    total[...] = combine(pos, m_s, before)


def half_rows(c):
    return pl.ds(pl.multiple_of(c * HALF, 8), HALF)


def join(pos, c, mine, others, m_s):
    for d, m, o in zip((3, 1, 2), mine, others):
        slot = lax.rem(pos - d + 4, 4)
        m_s[slot, half_rows(c), :] = m[...]
        m_s[slot, half_rows(1 - c), :] = o[...]


def plane_kernel(idx, own, h1, h2, h3, o1, o2, o3, half, before, m_s, all_s):
    pos, c = idx[Y], idx[C]
    m_s[pos] = own[...]
    join(pos, c, (h1, h2, h3), (o1, o2, o3), m_s)
    all_s[...] = combine(pos, m_s, before)
    half[...] = all_s[half_rows(c), :]


def pair_kernel(idx, own, other, before_in, total, half, before):
    c = idx[C]
    swap = c == 1

    @pl.when(swap)
    def _():
        total[...] = then(other[...], own[...])
        before[...] = then(other[...], before_in[...])

    @pl.when(jnp.logical_not(swap))
    def _():
        total[...] = then(own[...], other[...])
        before[...] = before_in[...]

    half[...] = total[half_rows(c), :]


def fold_kernel(idx, first, second, out):
    out[...] = then(first[...], second[...])


def states_kernel(idx, prior, h1, h2, h3, g1, g2, g3, before, pref, o0, o1, o2, o3, st_s, m_s, s_s):
    z, pos = idx[Z], idx[X]
    join(pos, idx[C], (h1, h2, h3), (g1, g2, g3), m_s)
    s_s[...] = jnp.where(lax.broadcasted_iota(jnp.int32, (PAD, N), 0) == 0, prior[...], 0.0)
    for i in range(3):

        @pl.when(i < pos)
        def _(i=i):
            s_s[...] = apply(s_s[...], m_s[i])

    s = apply(s_s[...], before[...])
    eye = lax.broadcasted_iota(jnp.int32, (N, N), 0) == lax.broadcasted_iota(jnp.int32, (N, N), 1)
    for end in range(SEG, SUB + 1, SEG):
        col = jnp.sum(jnp.where(eye, s[0:1, :], 0.0), axis=1, keepdims=True)
        for k in range(end - SEG, end):
            row = jnp.sum(pref[k, :N, :] * col, axis=0, keepdims=True) + pref[k, N : N + 1, :]
            for j in range(ROWS):
                st_s[j, k : k + 1, :] = row[:, j * 64 : (j + 1) * 64]
        if end < SUB:
            s = apply(s, pref[end - 1])
    for d, o in enumerate((o0, o1, o2, o3)):
        o[...] = st_s[lax.rem(z + d, ROWS)]


COPIED = 4


def send_kernel(idx, flat, ahead_far, back_far, ahead, back, sems):
    z = idx[Z]
    copies = []
    for out, d, first, count in (
        (ahead_far, 2, 0, HALF_SUB),
        (back_far, 2, HALF_SUB, HALF_SUB),
        (ahead, 1, 0, SUB),
        (back, 3, 0, SUB),
    ):
        for at in range(0, count, COPIED):
            source = lax.rem(z + d, ROWS) * (SUB * 64) + (first + at) * 64
            copies.append(
                pltpu.make_async_copy(
                    flat.at[pl.ds(pl.multiple_of(source, 64), COPIED * 64)],
                    out.at[pl.ds(at * 64, COPIED * 64)],
                    sems.at[len(copies)],
                )
            )
    for copy in copies:
        copy.start()
    for copy in copies:
        copy.wait()


def stage_kernel(idx, gains, flat, info, staged, own, sems):
    copies = [
        pltpu.make_async_copy(gains, staged, sems.at[0]),
        pltpu.make_async_copy(flat.at[pl.ds(pl.multiple_of(idx[Z] * (SUB * 64), 64), SUB * 64)], own, sems.at[1]),
    ]
    for copy in copies:
        copy.start()
    for copy in copies:
        copy.wait()


def sum_kernel(idx, sums, info):
    info[...] = jnp.sum(sums[...], axis=0)


def offset_kernel(idx, g, i0, r1, r3, r2, o0, o1, o2, o3, info_s, off_s):
    z = idx[Z]
    info_s[z] = i0[...]
    for d, r in ((1, r1), (2, r2), (3, r3)):
        info_s[lax.rem(z - d + ROWS, ROWS)] = r[...]
    lane = lax.broadcasted_iota(jnp.int32, (64, 128), 1)
    for q in range(4):
        full = jnp.concatenate([info_s[i, :, q * 64 : (q + 1) * 64] for i in range(ROWS)], axis=1)
        acc = jnp.zeros((64, 128), F32)
        for k in range(16):
            col = jnp.sum(g[16 * q + k] * full[k : k + 1, :], axis=1, keepdims=True)
            acc = jnp.where(lane == k, col, acc)
        off_s[q] = jnp.concatenate([acc, jnp.zeros((64, 128), F32)], axis=0).T[:16, :]
    for d, o in enumerate((o0, o1, o2, o3)):
        o[:, :128] = off_s[lax.rem(z + d, ROWS)]
        o[:, 128:] = jnp.zeros((16, 128), F32)


def place_kernel(idx, r0, r2, r1, r3, out):
    z = idx[Z]
    for d, r in enumerate((r0, r1, r2, r3)):
        slot = lax.rem(z - d + ROWS, ROWS)
        out[pl.ds(pl.multiple_of(slot * SUB, SUB), SUB), :] = r[...]


def along_row(x, d):
    return lax.ppermute(x, "row", [(i, (i + d) % ROWS) for i in range(ROWS)])


def shards(prior, dynamics, gains, observed, owner, step):
    tm = lax.axis_index("tm").astype(jnp.int32)
    z = lax.axis_index("row").astype(jnp.int32)
    idx = jnp.stack([z, tm & 1, (tm >> 1) & 3, tm >> 3])
    prior = prior.reshape(1, N)
    flat = dynamics.reshape(ROWS * SUB * 64, N)

    def along_rows(blocks):
        return [along_row(b, d) for d, b in enumerate(blocks, 1)]

    *far, ahead, back = call(
        send_kernel,
        [(HALF_SUB * 64, N)] * 2 + [(SUB * 64, N)] * 2,
        idx,
        (),
        [pltpu.SemaphoreType.DMA((3 * SUB // COPIED,))],
        far=(flat,),
    )
    far = [along_row(f, d) for f, d in zip(far, (1, 3))]
    prev, after = along_row(ahead, 1), along_row(back, 3)

    rid = owner[:, 0] * 16 + step % 16 + 512 * (step // 16)
    partial = binned(rid.reshape(1, -1), observed.T)
    sums = lax.all_to_all(partial, "tm", 0, 0, tiled=True).reshape(32, 16, N)
    (info,) = call(sum_kernel, [(16, N)], idx, (sums,))
    infos = [along_row(info, d) for d in (1, 3, 2)]
    staged, own = call(
        stage_kernel,
        [gains.shape, (SUB * 64, N)],
        idx,
        (info,),
        [pltpu.SemaphoreType.DMA((2,))],
        far=(gains, flat),
    )
    infos, staged, own, prev, after, far, idx, prior = lax.optimization_barrier(
        (infos, staged, own, prev, after, far, idx, prior)
    )
    relayed = [along_row(f, d) for f, d in zip(far, (1, 3))]
    offs = call(
        offset_kernel,
        [(16, N)] * 4,
        idx,
        (staged, info, *infos),
        [pltpu.VMEM((ROWS, 16, N), F32), pltpu.VMEM((ROWS, 16, 128), F32)],
    )
    offs = [offs[0], *along_rows(offs[1:])]
    pref, top, low = call(
        compose_kernel,
        [(SUB, R, N), (HALF, N), (HALF, N)],
        idx,
        (own, prev, after, *relayed, *offs),
        [pltpu.VMEM((SUB, N, N), BF16)] * 2 + [pltpu.VMEM((ROWS, 16, N), F32)],
        mib=16,
    )

    prev_top, after_low = along_row(top, 1), along_row(low, 3)
    prev_low, after_top = along_row(low, 1), along_row(top, 3)
    block, before = call(
        four_kernel,
        [(R, N), (R, N)],
        idx,
        (top, low, prev_top, prev_low, along_row(prev_top, 1), along_row(after_low, 3), after_top, after_low),
        [pltpu.VMEM((4, R, N), F32)],
    )

    def other_core(m):
        return lax.ppermute(m, "tm", [(i, i ^ 1) for i in range(32)])

    def gathered(half, stride):
        n = 4 * stride
        got = [
            lax.ppermute(half, "tm", [(i, i - i % n + (i + d * stride) % n) for i in range(32)]) for d in (3, 1, 2)
        ]
        return *got, *[other_core(g) for g in got]

    column, half, before = call(
        pair_kernel, [(R, N), (HALF, N), (R, N)], idx, (block, other_core(block), before)
    )
    half, ybefore = call(
        plane_kernel,
        [(HALF, N), (R, N)],
        idx,
        (column, *gathered(half, 2)),
        [pltpu.VMEM((4, R, N), F32), pltpu.VMEM((R, N), F32)],
    )
    (before,) = call(fold_kernel, [(R, N)], idx, (ybefore, before))
    outs = call(
        states_kernel,
        [(SUB, 64)] * 4,
        idx,
        (prior, *gathered(half, 8), before, pref),
        [pltpu.VMEM((ROWS, SUB, 64), F32), pltpu.VMEM((4, R, N), F32), pltpu.VMEM((PAD, N), F32)],
    )
    got = [outs[0], along_row(outs[2], 2), along_row(outs[1], 1), along_row(outs[3], 3)]
    return pl.pallas_call(
        place_kernel,
        out_shape=jax.ShapeDtypeStruct((64, 64), F32),
        in_specs=[SM] + [VM] * 4,
        out_specs=VM,
        compiler_params=pltpu.CompilerParams(vmem_limit_bytes=4 * MIB),
    )(idx, *[near(g) for g in got])


def solution(mesh):
    return jax.shard_map(
        shards,
        mesh=mesh,
        in_specs=(
            P(),
            P("tm", "row", None),
            P("tm", "row", None),
            P("tm", "row"),
            P("tm", None),
            P("tm"),
        ),
        out_specs=P("tm", "row"),
        check_vma=False,
    )
```

```python
import jax
import jax.numpy as jnp
from jax import lax
from jax.experimental import pallas as pl
from jax.experimental.pallas import tpu as pltpu
from jax.sharding import PartitionSpec as P

F32 = jnp.float32
BF16 = jnp.bfloat16
MIB = 1024 * 1024
VM = pl.BlockSpec(memory_space=pltpu.VMEM)
SM = pl.BlockSpec(memory_space=pltpu.SMEM)
N = 256
PAD = 16
R = N + PAD
Z, C, Y, X = range(4)
HALF = R // 2
ROWS = 4
SUB = 16
SEG = 4
HALF_SUB = SUB // 2
Z, C, Y, X = range(4)
HALF = R // 2
ROWS = 4
SUB = 16
CHUNKS = ((5, 5), (3, 3))
SEGS = tuple(n for chunk in CHUNKS for n in chunk)
SIZES = tuple(sum(chunk) for chunk in CHUNKS)
ENDS = tuple(sum(SEGS[: i + 1]) for i in range(len(SEGS)))


def split(x):
    hi = x.astype(BF16)
    return hi, (x - hi.astype(F32)).astype(BF16)


def dot_nn(a, b):
    return lax.dot_general(a, b, (((1,), (0,)), ((), ())), preferred_element_type=F32)


def dot_nt(a, b):
    return lax.dot_general(a, b, (((1,), (1,)), ((), ())), preferred_element_type=F32)


def mm(a, b, dot=dot_nn):
    ah, al = split(a)
    bh, bl = split(b)
    return dot(ah, bh) + dot(al, bh) + dot(ah, bl)


def then(first, second):
    out = mm(first, second[:N])
    return jnp.concatenate([out[:N], out[N:] + second[N:]], axis=0)


def apply(s, m):
    return mm(s, m[:N]) + m[N:]


def eye_map():
    r = lax.broadcasted_iota(jnp.int32, (R, N), 0)
    c = lax.broadcasted_iota(jnp.int32, (R, N), 1)
    return jnp.where(r == c, 1.0, 0.0).astype(F32)


FAR = pl.BlockSpec(memory_space=pltpu.HBM)


def near(x):
    return pltpu.with_memory_space_constraint(x, pltpu.VMEM)


def call(kernel, outs, idx, args, scratch=(), far=(), mib=8):
    outs = [o if isinstance(o[0], tuple) else (o, F32) for o in outs]
    return pl.pallas_call(
        kernel,
        out_shape=[pltpu.VMEM(s, t) for s, t in outs],
        in_specs=[SM] + [FAR] * len(far) + [VM] * len(args),
        out_specs=[VM] * len(outs),
        scratch_shapes=list(scratch),
        compiler_params=pltpu.CompilerParams(vmem_limit_bytes=mib * MIB),
    )(idx, *[pltpu.with_memory_space_constraint(f, pltpu.HBM) for f in far], *[near(a) for a in args])


BIN_M = 512


def bin_kernel(rid_ref, obs_ref, out_ref, rhs, acc):
    i = pl.program_id(0)
    n_m = pl.num_programs(0)

    @pl.when(i == 0)
    def _():
        x = obs_ref[...]
        hi = x.astype(BF16)
        rest = x - hi.astype(F32)
        mid = rest.astype(BF16)
        low = (rest - mid.astype(F32)).astype(BF16)
        rhs[...] = jnp.concatenate([hi, mid, low, jnp.zeros_like(hi)], axis=0)

    rows = lax.broadcasted_iota(jnp.int32, (BIN_M, rid_ref.shape[1]), 0) + i * BIN_M
    onehot = jnp.where(rows == rid_ref[...], 1.0, 0.0).astype(BF16)
    got = dot_nt(onehot, rhs[...])
    a = got[:, :128] + got[:, 128:]
    acc[pl.ds(pl.multiple_of(i * BIN_M, BIN_M), BIN_M), :] = a + pltpu.roll(a, 64, 1)

    @pl.when(i == n_m - 1)
    def _():
        part = out_ref.shape[0]
        low_half = lax.broadcasted_iota(jnp.int32, (part, 128), 1) < 64
        for h in range(2):
            even = acc[2 * h * part : (2 * h + 1) * part, :]
            odd = acc[(2 * h + 1) * part : (2 * h + 2) * part, :]
            out_ref[:, h * 128 : (h + 1) * 128] = jnp.where(low_half, even, odd)


def binned(rid, observed):
    n_bins = 2048
    width, obs_rows = observed.shape
    return pl.pallas_call(
        bin_kernel,
        out_shape=jax.ShapeDtypeStruct((n_bins // 4, N), F32),
        grid=(n_bins // BIN_M,),
        in_specs=[
            pl.BlockSpec((1, obs_rows), lambda i: (0, 0)),
            pl.BlockSpec((width, obs_rows), lambda i: (0, 0)),
        ],
        out_specs=pl.BlockSpec((n_bins // 4, N), lambda i: (0, 0)),
        scratch_shapes=[pltpu.VMEM((4 * width, obs_rows), BF16), pltpu.VMEM((n_bins, 128), F32)],
        compiler_params=pltpu.CompilerParams(vmem_limit_bytes=24 * MIB),
    )(rid, observed)


def assemble(z, own, prev, after, opposite, ah, al):
    for d in range(ROWS):
        slot = lax.rem(z - d + ROWS, ROWS)
        rows = pl.ds(pl.multiple_of(slot * 64, 64), 64)
        for k in range(SUB):
            ref, at = ((own, k), (prev, k), (opposite[k // HALF_SUB], k % HALF_SUB), (after, k))[d]
            hi, lo = split(ref[at * 64 : (at + 1) * 64, :])
            ah[k, rows, :] = hi
            al[k, rows, :] = lo


def compose_kernel(idx, own, prev, after, q1, q2, b0, b2, b1, b3, pref, top, low, ah, al, b_s):
    z = idx[Z]
    assemble(z, own, prev, after, (q1, q2), ah, al)
    for d, b in enumerate((b0, b1, b2, b3)):
        b_s[lax.rem(z - d + ROWS, ROWS)] = b[...]
    b = jnp.concatenate([b_s[i, :, :64] for i in range(ROWS)], axis=1)
    first = lax.broadcasted_iota(jnp.int32, (PAD, N), 0) == 0
    eye = lax.broadcasted_iota(jnp.int32, (N, N), 0) == lax.broadcasted_iota(jnp.int32, (N, N), 1)
    eye = jnp.where(eye, 1.0, 0.0).astype(BF16)
    chains = range(SUB // SEG)
    for t in range(SEG):
        for c in chains:
            k = c * SEG + t
            shift = jnp.where(first, b[k : k + 1, :], 0.0)
            if t == 0:
                pref[k, :N, :] = dot_nt(eye, ah[k]) + dot_nt(eye, al[k])
                pref[k, N:, :] = shift
            else:
                hi, lo = split(pref[k - 1])
                out = dot_nt(hi, ah[k]) + dot_nt(lo, ah[k]) + dot_nt(hi, al[k])
                pref[k, :N, :] = out[:N]
                pref[k, N:, :] = out[N:] + shift
    ends = [pref[c * SEG + SEG - 1] for c in chains]
    whole = then(then(ends[0], ends[1]), then(ends[2], ends[3]))
    top[...] = whole[:HALF]
    low[...] = whole[HALF:]


def combine(pos, m_s, before):
    m01 = then(m_s[0], m_s[1])
    m23 = then(m_s[2], m_s[3])
    before[...] = eye_map()

    @pl.when(pos == 1)
    def _():
        before[...] = m_s[0]

    @pl.when(pos == 2)
    def _():
        before[...] = m01

    @pl.when(pos == 3)
    def _():
        before[...] = then(m01, m_s[2])

    return then(m01, m23)


def four_kernel(idx, t0, l0, t1, l1, t2, l2, t3, l3, total, before, m_s):
    pos = idx[Z]
    for d, (t, l) in enumerate(((t0, l0), (t1, l1), (t2, l2), (t3, l3))):
        slot = lax.rem(pos - d + 4, 4)
        m_s[slot, :HALF, :] = t[...]
        m_s[slot, HALF:, :] = l[...]
    total[...] = combine(pos, m_s, before)


def half_rows(c):
    return pl.ds(pl.multiple_of(c * HALF, 8), HALF)


def join(pos, c, mine, others, m_s):
    for d, m, o in zip((3, 1, 2), mine, others):
        slot = lax.rem(pos - d + 4, 4)
        m_s[slot, half_rows(c), :] = m[...]
        m_s[slot, half_rows(1 - c), :] = o[...]


def plane_kernel(idx, own, h1, h2, h3, o1, o2, o3, half, before, m_s, all_s):
    pos, c = idx[Y], idx[C]
    m_s[pos] = own[...]
    join(pos, c, (h1, h2, h3), (o1, o2, o3), m_s)
    all_s[...] = combine(pos, m_s, before)
    half[...] = all_s[half_rows(c), :]


def pair_kernel(idx, own, other, before_in, total, half, before):
    c = idx[C]
    swap = c == 1

    @pl.when(swap)
    def _():
        total[...] = then(other[...], own[...])
        before[...] = then(other[...], before_in[...])

    @pl.when(jnp.logical_not(swap))
    def _():
        total[...] = then(own[...], other[...])
        before[...] = before_in[...]

    half[...] = total[half_rows(c), :]


def fold_kernel(idx, first, second, out):
    out[...] = then(first[...], second[...])


def states_kernel(idx, prior, h1, h2, h3, g1, g2, g3, before, pref, o0, o1, o2, o3, st_s, m_s, s_s):
    z, pos = idx[Z], idx[X]
    join(pos, idx[C], (h1, h2, h3), (g1, g2, g3), m_s)
    s_s[...] = jnp.where(lax.broadcasted_iota(jnp.int32, (PAD, N), 0) == 0, prior[...], 0.0)
    for i in range(3):

        @pl.when(i < pos)
        def _(i=i):
            s_s[...] = apply(s_s[...], m_s[i])

    s = apply(s_s[...], before[...])
    eye = lax.broadcasted_iota(jnp.int32, (N, N), 0) == lax.broadcasted_iota(jnp.int32, (N, N), 1)
    for end in range(SEG, SUB + 1, SEG):
        col = jnp.sum(jnp.where(eye, s[0:1, :], 0.0), axis=1, keepdims=True)
        for k in range(end - SEG, end):
            row = jnp.sum(pref[k, :N, :] * col, axis=0, keepdims=True) + pref[k, N : N + 1, :]
            for j in range(ROWS):
                st_s[j, k : k + 1, :] = row[:, j * 64 : (j + 1) * 64]
        if end < SUB:
            s = apply(s, pref[end - 1])
    for d, o in enumerate((o0, o1, o2, o3)):
        o[...] = st_s[lax.rem(z + d, ROWS)]


COPIED = 4


def send_kernel(idx, flat, ahead_far, back_far, ahead, back, sems):
    z = idx[Z]
    copies = []
    for out, d, first, count in (
        (ahead_far, 2, 0, HALF_SUB),
        (back_far, 2, HALF_SUB, HALF_SUB),
        (ahead, 1, 0, SUB),
        (back, 3, 0, SUB),
    ):
        for at in range(0, count, COPIED):
            source = lax.rem(z + d, ROWS) * (SUB * 64) + (first + at) * 64
            copies.append(
                pltpu.make_async_copy(
                    flat.at[pl.ds(pl.multiple_of(source, 64), COPIED * 64)],
                    out.at[pl.ds(at * 64, COPIED * 64)],
                    sems.at[len(copies)],
                )
            )
    for copy in copies:
        copy.start()
    for copy in copies:
        copy.wait()


def stage_kernel(idx, gains, flat, info, staged, own, sems):
    copies = [
        pltpu.make_async_copy(gains, staged, sems.at[0]),
        pltpu.make_async_copy(flat.at[pl.ds(pl.multiple_of(idx[Z] * (SUB * 64), 64), SUB * 64)], own, sems.at[1]),
    ]
    for copy in copies:
        copy.start()
    for copy in copies:
        copy.wait()


def sum_kernel(idx, sums, info):
    info[...] = jnp.sum(sums[...], axis=0)


def offset_kernel(idx, g, i0, r1, r3, r2, o0, o1, o2, o3, info_s, off_s):
    z = idx[Z]
    info_s[z] = i0[...]
    for d, r in ((1, r1), (2, r2), (3, r3)):
        info_s[lax.rem(z - d + ROWS, ROWS)] = r[...]
    lane = lax.broadcasted_iota(jnp.int32, (64, 128), 1)
    for q in range(4):
        full = jnp.concatenate([info_s[i, :, q * 64 : (q + 1) * 64] for i in range(ROWS)], axis=1)
        acc = jnp.zeros((64, 128), F32)
        for k in range(16):
            col = jnp.sum(g[16 * q + k] * full[k : k + 1, :], axis=1, keepdims=True)
            acc = jnp.where(lane == k, col, acc)
        off_s[q] = jnp.concatenate([acc, jnp.zeros((64, 128), F32)], axis=0).T[:16, :]
    for d, o in enumerate((o0, o1, o2, o3)):
        o[:, :128] = off_s[lax.rem(z + d, ROWS)]
        o[:, 128:] = jnp.zeros((16, 128), F32)


def place_kernel(idx, r0, r2, r1, r3, out):
    z = idx[Z]
    for d, r in enumerate((r0, r1, r2, r3)):
        slot = lax.rem(z - d + ROWS, ROWS)
        out[pl.ds(pl.multiple_of(slot * SUB, SUB), SUB), :] = r[...]


def along_row(x, d):
    return lax.ppermute(x, "row", [(i, (i + d) % ROWS) for i in range(ROWS)])


def shards(prior, dynamics, gains, observed, owner, step):
    tm = lax.axis_index("tm").astype(jnp.int32)
    z = lax.axis_index("row").astype(jnp.int32)
    idx = jnp.stack([z, tm & 1, (tm >> 1) & 3, tm >> 3])
    prior = prior.reshape(1, N)
    flat = dynamics.reshape(ROWS * SUB * 64, N)

    def along_rows(blocks):
        return [along_row(b, d) for d, b in enumerate(blocks, 1)]

    *far, ahead, back = call(
        send_kernel,
        [(HALF_SUB * 64, N)] * 2 + [(SUB * 64, N)] * 2,
        idx,
        (),
        [pltpu.SemaphoreType.DMA((3 * SUB // COPIED,))],
        far=(flat,),
    )
    far = [along_row(f, d) for f, d in zip(far, (1, 3))]
    prev, after = along_row(ahead, 1), along_row(back, 3)

    rid = owner[:, 0] * 16 + step % 16 + 512 * (step // 16)
    partial = binned(rid.reshape(1, -1), observed.T)
    sums = lax.all_to_all(partial, "tm", 0, 0, tiled=True).reshape(32, 16, N)
    (info,) = call(sum_kernel, [(16, N)], idx, (sums,))
    infos = [along_row(info, d) for d in (1, 3, 2)]
    staged, own = call(
        stage_kernel,
        [gains.shape, (SUB * 64, N)],
        idx,
        (info,),
        [pltpu.SemaphoreType.DMA((2,))],
        far=(gains, flat),
    )
    infos, staged, own, prev, after, far, idx, prior = lax.optimization_barrier(
        (infos, staged, own, prev, after, far, idx, prior)
    )
    relayed = [along_row(f, d) for f, d in zip(far, (1, 3))]
    offs = call(
        offset_kernel,
        [(16, N)] * 4,
        idx,
        (staged, info, *infos),
        [pltpu.VMEM((ROWS, 16, N), F32), pltpu.VMEM((ROWS, 16, 128), F32)],
    )
    offs = [offs[0], *[along_row(offs[d], d) for d in (2, 1, 3)]]
    pref, top, low = call(
        compose_kernel,
        [(SUB, R, N), (HALF, N), (HALF, N)],
        idx,
        (own, prev, after, *relayed, *offs),
        [pltpu.VMEM((SUB, N, N), BF16)] * 2 + [pltpu.VMEM((ROWS, 16, N), F32)],
        mib=16,
    )

    prev_top, after_low = along_row(top, 1), along_row(low, 3)
    prev_low, after_top = along_row(low, 1), along_row(top, 3)
    block, before = call(
        four_kernel,
        [(R, N), (R, N)],
        idx,
        (top, low, prev_top, prev_low, along_row(prev_top, 1), along_row(after_low, 3), after_top, after_low),
        [pltpu.VMEM((4, R, N), F32)],
    )

    def other_core(m):
        return lax.ppermute(m, "tm", [(i, i ^ 1) for i in range(32)])

    def gathered(half, stride):
        n = 4 * stride
        got = [
            lax.ppermute(half, "tm", [(i, i - i % n + (i + d * stride) % n) for i in range(32)]) for d in (3, 1, 2)
        ]
        return *got, *[other_core(g) for g in got]

    column, half, before = call(
        pair_kernel, [(R, N), (HALF, N), (R, N)], idx, (block, other_core(block), before)
    )
    half, ybefore = call(
        plane_kernel,
        [(HALF, N), (R, N)],
        idx,
        (column, *gathered(half, 2)),
        [pltpu.VMEM((4, R, N), F32), pltpu.VMEM((R, N), F32)],
    )
    (before,) = call(fold_kernel, [(R, N)], idx, (ybefore, before))
    outs = call(
        states_kernel,
        [(SUB, 64)] * 4,
        idx,
        (prior, *gathered(half, 8), before, pref),
        [pltpu.VMEM((ROWS, SUB, 64), F32), pltpu.VMEM((4, R, N), F32), pltpu.VMEM((PAD, N), F32)],
    )
    got = [outs[0], along_row(outs[2], 2), along_row(outs[1], 1), along_row(outs[3], 3)]
    return pl.pallas_call(
        place_kernel,
        out_shape=jax.ShapeDtypeStruct((64, 64), F32),
        in_specs=[SM] + [VM] * 4,
        out_specs=VM,
        compiler_params=pltpu.CompilerParams(vmem_limit_bytes=4 * MIB),
    )(idx, *[near(g) for g in got])


def solution(mesh):
    return jax.shard_map(
        shards,
        mesh=mesh,
        in_specs=(
            P(),
            P("tm", "row", None),
            P("tm", "row", None),
            P("tm", "row"),
            P("tm", None),
            P("tm"),
        ),
        out_specs=P("tm", "row"),
        check_vma=False,
    )
```
